32 devices in a mesh: seq: 8 (over z, y), dp: 4 (over x, core).
Axes of the slice: x: 2, y: 2, z: 4, core: 2. Of those that a mesh axis runs over, the one named last changes fastest.
Arguments:
- residual_in: bfloat16 [8, 6144, 768], P('dp', 'seq'), may hold values from -6 to 6
- cotangent: bfloat16 [8, 6144, 768], P('dp', 'seq'), may hold values from -6 to 6
- norm_gain: float32 [768], replicated, may hold values from 0.1 to 1.9
- in_weight: bfloat16 [768, 3352], P('dp'), may hold values from -0.21875 to 0.21875
- conv_weight: float32 [1792, 4], replicated, may hold values from -3 to 3
- conv_bias: float32 [1792], replicated, may hold values from -3 to 3
- step_bias: float32 [24], replicated, may hold values from -4.5 to -2.5
- decay_log: float32 [24], replicated, may hold values from -5.8 to -0.7
- skip_gain: float32 [24], replicated, may hold values from 0.5 to 1.5
- gate_gain: float32 [1536], replicated, may hold values from 0.1 to 1.9
- out_weight: bfloat16 [1536, 768], P('dp'), may hold values from -0.15625 to 0.15625
- in_down: bfloat16 [8, 768, 16], P('dp'), may hold values from -0.21875 to 0.21875
- in_up: bfloat16 [8, 16, 3352], P('dp'), may hold values from -0.75 to 0.75
- out_down: bfloat16 [8, 1536, 16], P('dp'), may hold values from -0.15625 to 0.15625
- out_up: bfloat16 [8, 16, 768], P('dp'), may hold values from -0.75 to 0.75
- in_index: int32 [8, 1], P('dp'), may hold values from 0 to 7
- out_index: int32 [8, 1], P('dp'), may hold values from 0 to 7
Outputs:
- block_out: bfloat16 [8, 6144, 768], P('dp', 'seq')
- grad_input: bfloat16 [8, 6144, 768], P('dp', 'seq')
- grad_in_down: float32 [8, 768, 16], P('dp')
- grad_in_up: float32 [8, 16, 3352], P('dp')
- grad_out_down: float32 [8, 1536, 16], P('dp')
- grad_out_up: float32 [8, 16, 768], P('dp')
The draws below stay inside these ranges and needn't reach their ends.
Inputs may be any that keep to these rules, and one draw needn't show every extreme that they name: `in_index`: every adapter is chosen by at least one sequence. `out_index`: every adapter is chosen by at least one sequence.
All inputs are finite; a program needn't handle non-finite values.
Results may differ from the reference program's by a relative error of at most 0.02.
Values may be sent and summed in bfloat16 or wider, within the bound.
A program may use at most 320 MiB of HBM per device.

```python
import jax
import jax.numpy as jnp
from jax import lax

D = 768
HEADS = 24
HEAD_DIM = 64
STATE = 128
KERNEL = 4
SPAN = 256
ADAPTERS = 8
RANK = 16
INNER = 1536
XBC = 1792
PROJ = 3352
SEQS = 8
LEN = 6144


def draw_decay_log(key, part):
    key = jax.random.fold_in(key, 7)
    return jax.random.uniform(key, (HEADS,), jnp.float32, -5.8, -0.7)


def shard_levels(stream_key, extent, shards, least, high):
    def one(axis_at, shards_of):
        heights = jax.random.uniform(jax.random.fold_in(jax.random.fold_in(stream_key, 6), axis_at), (shards_of,), jnp.float32, least / len(shards), high / len(shards))
        return jnp.repeat(jnp.exp(heights), extent[axis_at] // shards_of).reshape((-1,) + (1,) * (len(extent) - axis_at - 1))

    level = one(*shards[0])
    for cut in shards[1:]:
        level = level * one(*cut)
    return level


def different_ones(key, rows, number_of, top, lift):
    ranking = jax.random.permutation(jax.random.fold_in(key, 1), number_of)
    favour = ranking
    for power in range(3):
        favour = favour * favour // number_of
    favour = favour * lift // number_of
    lots = jax.random.randint(jax.random.fold_in(key, 2), (rows, number_of), 0, 4096) + favour
    sure = jax.random.permutation(jax.random.fold_in(key, 3), rows)[jnp.arange(number_of) % rows]
    lots = jnp.where(jnp.arange(rows)[:, None] == sure[None, :], 1 << 14, lots)
    merit = lots * number_of + jnp.arange(number_of)
    return lax.top_k(merit.astype(jnp.int32), top)[1].astype(jnp.int32)


def noise(own_key, dims, scale, most, cuts=(), dtype=jnp.bfloat16):
    loudness = shard_levels(own_key, dims, cuts, -0.22, 0.18) if cuts else 1.0
    values = jax.random.normal(own_key, dims, jnp.float32) * scale * loudness
    return jnp.minimum(jnp.maximum(values, -most), most).astype(dtype)


def setup_inputs(seed: int = 0) -> dict:
    key_list = jax.random.split(jax.random.key(seed), 18)
    return {
        "residual_in": noise(key_list[0], (SEQS, LEN, D), 1.0, 6.0, ((0, 4), (1, 8))),
        "cotangent": noise(key_list[1], (SEQS, LEN, D), 1.0, 6.0, ((0, 4), (1, 8))),
        "norm_gain": jnp.clip(1.0 + 0.18 * jax.random.normal(key_list[2], (D,), jnp.float32), 0.1, 1.9),
        "in_weight": noise(key_list[3], (D, PROJ), D ** -0.5, 0.21875, ((0, 4),)),
        "conv_weight": noise(key_list[4], (XBC, KERNEL), KERNEL ** -0.5, 3.0, (), jnp.float32),
        "conv_bias": noise(key_list[5], (XBC,), 0.5, 3.0, (), jnp.float32),
        "step_bias": jnp.clip(jax.random.uniform(key_list[6], (HEADS,), jnp.float32, -4.5, -2.5), -4.5, -2.5),
        "decay_log": draw_decay_log(jax.random.fold_in(key_list[17], 71), 0),
        "skip_gain": jnp.clip(jax.random.uniform(key_list[8], (HEADS,), jnp.float32, 0.5, 1.5), 0.5, 1.5),
        "gate_gain": jnp.clip(1.0 + 0.18 * jax.random.normal(key_list[9], (INNER,), jnp.float32), 0.1, 1.9),
        "out_weight": noise(key_list[10], (INNER, D), INNER ** -0.5, 0.15625, ((0, 4),)),
        "in_down": noise(key_list[11], (ADAPTERS, D, RANK), D ** -0.5, 0.21875, ((0, 4),)),
        "in_up": noise(key_list[12], (ADAPTERS, RANK, PROJ), (4 * RANK) ** -0.5, 0.75, ((0, 4),)),
        "out_down": noise(key_list[13], (ADAPTERS, INNER, RANK), INNER ** -0.5, 0.15625, ((0, 4),)),
        "out_up": noise(key_list[14], (ADAPTERS, RANK, D), (4 * RANK) ** -0.5, 0.75, ((0, 4),)),
        "in_index": different_ones(key_list[15], SEQS, ADAPTERS, 1, 0),
        "out_index": different_ones(key_list[16], SEQS, ADAPTERS, 1, 0),
    }


EPS = 1e-05
HIGH = lax.Precision.HIGHEST

@jax.custom_vjp
def low(v):
    return lax.optimization_barrier(v.astype(jnp.bfloat16)).astype(jnp.float32)

@jax.custom_vjp
def low_back(v):
    return v

def low_keep(v):
    return (low(v), None)

def low_pass(kept, grad):
    return (grad,)

def back_keep(v):
    return (v, None)

def back_low(kept, grad):
    return (low(grad),)
low.defvjp(low_keep, low_pass)
low_back.defvjp(back_keep, back_low)

def block_step(carry_state, block, decay_rate):
    values, widths, inputs_b, reads_c = block
    rates = widths * decay_rate[None, :]
    cumulative = jnp.cumsum(rates, axis=0)
    length = values.shape[0]
    rows_at = lax.broadcasted_iota(jnp.int32, (length, length), 0)
    cols_at = lax.broadcasted_iota(jnp.int32, (length, length), 1)
    lower_mask = rows_at >= cols_at
    spread = cumulative.T[:, :, None] - cumulative.T[:, None, :]
    kernel = jnp.exp(jnp.where(lower_mask[None], spread, -1e+30))
    scores = jnp.dot(reads_c, inputs_b.T, precision=HIGH)
    mixing = kernel * scores[None] * widths.T[:, None, :]
    inner_part = jnp.einsum('hij,jhp->ihp', mixing, values, precision=HIGH)
    carried = jnp.exp(cumulative)[:, :, None] * jnp.einsum('in,hpn->ihp', reads_c, carry_state, precision=HIGH)
    tail_weight = jnp.exp(cumulative[-1][None, :] - cumulative) * widths
    update = jnp.einsum('jh,jhp,jn->hpn', tail_weight, values, inputs_b, precision=HIGH)
    carry_state = jnp.exp(cumulative[-1])[:, None, None] * carry_state + update
    return (carry_state, inner_part + carried)

def state_space(values, widths, inputs_b, reads_c, decay_rate, start_state, block_size, skip_gain):
    total_rows, head_count, head_width = values.shape
    block_count = total_rows // block_size
    blocks = (values.reshape(block_count, block_size, head_count, head_width), widths.reshape(block_count, block_size, head_count), inputs_b.reshape(block_count, block_size, inputs_b.shape[1]), reads_c.reshape(block_count, block_size, reads_c.shape[1]))
    step_fn = jax.checkpoint(lambda carry_state, block: block_step(carry_state, block, decay_rate))
    final_state, outputs = lax.scan(step_fn, start_state, blocks)
    return (outputs.reshape(total_rows, head_count, head_width) + skip_gain[None, :, None] * values, final_state)

def convolve(extended, conv_weight, conv_bias):
    taps = conv_weight.shape[1]
    length = extended.shape[0] - taps + 1
    accumulated = conv_bias[None, :] + jnp.zeros((length, conv_weight.shape[0]), jnp.float32)
    for shift_at in range(taps):
        accumulated = accumulated + conv_weight[:, shift_at][None, :] * extended[shift_at:shift_at + length]
    return accumulated

def one_sequence(sequence_items, frozen):
    source, down_in, up_in, down_out, up_out = sequence_items
    norm_gain, in_weight, conv_weight, conv_bias, step_bias, decay_log, skip_gain, gate_gain, out_weight = frozen
    scale_in = lax.rsqrt(lax.optimization_barrier(jnp.mean(source * source, axis=1, keepdims=True)) + EPS)
    normed = low(source * scale_in * norm_gain[None, :])
    low_in = low_back(low(jnp.dot(normed, down_in, precision=HIGH)))
    project = low_back(low(jnp.dot(normed, in_weight, precision=HIGH) + jnp.dot(low_in, up_in, precision=HIGH)))
    gate_part = project[:, :INNER]
    mixer_part = project[:, INNER:INNER + XBC]
    width_raw = project[:, INNER + XBC:]
    extended = jnp.concatenate([jnp.zeros((KERNEL - 1, XBC), jnp.float32), mixer_part], axis=0)
    activated = jax.nn.silu(convolve(extended, conv_weight, conv_bias))
    values = activated[:, :INNER].reshape(LEN, HEADS, HEAD_DIM)
    inputs_b = activated[:, INNER:INNER + STATE]
    reads_c = activated[:, INNER + STATE:]
    widths = jax.nn.softplus(width_raw + step_bias[None, :])
    decay_rate = -jnp.exp(decay_log)
    start_state = jnp.zeros((HEADS, HEAD_DIM, STATE), jnp.float32)
    ssd_out, final_state = state_space(values, widths, inputs_b, reads_c, decay_rate, start_state, SPAN, skip_gain)
    gated = ssd_out.reshape(LEN, INNER) * jax.nn.silu(gate_part)
    scale_out = lax.rsqrt(lax.optimization_barrier(jnp.mean(gated * gated, axis=1, keepdims=True)) + EPS)
    normed_out = low(gated * scale_out * gate_gain[None, :])
    low_out = low_back(low(jnp.dot(normed_out, down_out, precision=HIGH)))
    return source + jnp.dot(normed_out, out_weight, precision=HIGH) + jnp.dot(low_out, up_out, precision=HIGH)

def reference(residual_in, cotangent, norm_gain, in_weight, conv_weight, conv_bias, step_bias, decay_log, skip_gain, gate_gain, out_weight, in_down, in_up, out_down, out_up, in_index, out_index):
    frozen = (norm_gain, in_weight.astype(jnp.float32), conv_weight, conv_bias, step_bias, decay_log, skip_gain, gate_gain, out_weight.astype(jnp.float32))
    in_pick = in_index[:, 0].astype(jnp.int32)
    out_pick = out_index[:, 0].astype(jnp.int32)

    def forward(source_all, in_down_f, in_up_f, out_down_f, out_up_f):
        selected = (source_all, in_down_f[in_pick], in_up_f[in_pick], out_down_f[out_pick], out_up_f[out_pick])
        return lax.map(jax.checkpoint(lambda sequence_items: one_sequence(sequence_items, frozen)), selected)
    result, pullback = jax.vjp(forward, residual_in.astype(jnp.float32), in_down.astype(jnp.float32), in_up.astype(jnp.float32), out_down.astype(jnp.float32), out_up.astype(jnp.float32))
    gradients = pullback(cotangent.astype(jnp.float32))
    return (result.astype(jnp.bfloat16), gradients[0].astype(jnp.bfloat16), gradients[1], gradients[2], gradients[3], gradients[4])
```

```python
import functools

import jax
import jax.numpy as jnp
from jax import lax
from jax.experimental import pallas as pl
from jax.experimental.pallas import tpu as pltpu
from jax.sharding import PartitionSpec as P

EPS = 1e-05
CHUNK = 128
BLOCK = 256
RIM = 16
LANES = 128
LOG2E = 1.4426950408889634
BF = jnp.bfloat16
F32 = jnp.float32
MESH = pl.DeviceIdType.MESH
VMEM_LIMIT = 56 * 2**20


def nn(a, b):
    return lax.dot_general(a, b, (((1,), (0,)), ((), ())), preferred_element_type=F32)


def nt(a, b):
    return lax.dot_general(a, b, (((1,), (1,)), ((), ())), preferred_element_type=F32)


def tn(a, b):
    return lax.dot_general(a, b, (((0,), (0,)), ((), ())), preferred_element_type=F32)


def exact(a, b):
    return lax.dot_general(
        a, b, (((1,), (0,)), ((), ())), precision=lax.Precision.HIGHEST, preferred_element_type=F32
    )


def sigmoid(v):
    return 0.5 * jnp.tanh(0.5 * v) + 0.5


def spread(values, onehot):
    high = values.astype(BF)
    rest = (values - high.astype(F32)).astype(BF)
    return nn(high, onehot) + nn(rest, onehot)


def gather_heads(values, onehot):
    return nt(values.astype(BF), onehot)


def head_onehot(heads, inner):
    width = inner // heads
    row = lax.broadcasted_iota(jnp.int32, (heads, inner), 0)
    col = lax.broadcasted_iota(jnp.int32, (heads, inner), 1)
    low = row * width
    return jnp.where((col >= low) & (col < low + width), 1.0, 0.0).astype(BF)


def lower_ones(length):
    row = lax.broadcasted_iota(jnp.int32, (length, length), 0)
    col = lax.broadcasted_iota(jnp.int32, (length, length), 1)
    return jnp.where(row >= col, 1.0, 0.0).astype(F32)


def upper_ones(length):
    row = lax.broadcasted_iota(jnp.int32, (length, length), 0)
    col = lax.broadcasted_iota(jnp.int32, (length, length), 1)
    return jnp.where(row <= col, 1.0, 0.0).astype(F32)


def tiles(width):
    return [slice(at, min(at + LANES, width)) for at in range(0, width, LANES)]


def rows_of(j):
    return slice(j * CHUNK, (j + 1) * CHUNK)


def write_normed(dst, src, gain, step):
    rows = src.shape[0]

    def body(k, _):
        at = pl.ds(pl.multiple_of(k * step, step), step)
        v = src[at, :].astype(F32)
        scale = lax.rsqrt(jnp.mean(v * v, axis=1, keepdims=True) + EPS)
        dst[at, :] = (v * scale * gain).astype(BF)
        return 0

    lax.fori_loop(0, rows // step, body, 0)


def project_kernel(
    idx_ref, res_ref, halo_ref, win_ref, down_ref, up_ref, gain_ref, cw_ref, cb_ref, sb_ref, rate_ref,
    low_ref, gate_ref, xbc_ref, dact_ref, wid_ref, cum_ref, sig_ref, sloc_ref, dpre_ref, tot_ref, dtot_ref,
    nrm, ext, state, run, onehot,
):
    blk = pl.program_id(1)
    rows = res_ref.shape[1]
    heads, inner = onehot.shape
    mixer = cb_ref.shape[1]
    states = (mixer - inner) // 2
    proj = win_ref.shape[1]
    gain = gain_ref[...]

    @pl.when(blk == 0)
    def _():
        onehot[...] = head_onehot(heads, inner)
        state[...] = jnp.zeros_like(state)
        run[...] = jnp.zeros_like(run)
        v = halo_ref[0].astype(F32)
        scale = lax.rsqrt(jnp.mean(v * v, axis=1, keepdims=True) + EPS)
        first = (v * scale * gain).astype(BF)
        low_first = nt(first, down_ref[0]).astype(BF)
        for at in range(0, mixer, 2 * LANES):
            cols = slice(inner + at, inner + at + 2 * LANES)
            ext[0:RIM, at : at + 2 * LANES] = nn(first, win_ref[:, cols]) + nn(low_first, up_ref[0, :, cols])

    @pl.when(blk > 0)
    def _():
        ext[0:RIM, :] = ext[rows : rows + RIM, :]

    write_normed(nrm, res_ref.at[0], gain, 32)
    normed = nrm[...]
    low = nt(normed, down_ref[0]).astype(BF)
    low_ref[0] = low
    for at in range(0, mixer, 2 * LANES):
        cols = slice(inner + at, inner + at + 2 * LANES)
        ext[RIM : RIM + rows, at : at + 2 * LANES] = nn(normed, win_ref[:, cols]) + nn(low, up_ref[0, :, cols])
    cols = slice(inner + mixer, proj)
    raw = nn(normed, win_ref[:, cols]) + nn(low, up_ref[0, :, cols]) + sb_ref[...]
    for at in range(0, inner, 2 * LANES):
        cols = slice(at, at + 2 * LANES)
        gate_ref[0, :, cols] = (nn(normed, win_ref[:, cols]) + nn(low, up_ref[0, :, cols])).astype(BF)
    sig_ref[0] = sigmoid(raw)
    widths = jnp.maximum(raw, 0.0) + jnp.log1p(jnp.exp(-jnp.abs(raw)))
    wid_ref[0] = widths
    ones = lower_ones(CHUNK)
    for j in range(rows // CHUNK):
        for t in tiles(mixer):
            pre = cb_ref[:, t]
            for k in range(4):
                at = RIM - 3 + k + j * CHUNK
                pre = pre + cw_ref[k : k + 1, t] * ext[at : at + CHUNK, t]
            s = sigmoid(pre)
            act = pre * s
            xbc_ref[0, rows_of(j), t] = act.astype(BF)
            dact_ref[0, rows_of(j), t] = (s + act * (1.0 - s)).astype(BF)
    for j in range(rows // CHUNK):
        w = widths[rows_of(j)]
        c = exact(ones, w * rate_ref[...])
        cum_ref[0, rows_of(j)] = c
        last = c[CHUNK - 1 : CHUNK]
        tail = spread(jnp.exp(last - c) * w, onehot[...])
        weighted = jnp.concatenate(
            [(xbc_ref[0, rows_of(j), t].astype(F32) * tail[:, t]).astype(BF) for t in tiles(inner)], axis=1
        )
        inputs_t = xbc_ref[0, rows_of(j), inner : inner + states].astype(F32).T.astype(BF)
        update = nn(inputs_t, weighted)
        before = run[...]
        dpre_ref[0, j] = spread(jnp.exp(before), onehot[...])
        keep = spread(jnp.exp(jnp.broadcast_to(last, before.shape)), onehot[...])[0:1]
        for t in tiles(inner):
            old = state[:, t]
            sloc_ref[0, j, :, t] = old.astype(BF)
            state[:, t] = keep[:, t] * old + update[:, t]
        run[...] = before + last

    @pl.when(blk == pl.num_programs(1) - 1)
    def _():
        tot_ref[0] = state[...].astype(BF)
        dtot_ref[0] = spread(jnp.exp(run[...]), onehot[...])


def intra_kernel(xbc_ref, wid_ref, cum_ref, y_ref, onehot):
    heads, inner = onehot.shape
    states = (xbc_ref.shape[2] - inner) // 2
    width = inner // heads

    @pl.when((pl.program_id(0) == 0) & (pl.program_id(1) == 0))
    def _():
        onehot[...] = head_onehot(heads, inner)

    for j in range(xbc_ref.shape[1] // CHUNK):
        c = cum_ref[0, rows_of(j)] * LOG2E
        c_rows = c.T
        wide = spread(wid_ref[0, rows_of(j)], onehot[...])
        inputs = xbc_ref[0, rows_of(j), inner : inner + states]
        reads = xbc_ref[0, rows_of(j), inner + states :]
        scores = nt(reads, inputs) * lower_ones(CHUNK)
        lane = lax.broadcasted_iota(jnp.int32, (CHUNK, LANES), 1)
        per = LANES // width
        for k, t in enumerate(tiles(inner)):
            weighted = xbc_ref[0, rows_of(j), t].astype(F32) * wide[:, t]
            mixing, parts = [], []
            for p in range(per):
                h = k * per + p
                kernel = jnp.exp2(jnp.minimum(c[:, h : h + 1] - c_rows[h : h + 1, :], 0.0))
                mixing.append((kernel * scores).astype(BF))
                inside = (lane >= p * width) & (lane < (p + 1) * width)
                parts.append(jnp.where(inside, weighted, 0.0).astype(BF))
            y_ref[0, rows_of(j), t] = nn(jnp.concatenate(mixing, axis=1), jnp.concatenate(parts, axis=0)).astype(BF)


def output_kernel(
    idx_ref, y_ref, xbc_ref, gate_ref, cum_ref, sloc_ref, dpre_ref, tot_ref, dtot_ref, start_ref,
    res_ref, cot_ref, wout_ref, down_ref, up_ref, ggain_ref, skip_ref,
    out_ref, ggate_ref, dy_ref, dreads_ref, rowt_ref, gloc_ref, dsuf_ref, snext_ref, gown_ref, gup_ref, gdown_ref,
    onehot, snow, cur, adj, run, yp, gated, nout, gno, prod,
):
    blk = pl.program_id(1)
    rows = res_ref.shape[1]
    heads, inner = onehot.shape
    states = (xbc_ref.shape[2] - inner) // 2
    chunks = rows // CHUNK

    @pl.when(blk == 0)
    def _():
        onehot[...] = head_onehot(heads, inner)
        adj[...] = jnp.zeros_like(adj)
        run[...] = jnp.zeros_like(run)
        gup_ref[...] = jnp.zeros_like(gup_ref)
        gdown_ref[...] = jnp.zeros_like(gdown_ref)
        for t in tiles(inner):
            cur[:, t] = tot_ref[0, :, t].astype(F32) + dtot_ref[0, 0:1, t] * start_ref[0, :, t].astype(F32)

    reach = []
    for j in reversed(range(chunks)):
        snext_ref[0, j] = cur[...].astype(BF)
        for t in tiles(inner):
            s = sloc_ref[0, j, :, t].astype(F32) + dpre_ref[0, j, 0:1, t] * start_ref[0, :, t].astype(F32)
            cur[:, t] = s
            snow[j, :, t] = s.astype(BF)
        reads = xbc_ref[0, rows_of(j), inner + states :]
        carried = nn(reads, snow[j])
        grow = spread(jnp.exp(cum_ref[0, rows_of(j)]), onehot[...])
        reach.insert(0, grow)
        for t in tiles(inner):
            yp[rows_of(j), t] = y_ref[0, rows_of(j), t].astype(F32) + grow[:, t] * carried[:, t]

    scale, shrink = [], []
    for j in range(chunks):
        total = jnp.zeros((CHUNK, LANES), F32)
        for t in tiles(inner):
            y = yp[rows_of(j), t] + skip_ref[:, t] * xbc_ref[0, rows_of(j), t].astype(F32)
            g = gate_ref[0, rows_of(j), t].astype(F32)
            v = y * (g * sigmoid(g))
            gated[rows_of(j), t] = v
            total = total + v * v
        r = lax.rsqrt(jnp.sum(total, axis=1, keepdims=True) * (1.0 / inner) + EPS)
        scale.append(r)
        for t in tiles(inner):
            nout[rows_of(j), t] = (gated[rows_of(j), t] * r * ggain_ref[:, t]).astype(BF)

    normed_out = nout[...]
    cot = cot_ref[0]
    low_out = nt(normed_out, down_ref[0]).astype(BF)
    for at in range(0, out_ref.shape[2], 2 * LANES):
        t = slice(at, at + 2 * LANES)
        part = nn(normed_out, wout_ref[:, t]) + nn(low_out, up_ref[0, :, t])
        out_ref[0, :, t] = (res_ref[0, :, t].astype(F32) + part).astype(BF)
    grad_low = nt(cot, up_ref[0]).astype(BF)
    for at in range(0, inner, 2 * LANES):
        t = slice(at, at + 2 * LANES)
        gno[:, t] = nt(cot, wout_ref[t, :]) + nn(grad_low, down_ref[0, :, t])
    gup_ref[0] += tn(low_out, cot)
    gdown_ref[0] += tn(grad_low, normed_out)

    for j in range(chunks):
        total = jnp.zeros((CHUNK, LANES), F32)
        for t in tiles(inner):
            q = gno[rows_of(j), t] * ggain_ref[:, t]
            gno[rows_of(j), t] = q
            total = total + gated[rows_of(j), t] * q
        r = scale[j]
        shrink = jnp.sum(total, axis=1, keepdims=True) * (1.0 / inner) * (r * r * r)
        for t in tiles(inner):
            grad = r * gno[rows_of(j), t] - gated[rows_of(j), t] * shrink
            y_local = yp[rows_of(j), t]
            y = y_local + skip_ref[:, t] * xbc_ref[0, rows_of(j), t].astype(F32)
            g = gate_ref[0, rows_of(j), t].astype(F32)
            s = sigmoid(g)
            dy = grad * (g * s)
            dy_ref[0, rows_of(j), t] = dy.astype(BF)
            ggate_ref[0, rows_of(j), t] = (grad * y * (s * (1.0 + g * (1.0 - s)))).astype(BF)
            prod[rows_of(j), t] = (dy * y_local).astype(BF)
    rowt_ref[0] = nt(prod[...], onehot[...])

    for j in reversed(range(chunks)):
        grow = reach[j]
        scaled = jnp.concatenate(
            [(dy_ref[0, rows_of(j), t].astype(F32) * grow[:, t]).astype(BF) for t in tiles(inner)], axis=1
        )
        reads_t = xbc_ref[0, rows_of(j), inner + states :].astype(F32).T.astype(BF)
        update = nn(reads_t, scaled)
        dreads_ref[0, rows_of(j)] = nt(scaled, snow[j])
        last = cum_ref[0, j * CHUNK + CHUNK - 1 : j * CHUNK + CHUNK]
        before = run[...]
        dsuf_ref[0, j] = spread(jnp.exp(before), onehot[...])
        keep = grow[CHUNK - 1 : CHUNK]
        for t in tiles(inner):
            old = adj[:, t]
            gloc_ref[0, j, :, t] = old.astype(BF)
            adj[:, t] = keep[:, t] * old + update[:, t]
        run[...] = before + last

    @pl.when(blk == pl.num_programs(1) - 1)
    def _():
        gown_ref[0] = adj[...].astype(BF)


def intra_back_kernel(xbc_ref, wid_ref, cum_ref, dy_ref, dreads_ref, z_ref, dinputs_ref, dreads_out_ref, onehot):
    heads, inner = onehot.shape
    states = (xbc_ref.shape[2] - inner) // 2
    width = inner // heads
    per = LANES // width

    @pl.when((pl.program_id(0) == 0) & (pl.program_id(1) == 0))
    def _():
        onehot[...] = head_onehot(heads, inner)

    for j in range(xbc_ref.shape[1] // CHUNK):
        c = cum_ref[0, rows_of(j)] * LOG2E
        c_rows = c.T
        wide = spread(wid_ref[0, rows_of(j)], onehot[...])
        inputs = xbc_ref[0, rows_of(j), inner : inner + states]
        reads = xbc_ref[0, rows_of(j), inner + states :]
        mask = upper_ones(CHUNK)
        scores_t = nt(inputs, reads) * mask
        lane = lax.broadcasted_iota(jnp.int32, (CHUNK, LANES), 1)
        total = jnp.zeros((CHUNK, CHUNK), F32)
        for k, t in enumerate(tiles(inner)):
            weighted = xbc_ref[0, rows_of(j), t].astype(F32) * wide[:, t]
            grads = dy_ref[0, rows_of(j), t]
            mixing, left, right = [], [], []
            for p in range(per):
                inside = (lane >= p * width) & (lane < (p + 1) * width)
                left.append(jnp.where(inside, weighted, 0.0).astype(BF))
                right.append(jnp.where(inside, grads.astype(F32), 0.0).astype(BF))
            products = nt(jnp.concatenate(left, axis=0), grads)
            for p in range(per):
                h = k * per + p
                kernel = jnp.exp2(jnp.minimum(c_rows[h : h + 1, :] - c[:, h : h + 1], 0.0))
                mixing.append((kernel * scores_t).astype(BF))
                total = total + kernel * products[p * CHUNK : (p + 1) * CHUNK]
            z_ref[0, rows_of(j), t] = nn(jnp.concatenate(mixing, axis=1), jnp.concatenate(right, axis=0)).astype(BF)
        total = total * mask
        dinputs_ref[0, rows_of(j)] = nn(total.astype(BF), reads)
        dreads_out_ref[0, rows_of(j)] = dreads_ref[0, rows_of(j)] + nn(total.T.astype(BF), inputs)


def adjoint_kernel(
    xbc_ref, dact_ref, wid_ref, cum_ref, sig_ref, dy_ref, z_ref, dinputs_ref, dreads_ref, rowt_ref,
    gloc_ref, dsuf_ref, end_ref, snext_ref, skip_ref, rate_ref,
    gpre_ref, graw_ref,
    onehot, adj, prod,
):
    heads, inner = onehot.shape
    states = (xbc_ref.shape[2] - inner) // 2

    @pl.when((pl.program_id(0) == 0) & (pl.program_id(1) == 0))
    def _():
        onehot[...] = head_onehot(heads, inner)

    for j in range(xbc_ref.shape[1] // CHUNK):
        at = rows_of(j)
        overlap = []
        for t in tiles(inner):
            g = gloc_ref[0, j, :, t].astype(F32) + dsuf_ref[0, j, 0:1, t] * end_ref[0, :, t].astype(F32)
            adj[:, t] = g.astype(BF)
            overlap.append(jnp.sum(g * snext_ref[0, j, :, t].astype(F32), axis=0, keepdims=True))
        held = jnp.broadcast_to(jnp.concatenate(overlap, axis=1), (8, inner))
        high = held.astype(BF)
        held = (nt(high, onehot[...]) + nt((held - high.astype(F32)).astype(BF), onehot[...]))[0:1]
        c = cum_ref[0, at]
        last = c[CHUNK - 1 : CHUNK]
        w = wid_ref[0, at]
        wide = spread(w, onehot[...])
        tail = spread(jnp.exp(last - c), onehot[...])
        inputs = xbc_ref[0, at, inner : inner + states]
        carried = nn(inputs, adj[...])
        weighted = []
        for t in tiles(inner):
            x = xbc_ref[0, at, t].astype(F32)
            z = z_ref[0, at, t].astype(F32) + tail[:, t] * carried[:, t]
            prod[:, t] = (x * z).astype(BF)
            grad = wide[:, t] * z + skip_ref[:, t] * dy_ref[0, at, t].astype(F32)
            gpre_ref[0, at, t] = (grad * dact_ref[0, at, t].astype(F32)).astype(BF)
            weighted.append((x * (wide[:, t] * tail[:, t])).astype(BF))
        dinputs = dinputs_ref[0, at] + nt(jnp.concatenate(weighted, axis=1), adj[...])
        t = slice(inner, inner + states)
        gpre_ref[0, at, t] = (dinputs * dact_ref[0, at, t].astype(F32)).astype(BF)
        t = slice(inner + states, inner + 2 * states)
        gpre_ref[0, at, t] = (dreads_ref[0, at] * dact_ref[0, at, t].astype(F32)).astype(BF)
        direct = nt(prod[...], onehot[...])
        grad_rate = held + exact(upper_ones(CHUNK), rowt_ref[0, at] - w * direct)
        graw_ref[0, at] = (direct + rate_ref[...] * grad_rate) * sig_ref[0, at]


def input_kernel(
    idx_ref, gpre_ref, rim_ref, ggate_ref, graw_ref, low_ref, res_ref, cot_ref, win_ref, down_ref, up_ref, gain_ref, cw_ref,
    gin_ref, gup_ref, gdown_ref,
    ext, gp, gn, nrm,
):
    blk = pl.program_id(1)
    rows = res_ref.shape[1]
    inner = ggate_ref.shape[2]
    mixer = gpre_ref.shape[2]
    proj = win_ref.shape[1]
    model = res_ref.shape[2]

    @pl.when(blk == 0)
    def _():
        ext[rows : rows + RIM, :] = rim_ref[0].astype(F32)
        gup_ref[...] = jnp.zeros_like(gup_ref)
        gdown_ref[...] = jnp.zeros_like(gdown_ref)

    @pl.when(blk > 0)
    def _():
        ext[rows : rows + RIM, :] = ext[0:RIM, :]

    for j in range(rows // CHUNK):
        for t in tiles(mixer):
            ext[rows_of(j), t] = gpre_ref[0, rows_of(j), t].astype(F32)
    for j in range(rows // CHUNK):
        for t in tiles(mixer):
            total = None
            for k in range(4):
                at = 3 - k + j * CHUNK
                term = cw_ref[k : k + 1, t] * ext[at : at + CHUNK, t]
                total = term if total is None else total + term
            gp[rows_of(j), inner + t.start : inner + t.stop] = total.astype(BF)
    gp[:, :inner] = ggate_ref[0]
    gp[:, inner + mixer : proj] = graw_ref[0].astype(BF)
    whole = slice(0, inner + mixer)
    rest = slice(inner + mixer, proj)
    grads, grads_rest = gp[:, whole], gp[:, rest]
    grad_low = (nt(grads, up_ref[0, :, whole]) + nt(grads_rest, up_ref[0, :, rest])).astype(BF)
    for at in range(0, model, 2 * LANES):
        t = slice(at, at + 2 * LANES)
        gn[:, t] = nt(grads, win_ref[t, whole]) + nt(grads_rest, win_ref[t, rest]) + nn(grad_low, down_ref[0, :, t])

    def body(k, _):
        at = pl.ds(pl.multiple_of(k * 32, 32), 32)
        v = res_ref[0, at, :].astype(F32)
        u = lax.rsqrt(jnp.mean(v * v, axis=1, keepdims=True) + EPS)
        nrm[at, :] = (v * u * gain_ref[...]).astype(BF)
        w = gn[at, :] * gain_ref[...]
        m = jnp.mean(v * w, axis=1, keepdims=True)
        gin_ref[0, at, :] = (cot_ref[0, at, :].astype(F32) + u * w - v * (u * u * u * m)).astype(BF)
        return 0

    lax.fori_loop(0, rows // 32, body, 0)
    gup_ref[0, :, whole] += tn(low_ref[0], grads)
    gup_ref[0, :, rest] += tn(low_ref[0], grads_rest)
    gdown_ref[0] += tn(grad_low, nrm[...])


def carry_kernel(count, backwards, tot_ref, dec_ref, out_ref, theirs, theirs_dec, prefix, passed, tail, mine, sems):
    dp = lax.axis_index("dp")
    seq = lax.axis_index("seq")
    rank = count - 1 - seq if backwards else seq
    pairs = count // 2
    pair, side = rank // 2, rank % 2
    seqs, states, inner = tot_ref.shape
    half = inner // 2
    parts = theirs.shape[0] // seqs
    wide = half // parts

    def device(other):
        return (count - 1 - other if backwards else other, dp)

    partner = device(pair * 2 + 1 - side)
    ahead = device(lax.rem(pair + 1, pairs) * 2 + side)
    behind = device(lax.rem(pair + pairs - 1, pairs) * 2 + side)
    barrier = pltpu.get_barrier_semaphore()
    for other in (partner, ahead, behind):
        pl.semaphore_signal(barrier, inc=1, device_id=other, device_id_type=MESH)
    pl.semaphore_wait(barrier, 3)

    def send(kind, n, src, dst, to):
        return pltpu.make_async_remote_copy(
            src_ref=src, dst_ref=dst, send_sem=sems.at[0, kind, n], recv_sem=sems.at[1, kind, n],
            device_id=to, device_id_type=MESH,
        )

    blocks = [(s, q) for s in range(seqs) for q in range(parts)]

    def cols(base, q):
        return pl.ds(pl.multiple_of(base * half + q * wide, LANES), wide)

    decs = send(3, 0, dec_ref, theirs_dec, partner)
    decs.start()
    swaps = []
    for n, (s, q) in enumerate(blocks):
        copy = send(0, n, tot_ref.at[s, :, cols(1 - side, q)], theirs.at[n], partner)
        copy.start()
        swaps.append(copy)
    decs.wait()
    hops = [send(1, n, passed.at[n], prefix.at[n], ahead) for n in range(len(blocks))]
    gives = [send(2, n, tail.at[n], mine.at[n], partner) for n in range(len(blocks))]
    for n, (s, q) in enumerate(blocks):
        swaps[n].wait()

        @pl.when(pair == 0)
        def _(n=n):
            prefix[n] = jnp.zeros_like(prefix[n])

        @pl.when(pair > 0)
        def _(n=n):
            hops[n].wait_recv()

        own_dec = dec_ref[s, 0:1, cols(side, q)]
        their_dec = theirs_dec[s, 0:1, cols(side, q)]
        own = tot_ref[s, :, cols(side, q)].astype(F32)
        other = theirs[n].astype(F32)
        before = prefix[n].astype(F32)
        first = jnp.where(side == 0, own, other)
        second = jnp.where(side == 0, other, own)
        first_dec = jnp.where(side == 0, own_dec, their_dec)
        second_dec = jnp.where(side == 0, their_dec, own_dec)
        middle = first_dec * before + first
        passed[n] = (second_dec * middle + second).astype(BF)

        @pl.when(pair < pairs - 1)
        def _(n=n):
            hops[n].start()

        out_ref[s, :, cols(side, q)] = jnp.where(side == 0, before, middle).astype(BF)
        tail[n] = jnp.where(side == 0, middle, before).astype(BF)
        gives[n].start()
    for n, (s, q) in enumerate(blocks):
        gives[n].wait()
        out_ref[s, :, cols(1 - side, q)] = mine[n]

        @pl.when(pair < pairs - 1)
        def _(n=n):
            hops[n].wait_send()


def carry(total, decay, count, backwards):
    seqs, states, inner = total.shape
    parts = 2
    blocks = seqs * parts
    slot = pltpu.VMEM((blocks, states, inner // 2 // parts), BF)
    return pl.pallas_call(
        functools.partial(carry_kernel, count, backwards),
        out_shape=jax.ShapeDtypeStruct(total.shape, BF),
        in_specs=[pl.BlockSpec(memory_space=pltpu.VMEM)] * 2,
        out_specs=pl.BlockSpec(memory_space=pltpu.VMEM),
        scratch_shapes=[
            slot,
            pltpu.VMEM(decay.shape, F32),
            slot,
            slot,
            slot,
            slot,
            pltpu.SemaphoreType.DMA((2, 4, blocks)),
        ],
        compiler_params=pltpu.CompilerParams(
            collective_id=2 if backwards else 1, has_side_effects=True, vmem_limit_bytes=VMEM_LIMIT
        ),
        name="adjoint_carry" if backwards else "state_carry",
    )(total, decay)


def call(kernel, grid, ins, outs, scratch, name, prefetch=()):
    arrays = [a for a, _, _ in ins]
    specs = [pl.BlockSpec(block, index) for _, block, index in ins]
    return pl.pallas_call(
        kernel,
        out_shape=[jax.ShapeDtypeStruct(shape, kind) for shape, kind, _, _ in outs],
        grid_spec=pltpu.PrefetchScalarGridSpec(
            num_scalar_prefetch=len(prefetch),
            grid=grid,
            in_specs=specs,
            out_specs=[pl.BlockSpec(block, index) for _, _, block, index in outs],
            scratch_shapes=scratch,
        ),
        compiler_params=pltpu.CompilerParams(
            dimension_semantics=("arbitrary",) * len(grid), vmem_limit_bytes=VMEM_LIMIT
        ),
        name=name,
    )(*prefetch, *arrays)


def on_device(
    residual_in,
    cotangent,
    norm_gain,
    in_weight,
    conv_weight,
    conv_bias,
    step_bias,
    decay_log,
    skip_gain,
    gate_gain,
    out_weight,
    in_down,
    in_up,
    out_down,
    out_up,
    in_index,
    out_index,
):
    seqs, tokens, model = residual_in.shape
    heads = step_bias.shape[0]
    inner = gate_gain.shape[0]
    mixer = conv_weight.shape[0]
    states = (mixer - inner) // 2
    rank = in_up.shape[1]
    proj = in_weight.shape[1]
    seq_count = lax.axis_size("seq")
    dp_count = lax.axis_size("dp")
    adapters = in_down.shape[0] * dp_count
    chunks = tokens // CHUNK
    blocks = tokens // BLOCK
    per = BLOCK // CHUNK

    rate = -jnp.exp(decay_log)[None, :]
    taps = conv_weight.T
    gain = norm_gain[None, :]
    skip_wide = jnp.repeat(skip_gain, inner // heads)[None, :]
    route = [(i, i + 1) for i in range(seq_count - 1)]
    halo = lax.ppermute(residual_in[:, tokens - RIM :], "seq", route)

    def gathered(part):
        return lax.all_gather(part, "dp", axis=0, tiled=True)

    w_in = gathered(in_weight)
    w_out = gathered(out_weight)
    full_in_down = gathered(in_down.transpose(0, 2, 1))
    full_in_up = gathered(in_up)
    full_out_down = gathered(out_down.transpose(0, 2, 1))
    full_out_up = gathered(out_up)

    grid = (seqs, blocks)

    def fixed(a):
        return (a, a.shape, lambda s, b, *_: (0,) * a.ndim)

    def by_seq(a):
        return (a, (1,) + a.shape[1:], lambda s, b, *_: (s,) + (0,) * (a.ndim - 1))

    def picked(a):
        return (a, (1,) + a.shape[1:], lambda s, b, idx, *_: (idx[s],) + (0,) * (a.ndim - 1))

    def by_row(a, turn=False):
        if turn:
            return (a, (1, BLOCK, a.shape[2]), lambda s, b, *_: (s, blocks - 1 - b, 0))
        return (a, (1, BLOCK, a.shape[2]), lambda s, b, *_: (s, b, 0))

    def by_chunk(a, turn=False):
        if turn:
            return (a, (1, per) + a.shape[2:], lambda s, b, *_: (s, blocks - 1 - b, 0, 0))
        return (a, (1, per) + a.shape[2:], lambda s, b, *_: (s, b, 0, 0))

    def out(pick, shape, kind, *rest):
        spec = pick(jax.ShapeDtypeStruct(shape, kind), *rest)
        return (shape, kind, spec[1], spec[2])

    row_of = lambda width: (seqs, tokens, width)
    low, gate, xbc, dact, wid, cum, sig, sloc, dpre, tot, dtot = call(
        project_kernel,
        grid,
        [
            by_row(residual_in),
            by_seq(halo),
            fixed(w_in),
            picked(full_in_down),
            picked(full_in_up),
            fixed(gain),
            fixed(taps),
            fixed(conv_bias[None, :]),
            fixed(step_bias[None, :]),
            fixed(rate),
        ],
        [
            out(by_row, row_of(rank), BF),
            out(by_row, row_of(inner), BF),
            out(by_row, row_of(mixer), BF),
            out(by_row, row_of(mixer), BF),
            out(by_row, row_of(heads), F32),
            out(by_row, row_of(heads), F32),
            out(by_row, row_of(heads), F32),
            out(by_chunk, (seqs, chunks, states, inner), BF),
            out(by_chunk, (seqs, chunks, 8, inner), F32),
            out(by_seq, (seqs, states, inner), BF),
            out(by_seq, (seqs, 8, inner), F32),
        ],
        [
            pltpu.VMEM((BLOCK, model), BF),
            pltpu.VMEM((BLOCK + RIM, mixer), F32),
            pltpu.VMEM((states, inner), F32),
            pltpu.VMEM((8, heads), F32),
            pltpu.VMEM((heads, inner), BF),
        ],
        "project",
        prefetch=(in_index[:, 0],),
    )
    start = carry(tot, dtot, seq_count, False)
    (y_intra,) = call(
        intra_kernel,
        grid,
        [by_row(xbc), by_row(wid), by_row(cum)],
        [out(by_row, row_of(inner), BF)],
        [pltpu.VMEM((heads, inner), BF)],
        "intra",
    )
    block_out, ggate, dy, dreads, rowt, gloc, dsuf, snext, gown, gout_up, gout_down = call(
        output_kernel,
        grid,
        [
            by_row(y_intra, True),
            by_row(xbc, True),
            by_row(gate, True),
            by_row(cum, True),
            by_chunk(sloc, True),
            by_chunk(dpre, True),
            by_seq(tot),
            by_seq(dtot),
            by_seq(start),
            by_row(residual_in, True),
            by_row(cotangent, True),
            fixed(w_out),
            picked(full_out_down),
            picked(full_out_up),
            fixed(gate_gain[None, :]),
            fixed(skip_wide),
        ],
        [
            out(by_row, row_of(model), BF, True),
            out(by_row, row_of(inner), BF, True),
            out(by_row, row_of(inner), BF, True),
            out(by_row, row_of(states), F32, True),
            out(by_row, row_of(heads), F32, True),
            out(by_chunk, (seqs, chunks, states, inner), BF, True),
            out(by_chunk, (seqs, chunks, 8, inner), F32, True),
            out(by_chunk, (seqs, chunks, states, inner), BF, True),
            out(by_seq, (seqs, states, inner), BF),
            out(by_seq, (seqs, rank, model), F32),
            out(by_seq, (seqs, rank, inner), F32),
        ],
        [
            pltpu.VMEM((heads, inner), BF),
            pltpu.VMEM((per, states, inner), BF),
            pltpu.VMEM((states, inner), F32),
            pltpu.VMEM((states, inner), F32),
            pltpu.VMEM((8, heads), F32),
            pltpu.VMEM((BLOCK, inner), F32),
            pltpu.VMEM((BLOCK, inner), F32),
            pltpu.VMEM((BLOCK, inner), BF),
            pltpu.VMEM((BLOCK, inner), F32),
            pltpu.VMEM((BLOCK, inner), BF),
        ],
        "output",
        prefetch=(out_index[:, 0],),
    )
    end = carry(gown, dtot, seq_count, True)
    z, dinputs, dreads = call(
        intra_back_kernel,
        grid,
        [by_row(xbc), by_row(wid), by_row(cum), by_row(dy), by_row(dreads)],
        [out(by_row, row_of(inner), BF), out(by_row, row_of(states), F32), out(by_row, row_of(states), F32)],
        [pltpu.VMEM((heads, inner), BF)],
        "intra_back",
    )
    gpre, graw = call(
        adjoint_kernel,
        grid,
        [
            by_row(xbc),
            by_row(dact),
            by_row(wid),
            by_row(cum),
            by_row(sig),
            by_row(dy),
            by_row(z),
            by_row(dinputs),
            by_row(dreads),
            by_row(rowt),
            by_chunk(gloc),
            by_chunk(dsuf),
            by_seq(end),
            by_chunk(snext),
            fixed(skip_wide),
            fixed(rate),
        ],
        [out(by_row, row_of(mixer), BF), out(by_row, row_of(heads), F32)],
        [pltpu.VMEM((heads, inner), BF), pltpu.VMEM((states, inner), BF), pltpu.VMEM((CHUNK, inner), BF)],
        "adjoint",
    )
    rim = lax.ppermute(gpre[:, :RIM], "seq", [(j, i) for i, j in route])
    grad_input, gin_up, gin_down = call(
        input_kernel,
        grid,
        [
            by_row(gpre, True),
            by_seq(rim),
            by_row(ggate, True),
            by_row(graw, True),
            by_row(low, True),
            by_row(residual_in, True),
            by_row(cotangent, True),
            fixed(w_in),
            picked(full_in_down),
            picked(full_in_up),
            fixed(gain),
            fixed(taps),
        ],
        [
            out(by_row, row_of(model), BF, True),
            out(by_seq, (seqs, rank, proj), F32),
            out(by_seq, (seqs, rank, model), F32),
        ],
        [
            pltpu.VMEM((BLOCK + RIM, mixer), F32),
            pltpu.VMEM((BLOCK, proj), BF),
            pltpu.VMEM((BLOCK, model), F32),
            pltpu.VMEM((BLOCK, model), BF),
        ],
        "input",
        prefetch=(in_index[:, 0],),
    )

    def owned(grads, index):
        grads = lax.psum(grads.astype(BF), "seq")
        onehot = (index[:, 0][None, :] == jnp.arange(adapters)[:, None]).astype(BF)
        mine = jnp.einsum("as,srn->arn", onehot, grads, preferred_element_type=F32).astype(BF)
        return lax.psum_scatter(mine, "dp", scatter_dimension=0, tiled=True).astype(F32)

    from_in = owned(jnp.concatenate([gin_up, gin_down], axis=2), in_index)
    from_out = owned(jnp.concatenate([gout_up, gout_down], axis=2), out_index)
    return (
        block_out,
        grad_input,
        from_in[:, :, proj:].transpose(0, 2, 1),
        from_in[:, :, :proj],
        from_out[:, :, model:].transpose(0, 2, 1),
        from_out[:, :, :model],
    )


def solution(mesh):
    rows = P("dp", "seq", None)
    split = P("dp", None, None)
    return jax.shard_map(
        on_device,
        mesh=mesh,
        in_specs=(
            rows,
            rows,
            P(),
            P("dp", None),
            P(),
            P(),
            P(),
            P(),
            P(),
            P(),
            P("dp", None),
            split,
            split,
            split,
            split,
            P("dp", None),
            P("dp", None),
        ),
        out_specs=(rows, rows, split, split, split, split),
        check_vma=False,
    )
```

```python
import functools

import jax
import jax.numpy as jnp
from jax import lax
from jax.experimental import pallas as pl
from jax.experimental.pallas import tpu as pltpu
from jax.sharding import PartitionSpec as P

EPS = 1e-05
CHUNK = 128
BLOCK = 256
RIM = 16
LANES = 128
LOG2E = 1.4426950408889634
BF = jnp.bfloat16
F32 = jnp.float32
MESH = pl.DeviceIdType.MESH
VMEM_LIMIT = 56 * 2**20
CONV_BIAS, GATE_GAIN, NORM_GAIN, SKIP, STEP_BIAS, RATE = (slice(4 + n, 5 + n) for n in range(6))


def nn(a, b):
    return lax.dot_general(a, b, (((1,), (0,)), ((), ())), preferred_element_type=F32)


def nt(a, b):
    return lax.dot_general(a, b, (((1,), (1,)), ((), ())), preferred_element_type=F32)


def tn(a, b):
    return lax.dot_general(a, b, (((0,), (0,)), ((), ())), preferred_element_type=F32)


def exact(a, b):
    return lax.dot_general(
        a, b, (((1,), (0,)), ((), ())), precision=lax.Precision.HIGHEST, preferred_element_type=F32
    )


def sigmoid(v):
    return 0.5 * jnp.tanh(0.5 * v) + 0.5


def spread(values, onehot):
    high = values.astype(BF)
    rest = (values - high.astype(F32)).astype(BF)
    return nn(high, onehot) + nn(rest, onehot)


def gather_heads(values, onehot):
    return nt(values.astype(BF), onehot)


def head_onehot(heads, inner):
    width = inner // heads
    row = lax.broadcasted_iota(jnp.int32, (heads, inner), 0)
    col = lax.broadcasted_iota(jnp.int32, (heads, inner), 1)
    low = row * width
    return jnp.where((col >= low) & (col < low + width), 1.0, 0.0).astype(BF)


def lower_ones(length):
    row = lax.broadcasted_iota(jnp.int32, (length, length), 0)
    col = lax.broadcasted_iota(jnp.int32, (length, length), 1)
    return jnp.where(row >= col, 1.0, 0.0).astype(F32)


def upper_ones(length):
    row = lax.broadcasted_iota(jnp.int32, (length, length), 0)
    col = lax.broadcasted_iota(jnp.int32, (length, length), 1)
    return jnp.where(row <= col, 1.0, 0.0).astype(F32)


def tiles(width):
    return [slice(at, min(at + LANES, width)) for at in range(0, width, LANES)]


def rows_of(j):
    return slice(j * CHUNK, (j + 1) * CHUNK)


def write_normed(dst, src, gain, step):
    rows = src.shape[0]

    def body(k, _):
        at = pl.ds(pl.multiple_of(k * step, step), step)
        v = src[at, :].astype(F32)
        scale = lax.rsqrt(jnp.mean(v * v, axis=1, keepdims=True) + EPS)
        dst[at, :] = (v * scale * gain).astype(BF)
        return 0

    lax.fori_loop(0, rows // step, body, 0)


def project_kernel(
    idx_ref, res_ref, halo_ref, win_ref, down_ref, up_ref, par_ref,
    low_ref, xbc_ref, dact_ref, wid_ref, cum_ref, sig_ref, sloc_ref, dpre_ref, tot_ref, dtot_ref,
    nrm, ext, state, run, onehot,
):
    blk = pl.program_id(1)
    rows = res_ref.shape[1]
    heads, inner = onehot.shape
    mixer = xbc_ref.shape[2]
    states = (mixer - inner) // 2
    gain = par_ref[NORM_GAIN, : res_ref.shape[2]]

    @pl.when(blk == 0)
    def _():
        onehot[...] = head_onehot(heads, inner)
        state[...] = jnp.zeros_like(state)
        run[...] = jnp.zeros_like(run)
        v = halo_ref[0].astype(F32)
        scale = lax.rsqrt(jnp.mean(v * v, axis=1, keepdims=True) + EPS)
        first = (v * scale * gain).astype(BF)
        low_first = nt(first, down_ref[0]).astype(BF)
        for at in range(0, mixer, 2 * LANES):
            cols = slice(inner + at, inner + at + 2 * LANES)
            t = slice(at, at + 2 * LANES)
            v2 = nn(first, win_ref[:, t]) + nn(low_first, up_ref[0, :, cols])
            ext[at // LANES, 0:RIM, :] = v2[:, :LANES]
            ext[at // LANES + 1, 0:RIM, :] = v2[:, LANES:]

    @pl.when(blk > 0)
    def _():
        ext[:, 0:RIM, :] = ext[:, rows : rows + RIM, :]

    write_normed(nrm, res_ref.at[0], gain, 32)
    normed = nrm[...]
    low = nt(normed, down_ref[0]).astype(BF)
    low_ref[0] = low
    for at in range(0, mixer, 2 * LANES):
        cols = slice(inner + at, inner + at + 2 * LANES)
        t = slice(at, at + 2 * LANES)
        v2 = nn(normed, win_ref[:, t]) + nn(low, up_ref[0, :, cols])
        ext[at // LANES, RIM : RIM + rows, :] = v2[:, :LANES]
        ext[at // LANES + 1, RIM : RIM + rows, :] = v2[:, LANES:]
    cols = slice(inner + mixer, inner + mixer + heads)
    raw = nn(normed, win_ref[:, mixer : mixer + heads]) + nn(low, up_ref[0, :, cols]) + par_ref[STEP_BIAS, :heads]
    sig_ref[0] = sigmoid(raw)
    widths = jnp.maximum(raw, 0.0) + jnp.log1p(jnp.exp(-jnp.abs(raw)))
    wid_ref[0] = widths
    ones = lower_ones(CHUNK)
    for j in range(rows // CHUNK):
        for t in tiles(mixer):
            pre = par_ref[CONV_BIAS, t]
            for k in range(4):
                at = RIM - 3 + k + j * CHUNK
                pre = pre + par_ref[k : k + 1, t] * ext[t.start // LANES, at : at + CHUNK, :]
            s = sigmoid(pre)
            act = pre * s
            xbc_ref[0, rows_of(j), t] = act.astype(BF)
            dact_ref[0, rows_of(j), t] = (s + act * (1.0 - s)).astype(BF)
    for j in range(rows // CHUNK):
        w = widths[rows_of(j)]
        c = exact(ones, w * par_ref[RATE, :heads])
        cum_ref[0, rows_of(j)] = c
        last = c[CHUNK - 1 : CHUNK]
        tail = spread(jnp.exp(last - c) * w, onehot[...])
        weighted = jnp.concatenate(
            [(xbc_ref[0, rows_of(j), t].astype(F32) * tail[:, t]).astype(BF) for t in tiles(inner)], axis=1
        )
        inputs_t = xbc_ref[0, rows_of(j), inner : inner + states].astype(F32).T.astype(BF)
        update = nn(inputs_t, weighted)
        before = run[...]
        dpre_ref[0, j] = spread(jnp.exp(before), onehot[...])
        keep = spread(jnp.exp(jnp.broadcast_to(last, before.shape)), onehot[...])[0:1]
        for t in tiles(inner):
            old = state[:, t]
            sloc_ref[0, j, :, t] = old.astype(BF)
            state[:, t] = keep[:, t] * old + update[:, t]
        run[...] = before + last

    @pl.when(blk == pl.num_programs(1) - 1)
    def _():
        tot_ref[0] = state[...].astype(BF)
        dtot_ref[0] = spread(jnp.exp(run[...]), onehot[...])


def intra_kernel(
    idx_ref, xbc_ref, wid_ref, cum_ref, res_ref, low_ref, win_ref, up_ref, par_ref, y_ref, gate_ref, nrm, onehot
):
    heads, inner = onehot.shape
    write_normed(nrm, res_ref.at[0], par_ref[NORM_GAIN, : res_ref.shape[2]], 32)
    normed, low = nrm[...], low_ref[0]
    for at in range(0, inner, 2 * LANES):
        t = slice(at, at + 2 * LANES)
        gate_ref[0, :, t] = (nn(normed, win_ref[:, t]) + nn(low, up_ref[0, :, t])).astype(BF)

    states = (xbc_ref.shape[2] - inner) // 2
    width = inner // heads

    @pl.when((pl.program_id(0) == 0) & (pl.program_id(1) == 0))
    def _():
        onehot[...] = head_onehot(heads, inner)

    for j in range(xbc_ref.shape[1] // CHUNK):
        c = cum_ref[0, rows_of(j)] * LOG2E
        c_rows = c.T
        wide = spread(wid_ref[0, rows_of(j)], onehot[...])
        inputs = xbc_ref[0, rows_of(j), inner : inner + states]
        reads = xbc_ref[0, rows_of(j), inner + states :]
        scores = nt(reads, inputs) * lower_ones(CHUNK)
        lane = lax.broadcasted_iota(jnp.int32, (CHUNK, LANES), 1)
        per = LANES // width
        for k, t in enumerate(tiles(inner)):
            weighted = xbc_ref[0, rows_of(j), t].astype(F32) * wide[:, t]
            mixing, parts = [], []
            for p in range(per):
                h = k * per + p
                kernel = jnp.exp2(jnp.minimum(c[:, h : h + 1] - c_rows[h : h + 1, :], 0.0))
                mixing.append((kernel * scores).astype(BF))
                inside = (lane >= p * width) & (lane < (p + 1) * width)
                parts.append(jnp.where(inside, weighted, 0.0).astype(BF))
            y_ref[0, rows_of(j), t] = nn(jnp.concatenate(mixing, axis=1), jnp.concatenate(parts, axis=0)).astype(BF)


def output_kernel(
    idx_ref, y_ref, xbc_ref, gate_ref, cum_ref, sloc_ref, dpre_ref, tot_ref, dtot_ref, start_ref,
    res_ref, cot_ref, wout_ref, down_ref, up_ref, par_ref,
    out_ref, ggate_ref, dy_ref, dreads_ref, rowt_ref, gloc_ref, dsuf_ref, snext_ref, gown_ref, gup_ref, gdown_ref,
    onehot, snow, cur, adj, run, yp, gated, nout, gno, prod,
):
    blk = pl.program_id(1)
    rows = res_ref.shape[1]
    heads, inner = onehot.shape
    states = (xbc_ref.shape[2] - inner) // 2
    chunks = rows // CHUNK

    @pl.when(blk == 0)
    def _():
        onehot[...] = head_onehot(heads, inner)
        adj[...] = jnp.zeros_like(adj)
        run[...] = jnp.zeros_like(run)
        gup_ref[...] = jnp.zeros_like(gup_ref)
        gdown_ref[...] = jnp.zeros_like(gdown_ref)
        for t in tiles(inner):
            cur[:, t] = tot_ref[0, :, t].astype(F32) + dtot_ref[0, 0:1, t] * start_ref[0, :, t].astype(F32)

    reach = []
    for j in reversed(range(chunks)):
        snext_ref[0, j] = cur[...].astype(BF)
        for t in tiles(inner):
            s = sloc_ref[0, j, :, t].astype(F32) + dpre_ref[0, j, 0:1, t] * start_ref[0, :, t].astype(F32)
            cur[:, t] = s
            snow[j, :, t] = s.astype(BF)
        reads = xbc_ref[0, rows_of(j), inner + states :]
        carried = nn(reads, snow[j])
        grow = spread(jnp.exp(cum_ref[0, rows_of(j)]), onehot[...])
        reach.insert(0, grow)
        for t in tiles(inner):
            yp[rows_of(j), t] = y_ref[0, rows_of(j), t].astype(F32) + grow[:, t] * carried[:, t]

    scale, shrink = [], []
    for j in range(chunks):
        total = jnp.zeros((CHUNK, LANES), F32)
        for t in tiles(inner):
            y = yp[rows_of(j), t] + par_ref[SKIP, t] * xbc_ref[0, rows_of(j), t].astype(F32)
            g = gate_ref[0, rows_of(j), t].astype(F32)
            v = y * (g * sigmoid(g))
            gated[rows_of(j), t] = v
            total = total + v * v
        r = lax.rsqrt(jnp.sum(total, axis=1, keepdims=True) * (1.0 / inner) + EPS)
        scale.append(r)
        for t in tiles(inner):
            nout[rows_of(j), t] = (gated[rows_of(j), t] * r * par_ref[GATE_GAIN, t]).astype(BF)

    normed_out = nout[...]
    cot = cot_ref[0]
    low_out = nt(normed_out, down_ref[0]).astype(BF)
    for at in range(0, out_ref.shape[2], 2 * LANES):
        t = slice(at, at + 2 * LANES)
        part = nn(normed_out, wout_ref[:, t]) + nn(low_out, up_ref[0, :, t])
        out_ref[0, :, t] = (res_ref[0, :, t].astype(F32) + part).astype(BF)
    grad_low = nt(cot, up_ref[0]).astype(BF)
    for at in range(0, inner, 2 * LANES):
        t = slice(at, at + 2 * LANES)
        gno[:, t] = nt(cot, wout_ref[t, :]) + nn(grad_low, down_ref[0, :, t])
    gup_ref[0] += tn(low_out, cot)
    gdown_ref[0] += tn(grad_low, normed_out)

    for j in range(chunks):
        total = jnp.zeros((CHUNK, LANES), F32)
        for t in tiles(inner):
            q = gno[rows_of(j), t] * par_ref[GATE_GAIN, t]
            gno[rows_of(j), t] = q
            total = total + gated[rows_of(j), t] * q
        r = scale[j]
        shrink = jnp.sum(total, axis=1, keepdims=True) * (1.0 / inner) * (r * r * r)
        for t in tiles(inner):
            grad = r * gno[rows_of(j), t] - gated[rows_of(j), t] * shrink
            y_local = yp[rows_of(j), t]
            y = y_local + par_ref[SKIP, t] * xbc_ref[0, rows_of(j), t].astype(F32)
            g = gate_ref[0, rows_of(j), t].astype(F32)
            s = sigmoid(g)
            dy = grad * (g * s)
            dy_ref[0, rows_of(j), t] = dy.astype(BF)
            ggate_ref[0, rows_of(j), t] = (grad * y * (s * (1.0 + g * (1.0 - s)))).astype(BF)
            prod[rows_of(j), t] = (dy * y_local).astype(BF)
    rowt_ref[0] = nt(prod[...], onehot[...])

    for j in reversed(range(chunks)):
        grow = reach[j]
        scaled = jnp.concatenate(
            [(dy_ref[0, rows_of(j), t].astype(F32) * grow[:, t]).astype(BF) for t in tiles(inner)], axis=1
        )
        reads_t = xbc_ref[0, rows_of(j), inner + states :].astype(F32).T.astype(BF)
        update = nn(reads_t, scaled)
        dreads_ref[0, rows_of(j)] = nt(scaled, snow[j])
        last = cum_ref[0, j * CHUNK + CHUNK - 1 : j * CHUNK + CHUNK]
        before = run[...]
        dsuf_ref[0, j] = spread(jnp.exp(before), onehot[...])
        keep = grow[CHUNK - 1 : CHUNK]
        for t in tiles(inner):
            old = adj[:, t]
            gloc_ref[0, j, :, t] = old.astype(BF)
            adj[:, t] = keep[:, t] * old + update[:, t]
        run[...] = before + last

    @pl.when(blk == pl.num_programs(1) - 1)
    def _():
        gown_ref[0] = adj[...].astype(BF)


def intra_back_kernel(xbc_ref, wid_ref, cum_ref, dy_ref, dreads_ref, z_ref, dinputs_ref, dreads_out_ref, onehot):
    heads, inner = onehot.shape
    states = (xbc_ref.shape[2] - inner) // 2
    width = inner // heads
    per = LANES // width

    @pl.when((pl.program_id(0) == 0) & (pl.program_id(1) == 0))
    def _():
        onehot[...] = head_onehot(heads, inner)

    for j in range(xbc_ref.shape[1] // CHUNK):
        c = cum_ref[0, rows_of(j)] * LOG2E
        c_rows = c.T
        wide = spread(wid_ref[0, rows_of(j)], onehot[...])
        inputs = xbc_ref[0, rows_of(j), inner : inner + states]
        reads = xbc_ref[0, rows_of(j), inner + states :]
        mask = upper_ones(CHUNK)
        scores_t = nt(inputs, reads) * mask
        lane = lax.broadcasted_iota(jnp.int32, (CHUNK, LANES), 1)
        total = jnp.zeros((CHUNK, CHUNK), F32)
        for k, t in enumerate(tiles(inner)):
            weighted = xbc_ref[0, rows_of(j), t].astype(F32) * wide[:, t]
            grads = dy_ref[0, rows_of(j), t]
            mixing, left, right = [], [], []
            for p in range(per):
                inside = (lane >= p * width) & (lane < (p + 1) * width)
                left.append(jnp.where(inside, weighted, 0.0).astype(BF))
                right.append(jnp.where(inside, grads.astype(F32), 0.0).astype(BF))
            products = nt(jnp.concatenate(left, axis=0), grads)
            for p in range(per):
                h = k * per + p
                kernel = jnp.exp2(jnp.minimum(c_rows[h : h + 1, :] - c[:, h : h + 1], 0.0))
                mixing.append((kernel * scores_t).astype(BF))
                total = total + kernel * products[p * CHUNK : (p + 1) * CHUNK]
            z_ref[0, rows_of(j), t] = nn(jnp.concatenate(mixing, axis=1), jnp.concatenate(right, axis=0)).astype(BF)
        total = total * mask
        dinputs_ref[0, rows_of(j)] = nn(total.astype(BF), reads)
        dreads_out_ref[0, rows_of(j)] = dreads_ref[0, rows_of(j)] + nn(total.T.astype(BF), inputs)


def adjoint_kernel(
    xbc_ref, dact_ref, wid_ref, cum_ref, sig_ref, dy_ref, z_ref, dinputs_ref, dreads_ref, rowt_ref,
    gloc_ref, dsuf_ref, end_ref, snext_ref, par_ref,
    gpre_ref, graw_ref,
    onehot, adj, prod,
):
    heads, inner = onehot.shape
    states = (xbc_ref.shape[2] - inner) // 2

    @pl.when((pl.program_id(0) == 0) & (pl.program_id(1) == 0))
    def _():
        onehot[...] = head_onehot(heads, inner)

    for j in range(xbc_ref.shape[1] // CHUNK):
        at = rows_of(j)
        overlap = []
        for t in tiles(inner):
            g = gloc_ref[0, j, :, t].astype(F32) + dsuf_ref[0, j, 0:1, t] * end_ref[0, :, t].astype(F32)
            adj[:, t] = g.astype(BF)
            overlap.append(jnp.sum(g * snext_ref[0, j, :, t].astype(F32), axis=0, keepdims=True))
        held = jnp.broadcast_to(jnp.concatenate(overlap, axis=1), (8, inner))
        high = held.astype(BF)
        held = (nt(high, onehot[...]) + nt((held - high.astype(F32)).astype(BF), onehot[...]))[0:1]
        c = cum_ref[0, at]
        last = c[CHUNK - 1 : CHUNK]
        w = wid_ref[0, at]
        wide = spread(w, onehot[...])
        tail = spread(jnp.exp(last - c), onehot[...])
        inputs = xbc_ref[0, at, inner : inner + states]
        carried = nn(inputs, adj[...])
        weighted = []
        for t in tiles(inner):
            x = xbc_ref[0, at, t].astype(F32)
            z = z_ref[0, at, t].astype(F32) + tail[:, t] * carried[:, t]
            prod[:, t] = (x * z).astype(BF)
            grad = wide[:, t] * z + par_ref[SKIP, t] * dy_ref[0, at, t].astype(F32)
            gpre_ref[0, at, t] = (grad * dact_ref[0, at, t].astype(F32)).astype(BF)
            weighted.append((x * (wide[:, t] * tail[:, t])).astype(BF))
        dinputs = dinputs_ref[0, at] + nt(jnp.concatenate(weighted, axis=1), adj[...])
        t = slice(inner, inner + states)
        gpre_ref[0, at, t] = (dinputs * dact_ref[0, at, t].astype(F32)).astype(BF)
        t = slice(inner + states, inner + 2 * states)
        gpre_ref[0, at, t] = (dreads_ref[0, at] * dact_ref[0, at, t].astype(F32)).astype(BF)
        direct = nt(prod[...], onehot[...])
        grad_rate = held + exact(upper_ones(CHUNK), rowt_ref[0, at] - w * direct)
        graw_ref[0, at] = (direct + par_ref[RATE, :heads] * grad_rate) * sig_ref[0, at]


def input_kernel(
    idx_ref, gpre_ref, rim_ref, ggate_ref, graw_ref, low_ref, res_ref, cot_ref, wgate_ref, win_ref, down_ref, up_ref, par_ref,
    gin_ref, gup_ref, gdown_ref,
    ext, gp, gn, nrm,
):
    blk = pl.program_id(1)
    rows = res_ref.shape[1]
    inner = ggate_ref.shape[2]
    mixer = gpre_ref.shape[2]
    proj = inner + win_ref.shape[1]
    model = res_ref.shape[2]
    gain = par_ref[NORM_GAIN, :model]

    @pl.when(blk == 0)
    def _():
        for n, t in enumerate(tiles(mixer)):
            ext[n, rows : rows + RIM, :] = rim_ref[0, :, t].astype(F32)
        gup_ref[...] = jnp.zeros_like(gup_ref)
        gdown_ref[...] = jnp.zeros_like(gdown_ref)

    @pl.when(blk > 0)
    def _():
        ext[:, rows : rows + RIM, :] = ext[:, 0:RIM, :]

    for j in range(rows // CHUNK):
        for t in tiles(mixer):
            ext[t.start // LANES, rows_of(j), :] = gpre_ref[0, rows_of(j), t].astype(F32)
    for j in range(rows // CHUNK):
        for t in tiles(mixer):
            total = None
            for k in range(4):
                at = 3 - k + j * CHUNK
                term = par_ref[k : k + 1, t] * ext[t.start // LANES, at : at + CHUNK, :]
                total = term if total is None else total + term
            gp[rows_of(j), inner + t.start : inner + t.stop] = total.astype(BF)
    gp[:, :inner] = ggate_ref[0]
    gp[:, inner + mixer : proj] = graw_ref[0].astype(BF)
    whole = slice(0, inner + mixer)
    rest = slice(inner + mixer, proj)
    grads, grads_rest = gp[:, whole], gp[:, rest]
    grad_low = (nt(grads, up_ref[0, :, whole]) + nt(grads_rest, up_ref[0, :, rest])).astype(BF)
    for at in range(0, model, 2 * LANES):
        t = slice(at, at + 2 * LANES)
        part = nt(gp[:, :inner], wgate_ref[t, :]) + nt(gp[:, inner : inner + mixer], win_ref[t, :mixer])
        gn[:, t] = part + nt(grads_rest, win_ref[t, mixer:]) + nn(grad_low, down_ref[0, :, t])

    def body(k, _):
        at = pl.ds(pl.multiple_of(k * 32, 32), 32)
        v = res_ref[0, at, :].astype(F32)
        u = lax.rsqrt(jnp.mean(v * v, axis=1, keepdims=True) + EPS)
        nrm[at, :] = (v * u * gain).astype(BF)
        w = gn[at, :] * gain
        m = jnp.mean(v * w, axis=1, keepdims=True)
        gin_ref[0, at, :] = (cot_ref[0, at, :].astype(F32) + u * w - v * (u * u * u * m)).astype(BF)
        return 0

    lax.fori_loop(0, rows // 32, body, 0)
    gup_ref[0, :, whole] += tn(low_ref[0], grads)
    gup_ref[0, :, rest] += tn(low_ref[0], grads_rest)
    gdown_ref[0] += tn(grad_low, nrm[...])


def carry_kernel(count, backwards, tot_ref, dec_ref, out_ref, theirs, theirs_dec, prefix, passed, tail, mine, sems):
    dp = lax.axis_index("dp")
    seq = lax.axis_index("seq")
    rank = count - 1 - seq if backwards else seq
    pairs = count // 2
    pair, side = rank // 2, rank % 2
    seqs, states, inner = tot_ref.shape
    half = inner // 2
    parts = theirs.shape[0] // seqs
    wide = half // parts

    def device(other):
        return (count - 1 - other if backwards else other, dp)

    partner = device(pair * 2 + 1 - side)
    ahead = device(lax.rem(pair + 1, pairs) * 2 + side)
    behind = device(lax.rem(pair + pairs - 1, pairs) * 2 + side)
    barrier = pltpu.get_barrier_semaphore()
    for other in (partner, ahead, behind):
        pl.semaphore_signal(barrier, inc=1, device_id=other, device_id_type=MESH)
    pl.semaphore_wait(barrier, 3)

    def send(kind, n, src, dst, to):
        return pltpu.make_async_remote_copy(
            src_ref=src, dst_ref=dst, send_sem=sems.at[0, kind, n], recv_sem=sems.at[1, kind, n],
            device_id=to, device_id_type=MESH,
        )

    blocks = [(s, q) for s in range(seqs) for q in range(parts)]

    def cols(base, q):
        return pl.ds(pl.multiple_of(base * half + q * wide, LANES), wide)

    decs = send(3, 0, dec_ref, theirs_dec, partner)
    decs.start()
    swaps = []
    for n, (s, q) in enumerate(blocks):
        copy = send(0, n, tot_ref.at[s, :, cols(1 - side, q)], theirs.at[n], partner)
        copy.start()
        swaps.append(copy)
    decs.wait()
    hops = [send(1, n, passed.at[n], prefix.at[n], ahead) for n in range(len(blocks))]
    gives = [send(2, n, tail.at[n], mine.at[n], partner) for n in range(len(blocks))]
    for n, (s, q) in enumerate(blocks):
        swaps[n].wait()

        @pl.when(pair == 0)
        def _(n=n):
            prefix[n] = jnp.zeros_like(prefix[n])

        @pl.when(pair > 0)
        def _(n=n):
            hops[n].wait_recv()

        own_dec = dec_ref[s, 0:1, cols(side, q)]
        their_dec = theirs_dec[s, 0:1, cols(side, q)]
        own = tot_ref[s, :, cols(side, q)].astype(F32)
        other = theirs[n].astype(F32)
        before = prefix[n].astype(F32)
        first = jnp.where(side == 0, own, other)
        second = jnp.where(side == 0, other, own)
        first_dec = jnp.where(side == 0, own_dec, their_dec)
        second_dec = jnp.where(side == 0, their_dec, own_dec)
        middle = first_dec * before + first
        passed[n] = (second_dec * middle + second).astype(BF)

        @pl.when(pair < pairs - 1)
        def _(n=n):
            hops[n].start()

        out_ref[s, :, cols(side, q)] = jnp.where(side == 0, before, middle).astype(BF)
        tail[n] = jnp.where(side == 0, middle, before).astype(BF)
        gives[n].start()
    for n, (s, q) in enumerate(blocks):
        gives[n].wait()
        out_ref[s, :, cols(1 - side, q)] = mine[n]

        @pl.when(pair < pairs - 1)
        def _(n=n):
            hops[n].wait_send()


def carry(total, decay, count, backwards):
    seqs, states, inner = total.shape
    parts = 2
    blocks = seqs * parts
    slot = pltpu.VMEM((blocks, states, inner // 2 // parts), BF)
    return pl.pallas_call(
        functools.partial(carry_kernel, count, backwards),
        out_shape=jax.ShapeDtypeStruct(total.shape, BF),
        in_specs=[pl.BlockSpec(memory_space=pltpu.VMEM)] * 2,
        out_specs=pl.BlockSpec(memory_space=pltpu.VMEM),
        scratch_shapes=[
            slot,
            pltpu.VMEM(decay.shape, F32),
            slot,
            slot,
            slot,
            slot,
            pltpu.SemaphoreType.DMA((2, 4, blocks)),
        ],
        compiler_params=pltpu.CompilerParams(
            collective_id=2 if backwards else 1, has_side_effects=True, vmem_limit_bytes=VMEM_LIMIT
        ),
        name="adjoint_carry" if backwards else "state_carry",
    )(total, decay)


def gather_kernel(count, seq_count, res_ref, win_ref, ad_ref, win_out, ad_out, halo_out, sems, local):
    dp = lax.axis_index("dp")
    seq = lax.axis_index("seq")
    side = lax.rem(seq, 2)
    partner = (seq + 1 - 2 * side, dp)
    sibling = (seq, dp + 1 - 2 * lax.rem(dp, 2))
    later = (lax.rem(seq + 1, seq_count), dp)
    earlier = (lax.rem(seq + seq_count - 1, seq_count), dp)
    chips = count // 2
    barrier = pltpu.get_barrier_semaphore()
    others = [(seq, lax.rem(dp + 2 * k, count)) for k in range(1, chips)]
    for other in [partner, sibling, later, earlier] + others:
        pl.semaphore_signal(barrier, inc=1, device_id=other, device_id_type=MESH)
    pl.semaphore_wait(barrier, 4 + len(others))

    def send(src, dst, to, *at):
        return pltpu.make_async_remote_copy(
            src_ref=src, dst_ref=dst, send_sem=sems.at[(0,) + at], recv_sem=sems.at[(1,) + at],
            device_id=to, device_id_type=MESH,
        )

    share, width = win_ref.shape[0], win_out.shape[1]
    half = share // 2
    owned = ad_ref.shape[1]
    split = width // 2 // LANES * LANES
    start = win_ref.shape[1] - width

    def columns(at, wide, piece):
        def source(which):
            return win_ref.at[pl.ds(pl.multiple_of(which * half, 16), half), pl.ds(start + at, wide)]

        def target(owner, which):
            return win_out.at[pl.ds(pl.multiple_of(owner * share + which * half, 16), half), pl.ds(at, wide)]

        return source, target, piece

    pieces = [
        (lambda which: ad_ref.at[which], lambda owner, which: ad_out.at[which, pl.ds(owner * owned, owned)], 0),
        columns(0, split, 1),
        columns(split, width - split, 2),
    ]
    out_going = []
    for source, target, n in pieces:
        for k in range(1, chips):
            copy = send(source(side), target(dp, side), others[k - 1], 0, k, n)
            copy.start()
            out_going.append(copy)
    rim = halo_out.shape[1]
    edge = send(res_ref.at[:, pl.ds(res_ref.shape[1] - rim, rim)], halo_out, later, 6, 0, 0)

    @pl.when(seq < seq_count - 1)
    def _():
        edge.start()

    kept = []
    for source, target, n in pieces:
        for which in range(2):
            copy = pltpu.make_async_copy(source(which), target(dp, which), local.at[which, n])
            copy.start()
            kept.append(copy)
            copy = send(source(which), target(dp, which), sibling, 3 + which, 0, n)
            copy.start()
            kept.append(copy)
    passed = []
    for source, target, n in pieces:
        for k in range(1, chips):
            owner = lax.rem(dp - 2 * k + count, count)
            here = target(owner, side)
            send(source(side), here, others[k - 1], 0, k, n).wait_recv()
            across = send(here, here, partner, 1, k, n)
            over = send(here, here, sibling, 2, k, n)
            across.start()
            over.start()
            passed += [(across, False), (over, True)]
    for source, target, n in pieces:
        for k in range(1, chips):
            owner = lax.rem(dp - 2 * k + count, count)
            there = target(owner, 1 - side)
            send(there, there, partner, 1, k, n).wait_recv()
            over = send(there, there, sibling, 5, k, n)
            over.start()
            passed.append((over, True))
    for copy in out_going:
        copy.wait_send()
    for copy in kept:
        copy.wait()
    for copy, both in passed:
        copy.wait_send()
        if both:
            copy.wait_recv()

    @pl.when(seq == 0)
    def _():
        halo_out[...] = jnp.zeros_like(halo_out)

    @pl.when(seq > 0)
    def _():
        edge.wait_recv()

    @pl.when(seq < seq_count - 1)
    def _():
        edge.wait_send()


def gather(residual, in_weight, packed, first, count, seq_count):
    pieces = 3
    return pl.pallas_call(
        functools.partial(gather_kernel, count, seq_count),
        out_shape=[
            jax.ShapeDtypeStruct((in_weight.shape[0] * count, in_weight.shape[1] - first), BF),
            jax.ShapeDtypeStruct((2, packed.shape[1] * count) + packed.shape[2:], BF),
            jax.ShapeDtypeStruct((residual.shape[0], RIM, residual.shape[2]), BF),
        ],
        in_specs=[pl.BlockSpec(memory_space=pl.ANY)] * 3,
        out_specs=[pl.BlockSpec(memory_space=pltpu.VMEM)] * 3,
        scratch_shapes=[
            pltpu.SemaphoreType.DMA((2, 7, count // 2, pieces)),
            pltpu.SemaphoreType.DMA((2, pieces)),
        ],
        compiler_params=pltpu.CompilerParams(collective_id=3, has_side_effects=True, vmem_limit_bytes=VMEM_LIMIT),
        name="gather",
    )(residual, in_weight, packed)


def sums_kernel(
    count, dp_count, up_in_ref, down_in_ref, up_out_ref, down_out_ref, coef_ref,
    final,
    pack, half, half_sent, first, line, red, give, owners, sems,
):
    dp = lax.axis_index("dp")
    seq = lax.axis_index("seq")
    pair, side = seq // 2, lax.rem(seq, 2)
    pairs = count // 2
    share = red.shape[0]
    seqs, rank, _ = up_in_ref.shape
    owned = final.shape[1] // rank
    partner = (seq + 1 - 2 * side, dp)
    along = [(lax.rem(pair + k, pairs) * 2 + side, dp) for k in range(1, pairs)]
    across = [(seq, lax.rem(dp + k, dp_count)) for k in range(1, dp_count)]
    barrier = pltpu.get_barrier_semaphore()
    for other in [partner] + along + across:
        pl.semaphore_signal(barrier, inc=1, device_id=other, device_id_type=MESH)

    places = []
    for n, ref in enumerate((up_in_ref, down_in_ref, up_out_ref, down_out_ref)):
        if n == 2:
            in_tiles = len(places)
        places += [(ref, t.start, t.stop - t.start) for t in tiles(ref.shape[2])]
    for n, (ref, at, wide) in enumerate(places):
        for s in range(seqs):
            v = ref[s, :, at : at + wide]
            if wide < LANES:
                v = jnp.concatenate([v, jnp.zeros((rank, LANES - wide), F32)], axis=1)
            pack[n, s * rank : (s + 1) * rank, :] = v.astype(BF)
    for n in range(len(places), pack.shape[0]):
        pack[n] = jnp.zeros_like(pack[n])
    pl.semaphore_wait(barrier, 1 + len(along) + len(across))

    def send(src, dst, to, *at):
        return pltpu.make_async_remote_copy(
            src_ref=src, dst_ref=dst, send_sem=sems.at[(0,) + at], recv_sem=sems.at[(1,) + at],
            device_id=to, device_id_type=MESH,
        )

    wide = pairs * share
    copy = send(pack.at[pl.ds((1 - side) * wide, wide)], first, partner, 0, 0)
    copy.start()
    copy.wait()

    def add(n, _):
        v = pack[side * wide + n].astype(F32) + first[n].astype(F32)
        half[n] = v
        half_sent[n] = v.astype(BF)
        return 0

    lax.fori_loop(0, wide, add, 0)
    copies = []
    for k in range(1, pairs):
        there = lax.rem(pair + k, pairs)
        copies.append(send(half_sent.at[pl.ds(there * share, share)], line.at[k - 1], along[k - 1], 1, k))
        copies[-1].start()
    for copy in copies:
        copy.wait()
    for n in range(share):
        v = half[pair * share + n]
        for k in range(pairs - 1):
            v = v + line[k, n].astype(F32)
        red[n] = v

    def part(owner, n, a):
        tile = (side * pairs + pair) * share + n
        kind = jnp.where(tile < in_tiles, 0, 1)
        total = None
        for s in range(seqs):
            c = coef_ref[kind, (owner * owned + a) * seqs + s]
            term = c * red[n, s * rank : (s + 1) * rank, :]
            total = term if total is None else total + term
        return total

    copies = []
    for k in range(1, dp_count):
        owner = lax.rem(dp + k, dp_count)
        for n in range(share):
            for a in range(owned):
                give[k - 1, n, a * rank : (a + 1) * rank, :] = part(owner, n, a).astype(BF)
        copies.append(send(give.at[k - 1], owners.at[k - 1], across[k - 1], 2, k))
        copies[-1].start()
    mine = [[part(dp, n, a) for a in range(owned)] for n in range(share)]
    for copy in copies:
        copy.wait()
    here = pl.ds((side * pairs + pair) * share, share)
    for n in range(share):
        for a in range(owned):
            v = mine[n][a]
            for k in range(dp_count - 1):
                v = v + owners[k, n, a * rank : (a + 1) * rank, :].astype(F32)
            final[(side * pairs + pair) * share + n, a * rank : (a + 1) * rank, :] = v.astype(BF)
    copies = []
    for k in range(1, pairs):
        copies.append(send(final.at[here], final.at[here], along[k - 1], 3, k))
        copies[-1].start()
    for copy in copies:
        copy.wait()
    ours = final.at[pl.ds(side * wide, wide)]
    copy = send(ours, ours, partner, 4, 0)
    copy.start()
    copy.wait()

def unpack_kernel(final, up_in_out, down_in_out, up_out_out, down_out_out):
    owned, rank, _ = up_in_out.shape
    n = 0
    for out in (up_in_out, down_in_out, up_out_out, down_out_out):
        for t in tiles(out.shape[2]):
            for a in range(owned):
                out[a, :, t] = final[n, a * rank : (a + 1) * rank, : t.stop - t.start].astype(F32)
            n += 1


def adapter_sums(grads, coef, owned, count, dp_count):
    up_in, down_in, up_out, down_out = grads
    seqs, rank, _ = up_in.shape
    total = sum(-(-g.shape[2] // LANES) for g in grads)
    share = -(-total // count)
    pairs = count // 2
    rows = seqs * rank
    own_rows = owned * rank
    whole = pl.BlockSpec(memory_space=pltpu.VMEM)
    final = pl.pallas_call(
        functools.partial(sums_kernel, count, dp_count),
        out_shape=jax.ShapeDtypeStruct((share * count, own_rows, LANES), BF),
        in_specs=[whole] * 4 + [pl.BlockSpec(memory_space=pltpu.SMEM)],
        out_specs=whole,
        scratch_shapes=[
            pltpu.VMEM((share * count, rows, LANES), BF),
            pltpu.VMEM((share * pairs, rows, LANES), F32),
            pltpu.VMEM((share * pairs, rows, LANES), BF),
            pltpu.VMEM((share * pairs, rows, LANES), BF),
            pltpu.VMEM((max(pairs - 1, 1), share, rows, LANES), BF),
            pltpu.VMEM((share, rows, LANES), F32),
            pltpu.VMEM((max(dp_count - 1, 1), share, own_rows, LANES), BF),
            pltpu.VMEM((max(dp_count - 1, 1), share, own_rows, LANES), BF),
            pltpu.SemaphoreType.DMA((2, 5, max(pairs, dp_count))),
        ],
        compiler_params=pltpu.CompilerParams(collective_id=4, has_side_effects=True, vmem_limit_bytes=VMEM_LIMIT),
        name="adapter_sums",
    )(up_in, down_in, up_out, down_out, coef)
    return pl.pallas_call(
        unpack_kernel,
        out_shape=[jax.ShapeDtypeStruct((owned, rank, g.shape[2]), F32) for g in grads],
        in_specs=[whole],
        out_specs=[whole] * 4,
        name="unpack",
    )(final)


def call(kernel, grid, ins, outs, scratch, name, prefetch=()):
    arrays = [a for a, _, _ in ins]
    specs = [pl.BlockSpec(block, index) for _, block, index in ins]
    return pl.pallas_call(
        kernel,
        out_shape=[jax.ShapeDtypeStruct(shape, kind) for shape, kind, _, _ in outs],
        grid_spec=pltpu.PrefetchScalarGridSpec(
            num_scalar_prefetch=len(prefetch),
            grid=grid,
            in_specs=specs,
            out_specs=[pl.BlockSpec(block, index) for _, _, block, index in outs],
            scratch_shapes=scratch,
        ),
        compiler_params=pltpu.CompilerParams(
            dimension_semantics=("arbitrary",) * len(grid), vmem_limit_bytes=VMEM_LIMIT
        ),
        name=name,
    )(*prefetch, *arrays)


def on_device(
    residual_in,
    cotangent,
    norm_gain,
    in_weight,
    conv_weight,
    conv_bias,
    step_bias,
    decay_log,
    skip_gain,
    gate_gain,
    out_weight,
    in_down,
    in_up,
    out_down,
    out_up,
    in_index,
    out_index,
):
    seqs, tokens, model = residual_in.shape
    heads = step_bias.shape[0]
    inner = gate_gain.shape[0]
    mixer = conv_weight.shape[0]
    states = (mixer - inner) // 2
    rank = in_up.shape[1]
    proj = in_weight.shape[1]
    seq_count = lax.axis_size("seq")
    dp_count = lax.axis_size("dp")
    adapters = in_down.shape[0] * dp_count
    chunks = tokens // CHUNK
    blocks = tokens // BLOCK
    per = BLOCK // CHUNK

    taps = conv_weight.T
    small = [conv_bias, gate_gain, norm_gain, jnp.repeat(skip_gain, inner // heads), step_bias, -jnp.exp(decay_log)]
    small = [jnp.pad(v, (0, mixer - v.shape[0]))[None, :] for v in small]
    params = jnp.concatenate([taps] + small, axis=0)
    route = [(i, i + 1) for i in range(seq_count - 1)]

    lanes = -(-proj // LANES) * LANES
    downs = jnp.concatenate([out_down.transpose(0, 2, 1), in_down.transpose(0, 2, 1), out_up], axis=2)
    packed = jnp.stack(
        [jnp.pad(part, ((0, 0), (0, 0), (0, lanes - part.shape[2]))) for part in (in_up, downs)]
    )
    w_mix, table, halo = gather(residual_in, in_weight, packed, inner, dp_count, seq_count)
    w_mix, own_gate, own_out = lax.optimization_barrier((w_mix, in_weight[:, :inner], out_weight))
    w_gate = lax.all_gather(own_gate, "dp", axis=0, tiled=True)
    w_out = lax.all_gather(own_out, "dp", axis=0, tiled=True)

    grid = (seqs, blocks)

    def fixed(a):
        return (a, a.shape, lambda s, b, *_: (0,) * a.ndim)

    def by_seq(a):
        return (a, (1,) + a.shape[1:], lambda s, b, *_: (s,) + (0,) * (a.ndim - 1))

    def picked(kind, width, at):
        return (table, (None, 1, rank, width), lambda s, b, idx, *_: (kind, idx[s], 0, at // width))

    in_adapter = [picked(1, model, inner), picked(0, lanes, 0)]
    out_adapter = [picked(1, inner, 0), picked(1, model, inner + model)]

    def by_row(a, turn=False):
        if turn:
            return (a, (1, BLOCK, a.shape[2]), lambda s, b, *_: (s, blocks - 1 - b, 0))
        return (a, (1, BLOCK, a.shape[2]), lambda s, b, *_: (s, b, 0))

    def by_chunk(a, turn=False):
        if turn:
            return (a, (1, per) + a.shape[2:], lambda s, b, *_: (s, blocks - 1 - b, 0, 0))
        return (a, (1, per) + a.shape[2:], lambda s, b, *_: (s, b, 0, 0))

    def out(pick, shape, kind, *rest):
        spec = pick(jax.ShapeDtypeStruct(shape, kind), *rest)
        return (shape, kind, spec[1], spec[2])

    row_of = lambda width: (seqs, tokens, width)
    low, xbc, dact, wid, cum, sig, sloc, dpre, tot, dtot = call(
        project_kernel,
        grid,
        [
            by_row(residual_in),
            by_seq(halo),
            fixed(w_mix),
            *in_adapter,
            fixed(params),
        ],
        [
            out(by_row, row_of(rank), BF),
            out(by_row, row_of(mixer), BF),
            out(by_row, row_of(mixer), BF),
            out(by_row, row_of(heads), F32),
            out(by_row, row_of(heads), F32),
            out(by_row, row_of(heads), F32),
            out(by_chunk, (seqs, chunks, states, inner), BF),
            out(by_chunk, (seqs, chunks, 8, inner), F32),
            out(by_seq, (seqs, states, inner), BF),
            out(by_seq, (seqs, 8, inner), F32),
        ],
        [
            pltpu.VMEM((BLOCK, model), BF),
            pltpu.VMEM((mixer // LANES, BLOCK + RIM, LANES), F32),
            pltpu.VMEM((states, inner), F32),
            pltpu.VMEM((8, heads), F32),
            pltpu.VMEM((heads, inner), BF),
        ],
        "project",
        prefetch=(in_index[:, 0],),
    )
    start = carry(tot, dtot, seq_count, False)
    y_intra, gate = call(
        intra_kernel,
        grid,
        [
            by_row(xbc),
            by_row(wid),
            by_row(cum),
            by_row(residual_in),
            by_row(low),
            fixed(w_gate),
            in_adapter[1],
            fixed(params),
        ],
        [out(by_row, row_of(inner), BF), out(by_row, row_of(inner), BF)],
        [pltpu.VMEM((BLOCK, model), BF), pltpu.VMEM((heads, inner), BF)],
        "intra",
        prefetch=(in_index[:, 0],),
    )
    block_out, ggate, dy, dreads, rowt, gloc, dsuf, snext, gown, gout_up, gout_down = call(
        output_kernel,
        grid,
        [
            by_row(y_intra, True),
            by_row(xbc, True),
            by_row(gate, True),
            by_row(cum, True),
            by_chunk(sloc, True),
            by_chunk(dpre, True),
            by_seq(tot),
            by_seq(dtot),
            by_seq(start),
            by_row(residual_in, True),
            by_row(cotangent, True),
            fixed(w_out),
            *out_adapter,
            fixed(params),
        ],
        [
            out(by_row, row_of(model), BF, True),
            out(by_row, row_of(inner), BF, True),
            out(by_row, row_of(inner), BF, True),
            out(by_row, row_of(states), F32, True),
            out(by_row, row_of(heads), F32, True),
            out(by_chunk, (seqs, chunks, states, inner), BF, True),
            out(by_chunk, (seqs, chunks, 8, inner), F32, True),
            out(by_chunk, (seqs, chunks, states, inner), BF, True),
            out(by_seq, (seqs, states, inner), BF),
            out(by_seq, (seqs, rank, model), F32),
            out(by_seq, (seqs, rank, inner), F32),
        ],
        [
            pltpu.VMEM((heads, inner), BF),
            pltpu.VMEM((per, states, inner), BF),
            pltpu.VMEM((states, inner), F32),
            pltpu.VMEM((states, inner), F32),
            pltpu.VMEM((8, heads), F32),
            pltpu.VMEM((BLOCK, inner), F32),
            pltpu.VMEM((BLOCK, inner), F32),
            pltpu.VMEM((BLOCK, inner), BF),
            pltpu.VMEM((BLOCK, inner), F32),
            pltpu.VMEM((BLOCK, inner), BF),
        ],
        "output",
        prefetch=(out_index[:, 0],),
    )
    end = carry(gown, dtot, seq_count, True)
    z, dinputs, dreads = call(
        intra_back_kernel,
        grid,
        [by_row(xbc), by_row(wid), by_row(cum), by_row(dy), by_row(dreads)],
        [out(by_row, row_of(inner), BF), out(by_row, row_of(states), F32), out(by_row, row_of(states), F32)],
        [pltpu.VMEM((heads, inner), BF)],
        "intra_back",
    )
    gpre, graw = call(
        adjoint_kernel,
        grid,
        [
            by_row(xbc),
            by_row(dact),
            by_row(wid),
            by_row(cum),
            by_row(sig),
            by_row(dy),
            by_row(z),
            by_row(dinputs),
            by_row(dreads),
            by_row(rowt),
            by_chunk(gloc),
            by_chunk(dsuf),
            by_seq(end),
            by_chunk(snext),
            fixed(params),
        ],
        [out(by_row, row_of(mixer), BF), out(by_row, row_of(heads), F32)],
        [pltpu.VMEM((heads, inner), BF), pltpu.VMEM((states, inner), BF), pltpu.VMEM((CHUNK, inner), BF)],
        "adjoint",
    )
    rim = lax.ppermute(gpre[:, :RIM], "seq", [(j, i) for i, j in route])
    grad_input, gin_up, gin_down = call(
        input_kernel,
        grid,
        [
            by_row(gpre, True),
            by_seq(rim),
            by_row(ggate, True),
            by_row(graw, True),
            by_row(low, True),
            by_row(residual_in, True),
            by_row(cotangent, True),
            fixed(w_gate),
            fixed(w_mix),
            *in_adapter,
            fixed(params),
        ],
        [
            out(by_row, row_of(model), BF, True),
            out(by_seq, (seqs, rank, proj), F32),
            out(by_seq, (seqs, rank, model), F32),
        ],
        [
            pltpu.VMEM((mixer // LANES, BLOCK + RIM, LANES), F32),
            pltpu.VMEM((BLOCK, proj), BF),
            pltpu.VMEM((BLOCK, model), F32),
            pltpu.VMEM((BLOCK, model), BF),
        ],
        "input",
        prefetch=(in_index[:, 0],),
    )

    owners = jnp.arange(adapters)[:, None]
    coef = jnp.stack([(index[:, 0][None, :] == owners).astype(F32).reshape(-1) for index in (in_index, out_index)])
    gin_up, gin_down, gout_up, gout_down = adapter_sums(
        (gin_up, gin_down, gout_up, gout_down), coef, in_down.shape[0], seq_count, dp_count
    )
    gin_down, gout_down = (g.transpose(0, 2, 1) for g in (gin_down, gout_down))
    return (block_out, grad_input, gin_down, gin_up, gout_down, gout_up)


def solution(mesh):
    rows = P("dp", "seq", None)
    split = P("dp", None, None)
    return jax.shard_map(
        on_device,
        mesh=mesh,
        in_specs=(
            rows,
            rows,
            P(),
            P("dp", None),
            P(),
            P(),
            P(),
            P(),
            P(),
            P(),
            P("dp", None),
            split,
            split,
            split,
            split,
            P("dp", None),
            P("dp", None),
        ),
        out_specs=(rows, rows, split, split, split, split),
        check_vma=False,
    )
```

```python
import functools

import jax
import jax.numpy as jnp
from jax import lax
from jax.experimental import pallas as pl
from jax.experimental.pallas import tpu as pltpu
from jax.sharding import PartitionSpec as P

EPS = 1e-05
CHUNK = 128
BLOCK = 256
RIM = 16
LANES = 128
LOG2E = 1.4426950408889634
BF = jnp.bfloat16
F32 = jnp.float32
MESH = pl.DeviceIdType.MESH
VMEM_LIMIT = 62 * 2**20
PARTS = 3
CONV_BIAS, GATE_GAIN, NORM_GAIN, SKIP, STEP_BIAS, RATE = (slice(4 + n, 5 + n) for n in range(6))


def nn(a, b):
    return lax.dot_general(a, b, (((1,), (0,)), ((), ())), preferred_element_type=F32)


def nt(a, b):
    return lax.dot_general(a, b, (((1,), (1,)), ((), ())), preferred_element_type=F32)


def tn(a, b):
    return lax.dot_general(a, b, (((0,), (0,)), ((), ())), preferred_element_type=F32)


def exact(a, b):
    return lax.dot_general(
        a, b, (((1,), (0,)), ((), ())), precision=lax.Precision.HIGHEST, preferred_element_type=F32
    )


def sigmoid(v):
    return 0.5 * jnp.tanh(0.5 * v) + 0.5


def spread(values, onehot):
    high = values.astype(BF)
    rest = (values - high.astype(F32)).astype(BF)
    return nn(high, onehot) + nn(rest, onehot)


def gather_heads(values, onehot):
    return nt(values.astype(BF), onehot)


def head_onehot(heads, inner):
    width = inner // heads
    row = lax.broadcasted_iota(jnp.int32, (heads, inner), 0)
    col = lax.broadcasted_iota(jnp.int32, (heads, inner), 1)
    low = row * width
    return jnp.where((col >= low) & (col < low + width), 1.0, 0.0).astype(BF)


def lower_ones(length):
    row = lax.broadcasted_iota(jnp.int32, (length, length), 0)
    col = lax.broadcasted_iota(jnp.int32, (length, length), 1)
    return jnp.where(row >= col, 1.0, 0.0).astype(F32)


def upper_ones(length):
    row = lax.broadcasted_iota(jnp.int32, (length, length), 0)
    col = lax.broadcasted_iota(jnp.int32, (length, length), 1)
    return jnp.where(row <= col, 1.0, 0.0).astype(F32)


def tiles(width):
    return [slice(at, min(at + LANES, width)) for at in range(0, width, LANES)]


def rows_of(j):
    return slice(j * CHUNK, (j + 1) * CHUNK)


def write_normed(dst, src, gain, step):
    rows = src.shape[0]

    def body(k, _):
        at = pl.ds(pl.multiple_of(k * step, step), step)
        v = src[at, :].astype(F32)
        scale = lax.rsqrt(jnp.mean(v * v, axis=1, keepdims=True) + EPS)
        dst[at, :] = (v * scale * gain).astype(BF)
        return 0

    lax.fori_loop(0, rows // step, body, 0)


def project_step(first_block, normed, halo, win, down, up, par, low_ref, xbc, dact, wid, cum, sig, sloc, cpre, ext, state, run, onehot):
    rows = normed.shape[0]
    heads, inner = onehot.shape
    mixer = xbc.shape[1]
    states = (mixer - inner) // 2

    @pl.when(first_block)
    def _():
        state[...] = jnp.zeros_like(state)
        run[...] = jnp.zeros_like(run)
        v = halo[...].astype(F32)
        scale = lax.rsqrt(jnp.mean(v * v, axis=1, keepdims=True) + EPS)
        first = (v * scale * par[NORM_GAIN, : normed.shape[1]]).astype(BF)
        low_first = nt(first, down[...]).astype(BF)
        for at in range(0, mixer, 2 * LANES):
            t = slice(at, at + 2 * LANES)
            v = nn(first, win[:, t]) + nn(low_first, up[:, inner + at : inner + at + 2 * LANES])
            ext[at // LANES, 0:RIM, :] = v[:, :LANES]
            ext[at // LANES + 1, 0:RIM, :] = v[:, LANES:]

    @pl.when(jnp.logical_not(first_block))
    def _():
        ext[:, 0:RIM, :] = ext[:, rows : rows + RIM, :]

    tokens = normed[...]
    low = nt(tokens, down[...]).astype(BF)
    low_ref[...] = low
    for at in range(0, mixer, 2 * LANES):
        t = slice(at, at + 2 * LANES)
        v = nn(tokens, win[:, t]) + nn(low, up[:, inner + at : inner + at + 2 * LANES])
        ext[at // LANES, RIM : RIM + rows, :] = v[:, :LANES]
        ext[at // LANES + 1, RIM : RIM + rows, :] = v[:, LANES:]
    cols = slice(inner + mixer, inner + mixer + heads)
    raw = nn(tokens, win[:, mixer : mixer + heads]) + nn(low, up[:, cols]) + par[STEP_BIAS, :heads]
    sig[...] = sigmoid(raw)
    widths = jnp.maximum(raw, 0.0) + jnp.log1p(jnp.exp(-jnp.abs(raw)))
    wid[...] = widths
    ones = lower_ones(CHUNK)
    for j in range(rows // CHUNK):
        for n, t in enumerate(tiles(mixer)):
            pre = par[CONV_BIAS, t]
            for k in range(4):
                at = RIM - 3 + k + j * CHUNK
                pre = pre + par[k : k + 1, t] * ext[n, at : at + CHUNK, :]
            s = sigmoid(pre)
            act = pre * s
            xbc[rows_of(j), t] = act.astype(BF)
            dact[rows_of(j), t] = (s + act * (1.0 - s)).astype(BF)
    for j in range(rows // CHUNK):
        w = widths[rows_of(j)]
        c = exact(ones, w * par[RATE, :heads])
        cum[rows_of(j)] = c
        last = c[CHUNK - 1 : CHUNK]
        tail = spread(jnp.exp(last - c) * w, onehot[...])
        weighted = jnp.concatenate(
            [(xbc[rows_of(j), t].astype(F32) * tail[:, t]).astype(BF) for t in tiles(inner)], axis=1
        )
        inputs_t = xbc[rows_of(j), inner : inner + states].astype(F32).T.astype(BF)
        update = nn(inputs_t, weighted)
        before = run[...]
        cpre[j] = before
        keep = spread(jnp.exp(jnp.broadcast_to(last, before.shape)), onehot[...])[0:1]
        for t in tiles(inner):
            old = state[:, t]
            sloc[j, :, t] = old.astype(BF)
            state[:, t] = keep[:, t] * old + update[:, t]
        run[...] = before + last


def intra_step(normed, low_ref, win, up, xbc, wid, cum, gate, y, onehot):
    heads, inner = onehot.shape
    states = (xbc.shape[1] - inner) // 2
    width = inner // heads
    per = LANES // width
    tokens, low = normed[...], low_ref[...]
    for at in range(0, inner, 2 * LANES):
        t = slice(at, at + 2 * LANES)
        gate[:, t] = (nn(tokens, win[:, t]) + nn(low, up[:, t])).astype(BF)
    lane = lax.broadcasted_iota(jnp.int32, (CHUNK, LANES), 1)
    mask = lower_ones(CHUNK)
    for j in range(xbc.shape[0] // CHUNK):
        c = cum[rows_of(j)] * LOG2E
        c_rows = c.T
        wide = spread(wid[rows_of(j)], onehot[...])
        inputs = xbc[rows_of(j), inner : inner + states]
        reads = xbc[rows_of(j), inner + states :]
        scores = nt(reads, inputs) * mask
        for k, t in enumerate(tiles(inner)):
            weighted = xbc[rows_of(j), t].astype(F32) * wide[:, t]
            mixing, parts = [], []
            for p in range(per):
                h = k * per + p
                kernel = jnp.exp2(jnp.minimum(c[:, h : h + 1] - c_rows[h : h + 1, :], 0.0))
                mixing.append((kernel * scores).astype(BF))
                inside = (lane >= p * width) & (lane < (p + 1) * width)
                parts.append(jnp.where(inside, weighted, 0.0).astype(BF))
            y[rows_of(j), t] = nn(jnp.concatenate(mixing, axis=1), jnp.concatenate(parts, axis=0)).astype(BF)


def output_step(
    first_block, middle, loaded, y, xbc, gate, cum, sloc, cpre, csuf, start, res, cot, out, wout, down, up, par,
    dreads, rowt, gup, gdown, onehot, snow, adj, run, gated, nout, gno, prod,
):
    rows = res.shape[0]
    heads, inner = onehot.shape
    states = (xbc.shape[1] - inner) // 2
    chunks = rows // CHUNK

    @pl.when(first_block)
    def _():
        adj[...] = jnp.zeros_like(adj)
        run[...] = jnp.zeros_like(run)
        gup[...] = jnp.zeros_like(gup)
        gdown[...] = jnp.zeros_like(gdown)

    reach, scale = [], []
    for j in range(chunks):
        since = spread(jnp.exp(cpre[j]), onehot[...])
        for t in tiles(inner):
            snow[j, :, t] = (sloc[j, :, t].astype(F32) + since[0:1, t] * start[:, t].astype(F32)).astype(BF)
        carried = nn(xbc[rows_of(j), inner + states :], snow[j])
        grow = spread(jnp.exp(cum[rows_of(j)]), onehot[...])
        reach.append(grow)
        total = jnp.zeros((CHUNK, LANES), F32)
        for t in tiles(inner):
            local = y[rows_of(j), t].astype(F32) + grow[:, t] * carried[:, t]
            y[rows_of(j), t] = local.astype(BF)
            g = gate[rows_of(j), t].astype(F32)
            v = (local + par[SKIP, t] * xbc[rows_of(j), t].astype(F32)) * (g * sigmoid(g))
            gated[rows_of(j), t] = v.astype(BF)
            total = total + v * v
        r = lax.rsqrt(jnp.sum(total, axis=1, keepdims=True) * (1.0 / inner) + EPS)
        scale.append(r)
        for t in tiles(inner):
            nout[rows_of(j), t] = (gated[rows_of(j), t].astype(F32) * r * par[GATE_GAIN, t]).astype(BF)

    middle()
    loaded()
    normed_out = nout[...]
    cot_rows = cot[...]
    low_out = nt(normed_out, down[...]).astype(BF)
    for at in range(0, out.shape[1], 2 * LANES):
        t = slice(at, at + 2 * LANES)
        part = nn(normed_out, wout[:, t]) + nn(low_out, up[:, t])
        out[:, t] = (res[:, t].astype(F32) + part).astype(BF)
    grad_low = nt(cot_rows, up[...]).astype(BF)
    for at in range(0, inner, 2 * LANES):
        t = slice(at, at + 2 * LANES)
        v = nt(cot_rows, wout[t, :]) + nn(grad_low, down[:, t])
        gno[at // LANES, 0:rows, :] = v[:, :LANES]
        gno[at // LANES + 1, 0:rows, :] = v[:, LANES:]
    gup[...] += tn(low_out, cot_rows)
    gdown[...] += tn(grad_low, normed_out)

    for j in reversed(range(chunks)):
        total = jnp.zeros((CHUNK, LANES), F32)
        for n, t in enumerate(tiles(inner)):
            q = gno[n, rows_of(j), :] * par[GATE_GAIN, t]
            total = total + gated[rows_of(j), t].astype(F32) * q
        r = scale[j]
        shrink = jnp.sum(total, axis=1, keepdims=True) * (1.0 / inner) * (r * r * r)
        scaled = []
        for n, t in enumerate(tiles(inner)):
            q = gno[n, rows_of(j), :] * par[GATE_GAIN, t]
            grad = r * q - gated[rows_of(j), t].astype(F32) * shrink
            local = y[rows_of(j), t].astype(F32)
            g = gate[rows_of(j), t].astype(F32)
            s = sigmoid(g)
            dy = grad * (g * s)
            y[rows_of(j), t] = dy.astype(BF)
            full = local + par[SKIP, t] * xbc[rows_of(j), t].astype(F32)
            gate[rows_of(j), t] = (grad * full * (s * (1.0 + g * (1.0 - s)))).astype(BF)
            prod[:, t] = (dy * local).astype(BF)
            scaled.append((dy * reach[j][:, t]).astype(BF))
        rowt[rows_of(j)] = nt(prod[...], onehot[...])
        scaled = jnp.concatenate(scaled, axis=1)
        reads_t = xbc[rows_of(j), inner + states :].astype(F32).T.astype(BF)
        update = nn(reads_t, scaled)
        dreads[rows_of(j)] = nt(scaled, snow[j])
        last = cum[j * CHUNK + CHUNK - 1 : j * CHUNK + CHUNK]
        before = run[...]
        csuf[j] = before
        keep = reach[j][CHUNK - 1 : CHUNK]
        for t in tiles(inner):
            old = adj[:, t]
            sloc[j, :, t] = old.astype(BF)
            adj[:, t] = keep[:, t] * old + update[:, t]
        run[...] = before + last


def adjoint_step(first_block, between, xbc, dact, wid, cum, sig, dy, dreads, rowt, gloc, csuf, end, final, par, onehot, adj, prod, z, held):
    heads, inner = onehot.shape
    states = (xbc.shape[1] - inner) // 2
    width = inner // heads
    per = LANES // width
    mask = upper_ones(CHUNK)
    lane = lax.broadcasted_iota(jnp.int32, (CHUNK, LANES), 1)

    @pl.when(first_block)
    def _():
        overlap = []
        for t in tiles(inner):
            overlap.append(jnp.sum(end[:, t].astype(F32) * final(t), axis=0, keepdims=True))
        v = jnp.broadcast_to(jnp.concatenate(overlap, axis=1), (8, inner))
        high = v.astype(BF)
        held[...] = nt(high, onehot[...]) + nt((v - high.astype(F32)).astype(BF), onehot[...])

    for j in reversed(range(xbc.shape[0] // CHUNK)):
        at = rows_of(j)
        c = cum[at]
        w = wid[at]
        c_two = c * LOG2E
        c_rows = c_two.T
        wide = spread(w, onehot[...])
        inputs = xbc[at, inner : inner + states]
        reads = xbc[at, inner + states :]
        scores_t = nt(inputs, reads) * mask
        total = jnp.zeros((CHUNK, CHUNK), F32)
        for k, t in enumerate(tiles(inner)):
            weighted = xbc[at, t].astype(F32) * wide[:, t]
            grads = dy[at, t]
            mixing, left, right = [], [], []
            for p in range(per):
                inside = (lane >= p * width) & (lane < (p + 1) * width)
                left.append(jnp.where(inside, weighted, 0.0).astype(BF))
                right.append(jnp.where(inside, grads.astype(F32), 0.0).astype(BF))
            products = nt(jnp.concatenate(left, axis=0), grads)
            for p in range(per):
                h = k * per + p
                kernel = jnp.exp2(jnp.minimum(c_rows[h : h + 1, :] - c_two[:, h : h + 1], 0.0))
                mixing.append((kernel * scores_t).astype(BF))
                total = total + kernel * products[p * CHUNK : (p + 1) * CHUNK]
            z[:, t] = nn(jnp.concatenate(mixing, axis=1), jnp.concatenate(right, axis=0))
        total = total * mask
        dinputs = nn(total.astype(BF), reads)
        dreads_all = dreads[at] + nn(total.T.astype(BF), inputs)

        since = spread(jnp.exp(csuf[j]), onehot[...])
        for t in tiles(inner):
            adj[:, t] = (gloc[j, :, t].astype(F32) + since[0:1, t] * end[:, t].astype(F32)).astype(BF)
        last = c[CHUNK - 1 : CHUNK]
        tail = spread(jnp.exp(last - c), onehot[...])
        carried = nn(inputs, adj[...])
        weighted = []
        for t in tiles(inner):
            x = xbc[at, t].astype(F32)
            v = z[:, t] + tail[:, t] * carried[:, t]
            prod[:, t] = (x * v).astype(BF)
            grad = wide[:, t] * v + par[SKIP, t] * dy[at, t].astype(F32)
            dact[at, t] = (grad * dact[at, t].astype(F32)).astype(BF)
            weighted.append((x * (wide[:, t] * tail[:, t])).astype(BF))
        dinputs = dinputs + nt(jnp.concatenate(weighted, axis=1), adj[...])
        t = slice(inner, inner + states)
        dact[at, t] = (dinputs * dact[at, t].astype(F32)).astype(BF)
        t = slice(inner + states, inner + 2 * states)
        dact[at, t] = (dreads_all * dact[at, t].astype(F32)).astype(BF)
        direct = nt(prod[...], onehot[...])
        grad_rate = held[0:1] + exact(mask, rowt[at] - w * direct)
        held[...] = jnp.broadcast_to(grad_rate[0:1], held.shape)
        sig[at] = (direct + par[RATE, :heads] * grad_rate) * sig[at]
        between(j)


def input_step(first_block, loaded, following, gpre, ggate, graw, low_ref, res, cot, gin, wgate, win, down, up, par, gup, gdown, ext, gn, nrm):
    rows = res.shape[0]
    inner = ggate.shape[1]
    mixer = gpre.shape[1]
    proj = inner + win.shape[1]
    model = res.shape[1]
    gain = par[NORM_GAIN, :model]

    @pl.when(first_block)
    def _():
        gup[...] = jnp.zeros_like(gup)
        gdown[...] = jnp.zeros_like(gdown)

    for n, t in enumerate(tiles(mixer)):
        for j in range(rows // CHUNK):
            ext[n, rows_of(j), :] = gpre[rows_of(j), t].astype(F32)
    following()
    for j in range(rows // CHUNK):
        for n, t in enumerate(tiles(mixer)):
            total = None
            for k in range(4):
                at = 3 - k + j * CHUNK
                term = par[k : k + 1, t] * ext[n, at : at + CHUNK, :]
                total = term if total is None else total + term
            gpre[rows_of(j), t] = total.astype(BF)
    whole = slice(inner, inner + mixer)
    rest = slice(inner + mixer, proj)
    grads_gate, grads_mix, grads_rest = ggate[...], gpre[...], graw[...].astype(BF)
    grad_low = (nt(grads_gate, up[:, :inner]) + nt(grads_mix, up[:, whole]) + nt(grads_rest, up[:, rest])).astype(BF)
    for at in range(0, model, 2 * LANES):
        t = slice(at, at + 2 * LANES)
        part = nt(grads_gate, wgate[t, :]) + nt(grads_mix, win[t, :mixer])
        gn[:, t] = part + nt(grads_rest, win[t, mixer:]) + nn(grad_low, down[:, t])
    loaded()

    def body(k, _):
        at = pl.ds(pl.multiple_of(k * 32, 32), 32)
        v = res[at, :].astype(F32)
        u = lax.rsqrt(jnp.mean(v * v, axis=1, keepdims=True) + EPS)
        nrm[at, :] = (v * u * gain).astype(BF)
        w = gn[at, :] * gain
        m = jnp.mean(v * w, axis=1, keepdims=True)
        gin[at, :] = (cot[at, :].astype(F32) + u * w - v * (u * u * u * m)).astype(BF)
        return 0

    lax.fori_loop(0, rows // 32, body, 0)
    low = low_ref[...]
    gup[:, :inner] += tn(low, grads_gate)
    gup[:, whole] += tn(low, grads_mix)
    gup[:, rest] += tn(low, grads_rest)
    gdown[...] += tn(grad_low, nrm[...])


def block_kernel(
    dp_count, seq_count,
    in_idx, out_idx, res_ref, cot_ref, win_ref, wout_ref, early_ref, late_ref, par,
    out_ref, gin_ref, gup_in, gdown_in, gup_out, gdown_out,
    xbc, dact, gate, yb, sloc, low, wid, cum, sig, rowt, dreads, cpre, csuf, tot, dtot, start, gown, end,
    theirs, theirs_dec, prefix, passed, tail, wmix, wgate, wout, early, late, up_in, down_in, up_out, down_out,
    halo, rim, stage_res, stage_cot, stage_out, ext, state, snow, gated, nout, prod, run, held, onehot, z, gn,
    wsems, csems, hsems, lsems,
):
    dp = lax.axis_index("dp")
    seq = lax.axis_index("seq")
    seqs, tokens, model = res_ref.shape
    blocks = tokens // BLOCK
    per = BLOCK // CHUNK
    heads, inner = onehot.shape
    mixer = xbc.shape[2]
    rank = up_in.shape[1]
    pairs = seq_count // 2
    side = lax.rem(seq, 2)
    pair = seq // 2
    chips = dp_count // 2
    partner = (seq + 1 - 2 * side, dp)
    sibling = (seq, dp + 1 - 2 * lax.rem(dp, 2))
    later = (lax.rem(seq + 1, seq_count), dp)
    earlier = (lax.rem(seq + seq_count - 1, seq_count), dp)
    upper = (lax.rem(pair + 1, pairs) * 2 + side, dp)
    lower = (lax.rem(pair + pairs - 1, pairs) * 2 + side, dp)
    others = [(seq, lax.rem(dp + 2 * k, dp_count)) for k in range(1, chips)]
    barrier = pltpu.get_barrier_semaphore()
    greeted = [partner, sibling, later, earlier, upper, lower] + others
    for other in greeted:
        pl.semaphore_signal(barrier, inc=1, device_id=other, device_id_type=MESH)

    def load(n):
        s, k = n // blocks, lax.rem(n, blocks) if not isinstance(n, int) else n % blocks
        rows = pl.ds(k * BLOCK, BLOCK)
        return pltpu.make_async_copy(res_ref.at[s, rows], yb.at[n, :, pl.ds(model, model)], lsems.at[n])

    for n in range(seqs * blocks):
        load(n).start()
    onehot[...] = head_onehot(heads, inner)
    pl.semaphore_wait(barrier, len(greeted))

    def send(src, dst, to, sems, *at):
        return pltpu.make_async_remote_copy(
            src_ref=src, dst_ref=dst, send_sem=sems.at[(0,) + at], recv_sem=sems.at[(1,) + at],
            device_id=to, device_id_type=MESH,
        )

    def rows_piece(ref, out, at, to, wide, n):
        share = ref.shape[0]
        half = share // 2

        def source(which):
            return ref.at[pl.ds(pl.multiple_of(which * half, 16), half), pl.ds(at, wide)]

        def target(owner, which):
            return out.at[pl.ds(pl.multiple_of(owner * share + which * half, 16), half), pl.ds(to, wide)]

        return source, target, n

    def table_piece(ref, out, n):
        owned = ref.shape[1]
        return (lambda which: ref.at[which]), (lambda owner, which: out.at[which, pl.ds(owner * owned, owned)]), n

    width = wmix.shape[1]
    split = width // 2 // LANES * LANES
    groups = [
        [
            table_piece(early_ref, early, 0),
            rows_piece(win_ref, wmix, inner, 0, split, 1),
            rows_piece(win_ref, wmix, inner + split, split, width - split, 2),
        ],
        [
            table_piece(late_ref, late, 3),
            rows_piece(win_ref, wgate, 0, 0, inner, 4),
            rows_piece(wout_ref, wout, 0, 0, wout_ref.shape[1], 5),
        ],
    ]

    def shards(k):
        return lax.rem(dp - 2 * k + dp_count, dp_count)

    def over_x(group):
        return [send(source(side), target(dp, side), others[k - 1], wsems, 0, k, n) for source, target, n in group for k in range(1, chips)]

    def own(group):
        copies = []
        for source, target, n in group:
            for which in range(2):
                copies.append(pltpu.make_async_copy(source(which), target(dp, which), wsems.at[0, 6 + which, 0, n]))
                copies.append(send(source(which), target(dp, which), sibling, wsems, 3 + which, 0, n))
        return copies

    def forward(group, start_it):
        for source, target, n in group:
            for k in range(1, chips):
                here = target(shards(k), side)
                if start_it:
                    send(source(side), here, others[k - 1], wsems, 0, k, n).wait_recv()
                across = send(here, here, partner, wsems, 1, k, n)
                over = send(here, here, sibling, wsems, 2, k, n)
                if start_it:
                    across.start()
                    over.start()
                else:
                    across.wait_send()
                    over.wait()

    def relay(group, start_it):
        for source, target, n in group:
            for k in range(1, chips):
                there = target(shards(k), 1 - side)
                over = send(there, there, sibling, wsems, 5, k, n)
                if start_it:
                    send(there, there, partner, wsems, 1, k, n).wait_recv()
                    over.start()
                else:
                    over.wait()

    edge = send(res_ref.at[:, pl.ds(tokens - RIM, RIM)], halo, later, hsems, 0)
    for copy in over_x(groups[0]):
        copy.start()

    @pl.when(seq < seq_count - 1)
    def _():
        edge.start()

    for copy in own(groups[0]):
        copy.start()
    gain = par[NORM_GAIN, :model]

    def norm_block(n, _):
        load(n).wait()
        write_normed(yb.at[n, :, pl.ds(0, model)], yb.at[n, :, pl.ds(model, model)], gain, 32)
        return 0

    lax.fori_loop(0, seqs * blocks, norm_block, 0)
    forward(groups[0], True)
    relay(groups[0], True)

    @pl.when(seq == 0)
    def _():
        halo[...] = jnp.zeros_like(halo)

    @pl.when(seq > 0)
    def _():
        edge.wait_recv()

    @pl.when(seq < seq_count - 1)
    def _():
        edge.wait_send()

    for copy in over_x(groups[0]):
        copy.wait_send()
    for copy in over_x(groups[1]):
        copy.start()
    for copy in own(groups[0]):
        copy.wait()
    forward(groups[0], False)
    relay(groups[0], False)
    for copy in own(groups[1]):
        copy.start()

    def pick(table, dests):
        half = table.shape[3] // LANES
        n = 0
        for dst, at, wide, idx_ref in dests:
            for k in range(wide // LANES):
                src = slice(n % half * LANES, n % half * LANES + LANES)
                for s in range(seqs):
                    dst[s, :, at + k * LANES : at + (k + 1) * LANES] = table[n // half, idx_ref[s, 0], :, src]
                n += 1

    lanes = up_in.shape[2]
    pick(early, [(up_in, inner, lanes - inner, in_idx), (down_in, 0, model, in_idx)])

    half = inner // 2
    wide = half // PARTS

    def cols(base, q):
        return pl.ds(pl.multiple_of(base * half + q * wide, LANES), wide)

    def chain(d, s):
        my_pair = pairs - 1 - pair if d else pair
        my_side = 1 - side if d else side
        ahead = lower if d else upper
        total, result = (gown, end) if d else (tot, start)

        def decs():
            return send(dtot.at[s], theirs_dec.at[d, s], partner, csems, d, s, 3, 0)

        def swap(q):
            return send(total.at[s, :, cols(1 - my_side, q)], theirs.at[d, s, q], partner, csems, d, s, 0, q)

        def hop(q):
            return send(passed.at[d, s, q], prefix.at[d, s, q], ahead, csems, d, s, 1, q)

        def give(q):
            return send(tail.at[d, s, q], result.at[s, :, cols(my_side, q)], partner, csems, d, s, 2, q)

        return my_pair, my_side, total, result, decs, swap, hop, give

    def chain_start(d, s):
        _, _, _, _, decs, swap, _, _ = chain(d, s)
        decs().start()
        for q in range(PARTS):
            swap(q).start()

    def chain_tick(d, s, tick, final):
        my_pair, my_side, total, result, decs, swap, hop, give = chain(d, s)
        for q in range(PARTS):
            turn = jnp.minimum(my_pair + (1 if q else 0), final)

            @pl.when(tick == turn)
            def _(q=q):
                if q == 0:
                    decs().wait_recv()
                swap(q).wait_recv()

                @pl.when(my_pair == 0)
                def _():
                    prefix[d, s, q] = jnp.zeros_like(prefix[d, s, q])

                @pl.when(my_pair > 0)
                def _():
                    hop(q).wait_recv()

                own_dec = dtot[s, 0:1, cols(my_side, q)]
                their_dec = theirs_dec[d, s, 0:1, cols(my_side, q)]
                own_total = total[s, :, cols(my_side, q)].astype(F32)
                other = theirs[d, s, q].astype(F32)
                before = prefix[d, s, q].astype(F32)
                left = my_side == 0
                first = jnp.where(left, own_total, other)
                second = jnp.where(left, other, own_total)
                first_dec = jnp.where(left, own_dec, their_dec)
                second_dec = jnp.where(left, their_dec, own_dec)
                middle = first_dec * before + first
                passed[d, s, q] = (second_dec * middle + second).astype(BF)

                @pl.when(my_pair < pairs - 1)
                def _():
                    hop(q).start()

                result[s, :, cols(my_side, q)] = jnp.where(left, before, middle).astype(BF)
                tail[d, s, q] = jnp.where(left, middle, before).astype(BF)
                give(q).start()

    def chain_end(d, s):
        my_pair, _, _, _, decs, swap, hop, give = chain(d, s)
        decs().wait_send()
        for q in range(PARTS):
            give(q).wait()
            swap(q).wait_send()

            @pl.when(my_pair < pairs - 1)
            def _(q=q):
                hop(q).wait_send()

    def chunk_of(n):
        return pl.ds(n * per, per)

    def project_block(n, _):
        s, k = n // blocks, lax.rem(n, blocks)
        project_step(
            k == 0, yb.at[n, :, pl.ds(0, model)], halo.at[s], wmix, down_in.at[s], up_in.at[s], par, low.at[n],
            xbc.at[n], dact.at[n], wid.at[n], cum.at[n], sig.at[n], sloc.at[chunk_of(n)], cpre.at[chunk_of(n)],
            ext, state, run, onehot,
        )

        @pl.when(k == blocks - 1)
        def _():
            tot[s] = state[...].astype(BF)
            dtot[s] = spread(jnp.exp(run[...]), onehot[...])

        @pl.when(n == blocks - 1)
        def _():
            forward(groups[1], True)
            chain_start(0, 0)

        @pl.when(n >= blocks)
        def _():
            chain_tick(0, 0, n - blocks, 2 * blocks)

        return 0

    lax.fori_loop(0, seqs * blocks, project_block, 0)
    chain_start(0, 1)
    relay(groups[1], True)
    for copy in over_x(groups[1]):
        copy.wait_send()
    for copy in own(groups[1]):
        copy.wait()
    forward(groups[1], False)
    relay(groups[1], False)
    pick(late, [(up_in, 0, inner, in_idx), (down_out, 0, inner, out_idx), (up_out, 0, model, out_idx)])

    def intra_block(n, _):
        s = n // blocks
        intra_step(
            yb.at[n, :, pl.ds(0, model)], low.at[n], wgate, up_in.at[s], xbc.at[n], wid.at[n], cum.at[n], gate.at[n],
            yb.at[n], onehot,
        )

        @pl.when(n <= blocks)
        def _():
            chain_tick(0, 0, n + blocks, 2 * blocks)

        chain_tick(0, 1, n, seqs * blocks - 1)
        return 0

    lax.fori_loop(0, seqs * blocks, intra_block, 0)
    chain_end(0, 0)

    def staged(s, k):
        rows = pl.ds(k * BLOCK, BLOCK)
        return [
            pltpu.make_async_copy(res_ref.at[s, rows], stage_res, lsems.at[0]),
            pltpu.make_async_copy(cot_ref.at[s, rows], stage_cot, lsems.at[1]),
        ]

    def stored(ref, s, k):
        return pltpu.make_async_copy(stage_out, ref.at[s, pl.ds(k * BLOCK, BLOCK)], lsems.at[2])

    def output_block(i, _):
        s, k = i // blocks, blocks - 1 - lax.rem(i, blocks)
        n = s * blocks + k
        for copy in staged(s, k):
            copy.start()

        @pl.when(i == blocks)
        def _():
            chain_end(0, 1)

        def middle():
            @pl.when(i >= blocks)
            def _():
                chain_tick(1, 0, 2 * (i - blocks), 2 * blocks - 1)

        def loaded():
            for copy in staged(s, k):
                copy.wait()

            @pl.when(i > 0)
            def _():
                stored(out_ref, s, k).wait()

        output_step(
            k == blocks - 1, middle, loaded, yb.at[n], xbc.at[n], gate.at[n], cum.at[n], sloc.at[chunk_of(n)],
            cpre.at[chunk_of(n)], csuf.at[chunk_of(n)], start.at[s], stage_res, stage_cot, stage_out, wout, down_out.at[s],
            up_out.at[s], par, dreads.at[n], rowt.at[n], gup_out.at[s], gdown_out.at[s], onehot, snow, state, run, gated,
            nout, ext, prod,
        )
        stored(out_ref, s, k).start()

        @pl.when(k == 0)
        def _():
            gown[s] = state[...].astype(BF)

        @pl.when(i == blocks - 1)
        def _():
            chain_start(1, 0)

        @pl.when(i >= blocks)
        def _():
            chain_tick(1, 0, 2 * (i - blocks) + 1, 2 * blocks - 1)

        return 0

    lax.fori_loop(0, seqs * blocks, output_block, 0)
    stored(out_ref, seqs - 1, 0).wait()
    chain_start(1, 1)

    def rim_edge(s):
        return send(dact.at[s * blocks, pl.ds(0, RIM)], rim.at[s], earlier, hsems, 1 + s)

    period = 2 * blocks - 1
    steps = seqs * period + seqs

    def back_block(i, _):
        late_one = i >= seqs * period
        s = jnp.where(late_one, i - seqs * period, i // period)
        r = jnp.where(late_one, 2 * blocks - 1, lax.rem(i, period))

        @pl.when(r < blocks)
        def _():
            k = blocks - 1 - r
            n = s * blocks + k

            @pl.when(i == 0)
            def _():
                chain_end(1, 0)

            @pl.when(i == period)
            def _():
                chain_end(1, 1)

            def between(j):
                @pl.when(i < blocks)
                def _():
                    chain_tick(1, 1, per * i + (per - 1 - j), per * blocks - 1)

            adjoint_step(
                k == blocks - 1, between, xbc.at[n], dact.at[n], wid.at[n], cum.at[n], sig.at[n], yb.at[n], dreads.at[n],
                rowt.at[n], sloc.at[chunk_of(n)], csuf.at[chunk_of(n)], end.at[s],
                lambda t: tot[s, :, t].astype(F32) + dtot[s, 0:1, t] * start[s, :, t].astype(F32),
                par, onehot, nout.at[pl.ds(0, CHUNK)], prod, z, held,
            )

            @pl.when(k == 0)
            def _():
                for q in range(seqs):
                    @pl.when((s == q) & (seq > 0))
                    def _(q=q):
                        rim_edge(q).start()

        @pl.when(r >= blocks)
        def _():
            k = r - blocks
            n = s * blocks + k
            for copy in staged(s, k):
                copy.start()
            for q in range(seqs):
                @pl.when((s == q) & (k == 0) & (seq > 0))
                def _(q=q):
                    rim_edge(q).wait_send()

                @pl.when((s == q) & late_one & (seq < seq_count - 1))
                def _(q=q):
                    rim_edge(q).wait_recv()

                @pl.when((s == q) & late_one & (seq == seq_count - 1))
                def _(q=q):
                    rim[q] = jnp.zeros_like(rim[q])

            def loaded():
                for copy in staged(s, k):
                    copy.wait()

                @pl.when(i > blocks)
                def _():
                    stored(gin_ref, s, k).wait()

            def following():
                @pl.when(late_one)
                def _():
                    for m, t in enumerate(tiles(mixer)):
                        ext[m, BLOCK : BLOCK + RIM, :] = rim[s, :, t].astype(F32)

                @pl.when(jnp.logical_not(late_one))
                def _():
                    for m, t in enumerate(tiles(mixer)):
                        ext[m, BLOCK : BLOCK + RIM, :] = dact[n + 1, 0:RIM, t].astype(F32)

            input_step(
                k == 0, loaded, following, dact.at[n], gate.at[n], sig.at[n], low.at[n], stage_res, stage_cot, stage_out,
                wgate, wmix, down_in.at[s], up_in.at[s], par, gup_in.at[s], gdown_in.at[s], ext, gn,
                nout.at[:, pl.ds(0, model)],
            )
            stored(gin_ref, s, k).start()

        return 0

    lax.fori_loop(0, steps, back_block, 0)
    stored(gin_ref, seqs - 1, blocks - 1).wait()


def block_call(in_index, out_index, residual, cotangent, in_weight, out_weight, early, late, params, sizes, dp_count, seq_count):
    heads, inner, mixer, rank = sizes
    seqs, tokens, model = residual.shape
    states = (mixer - inner) // 2
    count = tokens // BLOCK * seqs
    chunks = tokens // CHUNK * seqs
    proj = in_weight.shape[1]
    lanes = -(-proj // LANES) * LANES
    rows = lambda width, kind: pltpu.VMEM((count, BLOCK, width), kind)
    state = lambda: pltpu.VMEM((seqs, states, inner), BF)
    slots = lambda: pltpu.VMEM((2, seqs, PARTS, states, inner // 2 // PARTS), BF)
    stage = lambda: pltpu.VMEM((BLOCK, model), BF)
    picked = lambda width: pltpu.VMEM((seqs, rank, width), BF)
    any_space = pl.BlockSpec(memory_space=pl.ANY)
    vmem = pl.BlockSpec(memory_space=pltpu.VMEM)
    smem = pl.BlockSpec(memory_space=pltpu.SMEM)
    return pl.pallas_call(
        functools.partial(block_kernel, dp_count, seq_count),
        out_shape=[
            jax.ShapeDtypeStruct(residual.shape, BF),
            jax.ShapeDtypeStruct(residual.shape, BF),
            jax.ShapeDtypeStruct((seqs, rank, proj), F32),
            jax.ShapeDtypeStruct((seqs, rank, model), F32),
            jax.ShapeDtypeStruct((seqs, rank, model), F32),
            jax.ShapeDtypeStruct((seqs, rank, inner), F32),
        ],
        in_specs=[smem, smem] + [any_space] * 6 + [vmem],
        out_specs=[any_space] * 2 + [vmem] * 4,
        scratch_shapes=[
            rows(mixer, BF),
            rows(mixer, BF),
            rows(inner, BF),
            rows(inner, BF),
            pltpu.VMEM((chunks, states, inner), BF),
            rows(rank, BF),
            rows(heads, F32),
            rows(heads, F32),
            rows(heads, F32),
            rows(heads, F32),
            rows(states, F32),
            pltpu.VMEM((chunks, 8, heads), F32),
            pltpu.VMEM((chunks, 8, heads), F32),
            state(),
            pltpu.VMEM((seqs, 8, inner), F32),
            state(),
            state(),
            state(),
            slots(),
            pltpu.VMEM((2, seqs, 8, inner), F32),
            slots(),
            slots(),
            slots(),
            pltpu.VMEM((model, proj - inner), BF),
            pltpu.VMEM((model, inner), BF),
            pltpu.VMEM((inner, model), BF),
            pltpu.VMEM((2, early.shape[1] * dp_count) + early.shape[2:], BF),
            pltpu.VMEM((2, late.shape[1] * dp_count) + late.shape[2:], BF),
            picked(lanes),
            picked(model),
            picked(model),
            picked(inner),
            pltpu.VMEM((seqs, RIM, model), BF),
            pltpu.VMEM((seqs, RIM, mixer), BF),
            stage(),
            stage(),
            stage(),
            pltpu.VMEM((mixer // LANES, BLOCK + RIM, LANES), F32),
            pltpu.VMEM((states, inner), F32),
            pltpu.VMEM((BLOCK // CHUNK, states, inner), BF),
            pltpu.VMEM((BLOCK, inner), BF),
            pltpu.VMEM((BLOCK, inner), BF),
            pltpu.VMEM((CHUNK, inner), BF),
            pltpu.VMEM((8, heads), F32),
            pltpu.VMEM((8, heads), F32),
            pltpu.VMEM((heads, inner), BF),
            pltpu.VMEM((CHUNK, inner), F32),
            pltpu.VMEM((BLOCK, model), F32),
            pltpu.SemaphoreType.DMA((2, 8, max(dp_count // 2, 1), 6)),
            pltpu.SemaphoreType.DMA((2, 2, seqs, 4, PARTS)),
            pltpu.SemaphoreType.DMA((2, 1 + seqs)),
            pltpu.SemaphoreType.DMA((max(count, 3),)),
        ],
        compiler_params=pltpu.CompilerParams(collective_id=1, has_side_effects=True, vmem_limit_bytes=VMEM_LIMIT),
        name="block",
    )(in_index, out_index, residual, cotangent, in_weight, out_weight, early, late, params)


def sums_kernel(
    count, dp_count, up_in_ref, down_in_ref, up_out_ref, down_out_ref, coef_ref,
    final,
    pack, half, half_sent, first, line, red, give, owners, sems,
):
    dp = lax.axis_index("dp")
    seq = lax.axis_index("seq")
    pair, side = seq // 2, lax.rem(seq, 2)
    pairs = count // 2
    share = red.shape[0]
    seqs, rank, _ = up_in_ref.shape
    owned = final.shape[1] // rank
    partner = (seq + 1 - 2 * side, dp)
    along = [(lax.rem(pair + k, pairs) * 2 + side, dp) for k in range(1, pairs)]
    across = [(seq, lax.rem(dp + k, dp_count)) for k in range(1, dp_count)]
    barrier = pltpu.get_barrier_semaphore()
    for other in [partner] + along + across:
        pl.semaphore_signal(barrier, inc=1, device_id=other, device_id_type=MESH)

    places = []
    for n, ref in enumerate((up_in_ref, down_in_ref, up_out_ref, down_out_ref)):
        if n == 2:
            in_tiles = len(places)
        places += [(ref, t.start, t.stop - t.start) for t in tiles(ref.shape[2])]
    for n, (ref, at, wide) in enumerate(places):
        for s in range(seqs):
            v = ref[s, :, at : at + wide]
            if wide < LANES:
                v = jnp.concatenate([v, jnp.zeros((rank, LANES - wide), F32)], axis=1)
            pack[n, s * rank : (s + 1) * rank, :] = v.astype(BF)
    for n in range(len(places), pack.shape[0]):
        pack[n] = jnp.zeros_like(pack[n])
    pl.semaphore_wait(barrier, 1 + len(along) + len(across))

    def send(src, dst, to, *at):
        return pltpu.make_async_remote_copy(
            src_ref=src, dst_ref=dst, send_sem=sems.at[(0,) + at], recv_sem=sems.at[(1,) + at],
            device_id=to, device_id_type=MESH,
        )

    wide = pairs * share
    copy = send(pack.at[pl.ds((1 - side) * wide, wide)], first, partner, 0, 0)
    copy.start()
    copy.wait()

    def add(n, _):
        v = pack[side * wide + n].astype(F32) + first[n].astype(F32)
        half[n] = v
        half_sent[n] = v.astype(BF)
        return 0

    lax.fori_loop(0, wide, add, 0)
    copies = []
    for k in range(1, pairs):
        there = lax.rem(pair + k, pairs)
        copies.append(send(half_sent.at[pl.ds(there * share, share)], line.at[k - 1], along[k - 1], 1, k))
        copies[-1].start()
    for copy in copies:
        copy.wait()
    for n in range(share):
        v = half[pair * share + n]
        for k in range(pairs - 1):
            v = v + line[k, n].astype(F32)
        red[n] = v

    def part(owner, n, a):
        tile = (side * pairs + pair) * share + n
        kind = jnp.where(tile < in_tiles, 0, 1)
        total = None
        for s in range(seqs):
            c = coef_ref[kind, (owner * owned + a) * seqs + s]
            term = c * red[n, s * rank : (s + 1) * rank, :]
            total = term if total is None else total + term
        return total

    copies = []
    for k in range(1, dp_count):
        owner = lax.rem(dp + k, dp_count)
        for n in range(share):
            for a in range(owned):
                give[k - 1, n, a * rank : (a + 1) * rank, :] = part(owner, n, a).astype(BF)
        copies.append(send(give.at[k - 1], owners.at[k - 1], across[k - 1], 2, k))
        copies[-1].start()
    mine = [[part(dp, n, a) for a in range(owned)] for n in range(share)]
    for copy in copies:
        copy.wait()
    here = pl.ds((side * pairs + pair) * share, share)
    for n in range(share):
        for a in range(owned):
            v = mine[n][a]
            for k in range(dp_count - 1):
                v = v + owners[k, n, a * rank : (a + 1) * rank, :].astype(F32)
            final[(side * pairs + pair) * share + n, a * rank : (a + 1) * rank, :] = v.astype(BF)
    copies = []
    for k in range(1, pairs):
        copies.append(send(final.at[here], final.at[here], along[k - 1], 3, k))
        copies[-1].start()
    for copy in copies:
        copy.wait()
    ours = final.at[pl.ds(side * wide, wide)]
    copy = send(ours, ours, partner, 4, 0)
    copy.start()
    copy.wait()

def unpack_kernel(final, up_in_out, down_in_out, up_out_out, down_out_out):
    owned, rank, _ = up_in_out.shape
    n = 0
    for out in (up_in_out, down_in_out, up_out_out, down_out_out):
        for t in tiles(out.shape[2]):
            for a in range(owned):
                out[a, :, t] = final[n, a * rank : (a + 1) * rank, : t.stop - t.start].astype(F32)
            n += 1


def adapter_sums(grads, coef, owned, count, dp_count):
    up_in, down_in, up_out, down_out = grads
    seqs, rank, _ = up_in.shape
    total = sum(-(-g.shape[2] // LANES) for g in grads)
    share = -(-total // count)
    pairs = count // 2
    rows = seqs * rank
    own_rows = owned * rank
    whole = pl.BlockSpec(memory_space=pltpu.VMEM)
    final = pl.pallas_call(
        functools.partial(sums_kernel, count, dp_count),
        out_shape=jax.ShapeDtypeStruct((share * count, own_rows, LANES), BF),
        in_specs=[whole] * 4 + [pl.BlockSpec(memory_space=pltpu.SMEM)],
        out_specs=whole,
        scratch_shapes=[
            pltpu.VMEM((share * count, rows, LANES), BF),
            pltpu.VMEM((share * pairs, rows, LANES), F32),
            pltpu.VMEM((share * pairs, rows, LANES), BF),
            pltpu.VMEM((share * pairs, rows, LANES), BF),
            pltpu.VMEM((max(pairs - 1, 1), share, rows, LANES), BF),
            pltpu.VMEM((share, rows, LANES), F32),
            pltpu.VMEM((max(dp_count - 1, 1), share, own_rows, LANES), BF),
            pltpu.VMEM((max(dp_count - 1, 1), share, own_rows, LANES), BF),
            pltpu.SemaphoreType.DMA((2, 5, max(pairs, dp_count))),
        ],
        compiler_params=pltpu.CompilerParams(collective_id=4, has_side_effects=True, vmem_limit_bytes=VMEM_LIMIT),
        name="adapter_sums",
    )(up_in, down_in, up_out, down_out, coef)
    return pl.pallas_call(
        unpack_kernel,
        out_shape=[jax.ShapeDtypeStruct((owned, rank, g.shape[2]), F32) for g in grads],
        in_specs=[whole],
        out_specs=[whole] * 4,
        name="unpack",
    )(final)


def halves(parts):
    padded = [jnp.pad(part, ((0, 0), (0, 0), (0, -part.shape[2] % LANES))) for part in parts]
    whole = jnp.concatenate(padded, axis=2)
    whole = jnp.pad(whole, ((0, 0), (0, 0), (0, -whole.shape[2] % (2 * LANES))))
    half = whole.shape[2] // 2
    return jnp.stack([whole[:, :, :half], whole[:, :, half:]])


def on_device(
    residual_in,
    cotangent,
    norm_gain,
    in_weight,
    conv_weight,
    conv_bias,
    step_bias,
    decay_log,
    skip_gain,
    gate_gain,
    out_weight,
    in_down,
    in_up,
    out_down,
    out_up,
    in_index,
    out_index,
):
    heads = step_bias.shape[0]
    inner = gate_gain.shape[0]
    mixer = conv_weight.shape[0]
    rank = in_up.shape[1]
    seq_count = lax.axis_size("seq")
    dp_count = lax.axis_size("dp")
    adapters = in_down.shape[0] * dp_count

    taps = conv_weight.T
    small = [conv_bias, gate_gain, norm_gain, jnp.repeat(skip_gain, inner // heads), step_bias, -jnp.exp(decay_log)]
    small = [jnp.pad(v, (0, mixer - v.shape[0]))[None, :] for v in small]
    params = jnp.concatenate([taps] + small, axis=0)
    early = halves([in_up[:, :, inner:], in_down.transpose(0, 2, 1)])
    late = halves([in_up[:, :, :inner], out_down.transpose(0, 2, 1), out_up])
    block_out, grad_input, gin_up, gin_down, gout_up, gout_down = block_call(
        in_index, out_index, residual_in, cotangent, in_weight, out_weight, early, late, params,
        (heads, inner, mixer, rank), dp_count, seq_count,
    )
    owners = jnp.arange(adapters)[:, None]
    coef = jnp.stack([(index[:, 0][None, :] == owners).astype(F32).reshape(-1) for index in (in_index, out_index)])
    gin_up, gin_down, gout_up, gout_down = adapter_sums(
        (gin_up, gin_down, gout_up, gout_down), coef, in_down.shape[0], seq_count, dp_count
    )
    gin_down, gout_down = (g.transpose(0, 2, 1) for g in (gin_down, gout_down))
    return (block_out, grad_input, gin_down, gin_up, gout_down, gout_up)


def solution(mesh):
    rows = P("dp", "seq", None)
    split = P("dp", None, None)
    return jax.shard_map(
        on_device,
        mesh=mesh,
        in_specs=(
            rows,
            rows,
            P(),
            P("dp", None),
            P(),
            P(),
            P(),
            P(),
            P(),
            P(),
            P("dp", None),
            split,
            split,
            split,
            split,
            P("dp", None),
            P("dp", None),
        ),
        out_specs=(rows, rows, split, split, split, split),
        check_vma=False,
    )
```

```python
import functools

import jax
import jax.numpy as jnp
from jax import lax
from jax.experimental import pallas as pl
from jax.experimental.pallas import tpu as pltpu
from jax.sharding import PartitionSpec as P

EPS = 1e-05
CHUNK = 128
BLOCK = 256
RIM = 16
LANES = 128
LOG2E = 1.4426950408889634
BF = jnp.bfloat16
F32 = jnp.float32
MESH = pl.DeviceIdType.MESH
VMEM_LIMIT = 62 * 2**20
PARTS = 3
FINAL = 4
CONV_BIAS, GATE_GAIN, NORM_GAIN, SKIP, STEP_BIAS, RATE = (slice(4 + n, 5 + n) for n in range(6))


def nn(a, b):
    return lax.dot_general(a, b, (((1,), (0,)), ((), ())), preferred_element_type=F32)


def nt(a, b):
    return lax.dot_general(a, b, (((1,), (1,)), ((), ())), preferred_element_type=F32)


def tn(a, b):
    return lax.dot_general(a, b, (((0,), (0,)), ((), ())), preferred_element_type=F32)


def sigmoid(v):
    return 0.5 * jnp.tanh(0.5 * v) + 0.5


def two_terms(values, heads):
    lane = lax.broadcasted_iota(jnp.int32, values.shape, 1)
    values = jnp.where(lane < heads, values, 0.0)
    high = values.astype(BF).astype(F32)
    return (high + pltpu.roll(values - high, LANES // 2, 1)).astype(BF)


def spread(values, onehot, heads):
    return nn(two_terms(values, heads), onehot)


def gather_heads(values, onehot, heads):
    sums = nt(values, onehot)
    lane = lax.broadcasted_iota(jnp.int32, sums.shape, 1)
    return jnp.where(lane < heads, sums, 0.0)


def running(ones, values, heads):
    sums = nn(ones.astype(BF), two_terms(values, heads))
    return sums + pltpu.roll(sums, LANES // 2, 1)


def head_onehot(heads, inner):
    width = inner // heads
    row = lax.broadcasted_iota(jnp.int32, (LANES, inner), 0)
    col = lax.broadcasted_iota(jnp.int32, (LANES, inner), 1)
    row = jnp.where(row < LANES // 2, row, row - LANES // 2)
    low = row * width
    return jnp.where((col >= low) & (col < low + width), 1.0, 0.0).astype(BF)


def lower_ones(length):
    row = lax.broadcasted_iota(jnp.int32, (length, length), 0)
    col = lax.broadcasted_iota(jnp.int32, (length, length), 1)
    return jnp.where(row >= col, 1.0, 0.0).astype(F32)


def upper_ones(length):
    row = lax.broadcasted_iota(jnp.int32, (length, length), 0)
    col = lax.broadcasted_iota(jnp.int32, (length, length), 1)
    return jnp.where(row <= col, 1.0, 0.0).astype(F32)


def tiles(width):
    return [slice(at, min(at + LANES, width)) for at in range(0, width, LANES)]


def rows_of(j):
    return slice(j * CHUNK, (j + 1) * CHUNK)


def write_normed(dst, src, gain, step):
    rows = src.shape[0]

    def body(k, _):
        at = pl.ds(pl.multiple_of(k * step, step), step)
        v = src[at, :].astype(F32)
        scale = lax.rsqrt(jnp.mean(v * v, axis=1, keepdims=True) + EPS)
        dst[at, :] = (v * scale * gain).astype(BF)
        return 0

    lax.fori_loop(0, rows // step, body, 0)


def project_step(heads, first_block, normed, halo, win, wtail, down, up, par, low_ref, xbc, dact, wid, cum, sig, sloc, cpre, ext, state, run, onehot):
    rows = normed.shape[0]
    inner = onehot.shape[1]
    mixer = xbc.shape[1]
    states = (mixer - inner) // 2

    @pl.when(first_block)
    def _():
        state[...] = jnp.zeros_like(state)
        run[...] = jnp.zeros_like(run)
        v = halo[...].astype(F32)
        scale = lax.rsqrt(jnp.mean(v * v, axis=1, keepdims=True) + EPS)
        first = (v * scale * par[NORM_GAIN, : normed.shape[1]]).astype(BF)
        both = jnp.concatenate([first, nt(first, down[...]).astype(BF)], axis=1)
        for at in range(0, mixer, 2 * LANES):
            t = slice(at, at + 2 * LANES)
            v = nn(both, jnp.concatenate([win[:, t], up[:, inner + at : inner + at + 2 * LANES]], axis=0))
            ext[at // LANES, 0:RIM, :] = v[:, :LANES]
            ext[at // LANES + 1, 0:RIM, :] = v[:, LANES:]

    @pl.when(jnp.logical_not(first_block))
    def _():
        ext[:, 0:RIM, :] = ext[:, rows : rows + RIM, :]

    tokens = normed[...]
    low = nt(tokens, down[...]).astype(BF)
    low_ref[...] = low
    both = jnp.concatenate([tokens, low], axis=1)
    for at in range(0, mixer, 2 * LANES):
        t = slice(at, at + 2 * LANES)
        v = nn(both, jnp.concatenate([win[:, t], up[:, inner + at : inner + at + 2 * LANES]], axis=0))
        ext[at // LANES, RIM : RIM + rows, :] = v[:, :LANES]
        ext[at // LANES + 1, RIM : RIM + rows, :] = v[:, LANES:]
    raw = nn(both, jnp.concatenate([wtail[...], up[:, inner + mixer :]], axis=0))
    raw = raw + par[STEP_BIAS, :LANES]
    sig[...] = sigmoid(raw)
    widths = jnp.maximum(raw, 0.0) + jnp.log1p(jnp.exp(-jnp.abs(raw)))
    wid[...] = widths
    ones = lower_ones(CHUNK)
    for j in range(rows // CHUNK):
        for n, t in enumerate(tiles(mixer)):
            pre = par[CONV_BIAS, t]
            for k in range(4):
                at = RIM - 3 + k + j * CHUNK
                pre = pre + par[k : k + 1, t] * ext[n, at : at + CHUNK, :]
            s = sigmoid(pre)
            act = pre * s
            xbc[rows_of(j), t] = act.astype(BF)
            dact[rows_of(j), t] = (s + act * (1.0 - s)).astype(BF)
    for j in range(rows // CHUNK):
        w = widths[rows_of(j)]
        c = running(ones, w * par[RATE, :LANES], heads)
        cum[rows_of(j)] = c
        last = c[CHUNK - 1 : CHUNK]
        tail = spread(jnp.exp(last - c) * w, onehot[...], heads)
        weighted = jnp.concatenate(
            [(xbc[rows_of(j), t].astype(F32) * tail[:, t]).astype(BF) for t in tiles(inner)], axis=1
        )
        inputs_t = xbc[rows_of(j), inner : inner + states].astype(F32).T.astype(BF)
        update = nn(inputs_t, weighted)
        before = run[...]
        cpre[j] = before
        keep = spread(jnp.exp(jnp.broadcast_to(last, before.shape)), onehot[...], heads)[0:1]
        for t in tiles(inner):
            old = state[:, t]
            sloc[j, :, t] = old.astype(BF)
            state[:, t] = keep[:, t] * old + update[:, t]
        run[...] = before + last


def intra_step(heads, normed, low_ref, win, up, xbc, wid, cum, gate, y, onehot):
    inner = onehot.shape[1]
    states = (xbc.shape[1] - inner) // 2
    width = inner // heads
    per = LANES // width
    both = jnp.concatenate([normed[...], low_ref[...]], axis=1)
    for at in range(0, inner, 2 * LANES):
        t = slice(at, at + 2 * LANES)
        gate[:, t] = nn(both, jnp.concatenate([win[:, t], up[:, t]], axis=0)).astype(BF)
    lane = lax.broadcasted_iota(jnp.int32, (CHUNK, LANES), 1)
    mask = lower_ones(CHUNK)
    for j in range(xbc.shape[0] // CHUNK):
        c = cum[rows_of(j)] * LOG2E
        c_rows = c.T
        wide = spread(wid[rows_of(j)], onehot[...], heads)
        inputs = xbc[rows_of(j), inner : inner + states]
        reads = xbc[rows_of(j), inner + states :]
        scores = nt(reads, inputs) * mask
        for k, t in enumerate(tiles(inner)):
            weighted = xbc[rows_of(j), t].astype(F32) * wide[:, t]
            mixing, parts = [], []
            for p in range(per):
                h = k * per + p
                kernel = jnp.exp2(jnp.minimum(c[:, h : h + 1] - c_rows[h : h + 1, :], 0.0))
                mixing.append((kernel * scores).astype(BF))
                inside = (lane >= p * width) & (lane < (p + 1) * width)
                parts.append(jnp.where(inside, weighted, 0.0).astype(BF))
            y[rows_of(j), t] = nn(jnp.concatenate(mixing, axis=1), jnp.concatenate(parts, axis=0)).astype(BF)


def output_step(
    heads, first_block, middle, loaded, y, xbc, gate, cum, sloc, cpre, csuf, start, res, cot, out, wout, down, up, par,
    dreads, rowt, gup, gdown, onehot, snow, adj, run, gated, nout, gno, prod,
):
    rows = res.shape[0]
    inner = onehot.shape[1]
    states = (xbc.shape[1] - inner) // 2
    chunks = rows // CHUNK

    @pl.when(first_block)
    def _():
        adj[...] = jnp.zeros_like(adj)
        run[...] = jnp.zeros_like(run)
        gup[...] = jnp.zeros_like(gup)
        gdown[...] = jnp.zeros_like(gdown)

    reach, scale = [], []
    for j in range(chunks):
        since = spread(jnp.exp(cpre[j]), onehot[...], heads)
        for t in tiles(inner):
            snow[j, :, t] = (sloc[j, :, t].astype(F32) + since[0:1, t] * start[:, t].astype(F32)).astype(BF)
        carried = nn(xbc[rows_of(j), inner + states :], snow[j])
        grow = spread(jnp.exp(cum[rows_of(j)]), onehot[...], heads)
        reach.append(grow)
        total = jnp.zeros((CHUNK, LANES), F32)
        for t in tiles(inner):
            local = y[rows_of(j), t].astype(F32) + grow[:, t] * carried[:, t]
            y[rows_of(j), t] = local.astype(BF)
            g = gate[rows_of(j), t].astype(F32)
            v = (local + par[SKIP, t] * xbc[rows_of(j), t].astype(F32)) * (g * sigmoid(g))
            gated[rows_of(j), t] = v.astype(BF)
            total = total + v * v
        r = lax.rsqrt(jnp.sum(total, axis=1, keepdims=True) * (1.0 / inner) + EPS)
        scale.append(r)
        for t in tiles(inner):
            nout[rows_of(j), t] = (gated[rows_of(j), t].astype(F32) * r * par[GATE_GAIN, t]).astype(BF)

    middle()
    loaded()
    normed_out = nout[...]
    cot_rows = cot[...]
    low_out = nt(normed_out, down[...]).astype(BF)
    both = jnp.concatenate([normed_out, low_out], axis=1)
    for at in range(0, out.shape[1], 2 * LANES):
        t = slice(at, at + 2 * LANES)
        part = nn(both, jnp.concatenate([wout[:, t], up[:, t]], axis=0))
        out[:, t] = (res[:, t].astype(F32) + part).astype(BF)
    grad_low = nt(cot_rows, up[...]).astype(BF)
    for at in range(0, inner, 2 * LANES):
        t = slice(at, at + 2 * LANES)
        v = nt(cot_rows, wout[t, :]) + nn(grad_low, down[:, t])
        gno[at // LANES, 0:rows, :] = v[:, :LANES]
        gno[at // LANES + 1, 0:rows, :] = v[:, LANES:]
    gup[...] += tn(low_out, cot_rows)
    gdown[...] += tn(grad_low, normed_out)

    for j in reversed(range(chunks)):
        total = jnp.zeros((CHUNK, LANES), F32)
        for n, t in enumerate(tiles(inner)):
            q = gno[n, rows_of(j), :] * par[GATE_GAIN, t]
            total = total + gated[rows_of(j), t].astype(F32) * q
        r = scale[j]
        shrink = jnp.sum(total, axis=1, keepdims=True) * (1.0 / inner) * (r * r * r)
        scaled = []
        for n, t in enumerate(tiles(inner)):
            q = gno[n, rows_of(j), :] * par[GATE_GAIN, t]
            grad = r * q - gated[rows_of(j), t].astype(F32) * shrink
            local = y[rows_of(j), t].astype(F32)
            g = gate[rows_of(j), t].astype(F32)
            s = sigmoid(g)
            dy = grad * (g * s)
            y[rows_of(j), t] = dy.astype(BF)
            full = local + par[SKIP, t] * xbc[rows_of(j), t].astype(F32)
            gate[rows_of(j), t] = (grad * full * (s * (1.0 + g * (1.0 - s)))).astype(BF)
            prod[:, t] = (dy * local).astype(BF)
            scaled.append((dy * reach[j][:, t]).astype(BF))
        rowt[rows_of(j)] = gather_heads(prod[...], onehot[...], heads)
        scaled = jnp.concatenate(scaled, axis=1)
        reads_t = xbc[rows_of(j), inner + states :].astype(F32).T.astype(BF)
        update = nn(reads_t, scaled)
        dreads[rows_of(j)] = nt(scaled, snow[j])
        last = cum[j * CHUNK + CHUNK - 1 : j * CHUNK + CHUNK]
        before = run[...]
        csuf[j] = before
        keep = reach[j][CHUNK - 1 : CHUNK]
        for t in tiles(inner):
            old = adj[:, t]
            sloc[j, :, t] = old.astype(BF)
            adj[:, t] = keep[:, t] * old + update[:, t]
        run[...] = before + last


def adjoint_step(heads, first_block, between, xbc, dact, wid, cum, sig, dy, dreads, rowt, gloc, csuf, end, final, par, onehot, adj, prod, z, held):
    inner = onehot.shape[1]
    states = (xbc.shape[1] - inner) // 2
    width = inner // heads
    per = LANES // width
    mask = upper_ones(CHUNK)
    lane = lax.broadcasted_iota(jnp.int32, (CHUNK, LANES), 1)

    @pl.when(first_block)
    def _():
        overlap = []
        for t in tiles(inner):
            overlap.append(jnp.sum(end[:, t].astype(F32) * final(t), axis=0, keepdims=True))
        v = jnp.broadcast_to(jnp.concatenate(overlap, axis=1), (8, inner))
        high = v.astype(BF)
        rest = (v - high.astype(F32)).astype(BF)
        held[...] = gather_heads(high, onehot[...], heads) + gather_heads(rest, onehot[...], heads)

    for j in reversed(range(xbc.shape[0] // CHUNK)):
        at = rows_of(j)
        c = cum[at]
        w = wid[at]
        c_two = c * LOG2E
        c_rows = c_two.T
        wide = spread(w, onehot[...], heads)
        inputs = xbc[at, inner : inner + states]
        reads = xbc[at, inner + states :]
        scores_t = nt(inputs, reads) * mask
        total = jnp.zeros((CHUNK, CHUNK), F32)
        for k, t in enumerate(tiles(inner)):
            weighted = (xbc[at, t].astype(F32) * wide[:, t]).astype(BF)
            grads = dy[at, t].astype(F32)
            mixing, right = [], []
            for p in range(per):
                inside = (lane >= p * width) & (lane < (p + 1) * width)
                right.append(jnp.where(inside, grads, 0.0).astype(BF))
            right = jnp.concatenate(right, axis=0)
            products = nt(weighted, right)
            for p in range(per):
                h = k * per + p
                kernel = jnp.exp2(jnp.minimum(c_rows[h : h + 1, :] - c_two[:, h : h + 1], 0.0))
                mixing.append((kernel * scores_t).astype(BF))
                total = total + kernel * products[:, p * CHUNK : (p + 1) * CHUNK]
            z[:, t] = nn(jnp.concatenate(mixing, axis=1), right)
        total = total * mask
        dinputs = nn(total.astype(BF), reads)
        dreads_all = dreads[at] + nn(total.T.astype(BF), inputs)

        since = spread(jnp.exp(csuf[j]), onehot[...], heads)
        for t in tiles(inner):
            adj[:, t] = (gloc[j, :, t].astype(F32) + since[0:1, t] * end[:, t].astype(F32)).astype(BF)
        last = c[CHUNK - 1 : CHUNK]
        tail = spread(jnp.exp(last - c), onehot[...], heads)
        carried = nn(inputs, adj[...])
        weighted = []
        for t in tiles(inner):
            x = xbc[at, t].astype(F32)
            v = z[:, t] + tail[:, t] * carried[:, t]
            prod[:, t] = (x * v).astype(BF)
            grad = wide[:, t] * v + par[SKIP, t] * dy[at, t].astype(F32)
            dact[at, t] = (grad * dact[at, t].astype(F32)).astype(BF)
            weighted.append((x * (wide[:, t] * tail[:, t])).astype(BF))
        dinputs = dinputs + nt(jnp.concatenate(weighted, axis=1), adj[...])
        t = slice(inner, inner + states)
        dact[at, t] = (dinputs * dact[at, t].astype(F32)).astype(BF)
        t = slice(inner + states, inner + 2 * states)
        dact[at, t] = (dreads_all * dact[at, t].astype(F32)).astype(BF)
        direct = gather_heads(prod[...], onehot[...], heads)
        grad_rate = held[0:1] + running(mask, rowt[at] - w * direct, heads)
        held[...] = jnp.broadcast_to(grad_rate[0:1], held.shape)
        sig[at] = (direct + par[RATE, :LANES] * grad_rate) * sig[at]
        between(j)


def input_step(heads, first_block, loaded, following, gpre, ggate, graw, low_ref, res, cot, gin, wgate, win, wtail, down, up, par, gup, gdown, ext, gn, nrm):
    rows = res.shape[0]
    inner = ggate.shape[1]
    mixer = gpre.shape[1]
    proj = inner + mixer + heads
    model = res.shape[1]
    gain = par[NORM_GAIN, :model]

    @pl.when(first_block)
    def _():
        gup[...] = jnp.zeros_like(gup)
        gdown[...] = jnp.zeros_like(gdown)

    for n, t in enumerate(tiles(mixer)):
        for j in range(rows // CHUNK):
            ext[n, rows_of(j), :] = gpre[rows_of(j), t].astype(F32)
    following()
    for j in range(rows // CHUNK):
        for n, t in enumerate(tiles(mixer)):
            total = None
            for k in range(4):
                at = 3 - k + j * CHUNK
                term = par[k : k + 1, t] * ext[n, at : at + CHUNK, :]
                total = term if total is None else total + term
            gpre[rows_of(j), t] = total.astype(BF)
    grads_gate, grads_mix = ggate[...], jnp.concatenate([gpre[...], graw[...].astype(BF)], axis=1)
    grad_low = (nt(grads_gate, up[:, :inner]) + nt(grads_mix, up[:, inner:])).astype(BF)
    for at in range(0, model, 2 * LANES):
        t = slice(at, at + 2 * LANES)
        mix = jnp.concatenate([win[t, :mixer], wtail[t, :]], axis=1)
        gn[:, t] = nt(grads_gate, wgate[t, :]) + nt(grads_mix, mix) + nn(grad_low, down[:, t])
    loaded()

    def body(k, _):
        at = pl.ds(pl.multiple_of(k * 32, 32), 32)
        v = res[at, :].astype(F32)
        u = lax.rsqrt(jnp.mean(v * v, axis=1, keepdims=True) + EPS)
        nrm[at, :] = (v * u * gain).astype(BF)
        w = gn[at, :] * gain
        m = jnp.mean(v * w, axis=1, keepdims=True)
        gin[at, :] = (cot[at, :].astype(F32) + u * w - v * (u * u * u * m)).astype(BF)
        return 0

    lax.fori_loop(0, rows // 32, body, 0)
    low = low_ref[...]
    gup[:, :inner] += tn(low, grads_gate)
    gup[:, inner:] += tn(low, grads_mix)[:, : proj - inner]
    gdown[...] += tn(grad_low, nrm[...])


def block_kernel(
    dp_count, seq_count,
    in_idx, out_idx, res_ref, cot_ref, win_ref, wout_ref, up_in_ref, down_in_ref, up_out_ref, down_out_ref,
    taps_ref, conv_bias_ref, gate_gain_ref, norm_gain_ref, skip_ref, step_bias_ref, decay_ref,
    out_ref, gin_ref, gup_in, gdown_in, gup_out, gdown_out,
    xbc, dact, gate, yb, sloc, low, wid, cum, sig, rowt, dreads, cpre, csuf, tot, dtot, start, gown, end,
    theirs, theirs_dec, prefix, passed, tail, wmix, wtail, wgate, wout, up_mix_all, up_gate_all, down_in_all, up_out_all, down_out_all,
    up_in, down_in, up_out, down_out, par,
    halo, rim, stage_res, stage_cot, stage_out, ext, state, snow, gated, nout, prod, run, held, onehot, z, gn,
    wsems, csems, hsems, lsems,
):
    dp = lax.axis_index("dp")
    seq = lax.axis_index("seq")
    seqs, tokens, model = res_ref.shape
    blocks = tokens // BLOCK
    per = BLOCK // CHUNK
    heads = step_bias_ref.shape[0]
    inner = onehot.shape[1]
    mixer = xbc.shape[2]
    proj = win_ref.shape[1]
    pairs = seq_count // 2
    side = lax.rem(seq, 2)
    pair = seq // 2
    chips = dp_count // 2
    partner = (seq + 1 - 2 * side, dp)
    sibling = (seq, dp + 1 - 2 * lax.rem(dp, 2))
    later = (lax.rem(seq + 1, seq_count), dp)
    earlier = (lax.rem(seq + seq_count - 1, seq_count), dp)
    upper = (lax.rem(pair + 1, pairs) * 2 + side, dp)
    lower = (lax.rem(pair + pairs - 1, pairs) * 2 + side, dp)
    others = [(seq, lax.rem(dp + 2 * k, dp_count)) for k in range(1, chips)]
    barrier = pltpu.get_barrier_semaphore()
    greeted = [partner, sibling, later, earlier, upper, lower] + others
    for other in greeted:
        pl.semaphore_signal(barrier, inc=1, device_id=other, device_id_type=MESH)

    def load(n):
        s, k = n // blocks, lax.rem(n, blocks) if not isinstance(n, int) else n % blocks
        rows = pl.ds(k * BLOCK, BLOCK)
        return pltpu.make_async_copy(res_ref.at[s, rows], yb.at[n, :, pl.ds(model, model)], lsems.at[n])

    for n in range(seqs * blocks):
        load(n).start()
    onehot[...] = head_onehot(heads, inner)
    par[...] = jnp.zeros_like(par)
    par[0:4] = taps_ref[...]
    par[CONV_BIAS] = conv_bias_ref[...][None, :]
    par[GATE_GAIN, :inner] = gate_gain_ref[...][None, :]
    par[NORM_GAIN, :model] = norm_gain_ref[...][None, :]
    par[STEP_BIAS, :heads] = step_bias_ref[...][None, :]
    par[RATE, :heads] = -jnp.exp(decay_ref[...][None, :])
    par[SKIP, :heads] = skip_ref[...][None, :]
    v = jnp.broadcast_to(par[SKIP, :LANES], (8, LANES))
    par[SKIP, :inner] = spread(v, onehot[...], heads)[0:1]
    wtail[...] = jnp.zeros_like(wtail)
    up_in[:, :, inner + mixer :] = jnp.zeros(up_in.shape[:2] + (LANES,), BF)
    pl.semaphore_wait(barrier, len(greeted))

    def send(src, dst, to, sems, *at):
        return pltpu.make_async_remote_copy(
            src_ref=src, dst_ref=dst, send_sem=sems.at[(0,) + at], recv_sem=sems.at[(1,) + at],
            device_id=to, device_id_type=MESH,
        )

    def rows_piece(ref, out, at, to, wide, n):
        share = ref.shape[0]
        half = share // 2

        def source(which):
            return ref.at[pl.ds(pl.multiple_of(which * half, 16), half), pl.ds(at, wide)]

        def target(owner, which):
            return out.at[pl.ds(pl.multiple_of(owner * share + which * half, 16), half), pl.ds(to, wide)]

        return source, target, n

    def table_piece(ref, out, at, wide, n):
        owned = ref.shape[0]
        return (lambda _: ref.at[:, :, pl.ds(at, wide)]), (lambda owner, _: out.at[pl.ds(owner * owned, owned)]), n, None, 0

    width = proj - inner
    split = mixer // 2 // LANES * LANES
    odd = lax.rem(pair, 2)
    across_y = (partner, side)
    across_z = (((pair + 1 - 2 * odd) * 2 + side, dp), odd)
    groups = [
        [
            (*rows_piece(win_ref, wmix, inner, 0, split, 0), *across_y),
            (*rows_piece(win_ref, wmix, inner + split, split, width - split, 1), *across_y),
            table_piece(down_in_ref, down_in_all, 0, model, 2),
            table_piece(up_in_ref, up_mix_all, inner, width, 3),
        ],
        [
            table_piece(up_in_ref, up_gate_all, 0, inner, 4),
            (*rows_piece(win_ref, wgate, 0, 0, inner, 5), *across_z),
        ],
        [
            (*rows_piece(wout_ref, wout, 0, 0, wout_ref.shape[1], 6), *across_z),
            table_piece(down_out_ref, down_out_all, 0, inner, 7),
            table_piece(up_out_ref, up_out_all, 0, model, 8),
        ],
    ]

    def shards(k):
        return lax.rem(dp - 2 * k + dp_count, dp_count)

    def over_x(group):
        return [
            send(source(mine), target(dp, mine), others[k - 1], wsems, 0, k, n)
            for source, target, n, _, mine in group
            for k in range(1, chips)
        ]

    def own(group):
        copies = []
        for source, target, n, mate, _ in group:
            for which in range(1 if mate is None else 2):
                copies.append(pltpu.make_async_copy(source(which), target(dp, which), wsems.at[0, 6 + which, 0, n]))
                copies.append(send(source(which), target(dp, which), sibling, wsems, 3 + which, 0, n))
        return copies

    def forward(group, start_it):
        for source, target, n, mate, mine in group:
            for k in range(1, chips):
                here = target(shards(k), mine)
                if start_it:
                    send(source(mine), here, others[k - 1], wsems, 0, k, n).wait_recv()
                copies = [send(here, here, sibling, wsems, 2, k, n)]
                if mate is not None:
                    copies.append(send(here, here, mate, wsems, 1, k, n))
                if start_it:
                    for copy in copies:
                        copy.start()
                else:
                    copies[0].wait()
                    if mate is not None:
                        copies[1].wait_send()

    def relay(group, start_it):
        for source, target, n, mate, mine in group:
            if mate is None:
                continue
            for k in range(1, chips):
                there = target(shards(k), 1 - mine)
                if start_it:
                    send(there, there, mate, wsems, 1, k, n).wait_recv()
                over = send(there, there, sibling, wsems, 5, k, n)
                if start_it:
                    over.start()
                else:
                    over.wait()

    def settle(group):
        for copy in over_x(group):
            copy.wait_send()
        for copy in own(group):
            copy.wait()
        forward(group, False)
        relay(group, False)

    edge = send(res_ref.at[:, pl.ds(tokens - RIM, RIM)], halo, later, hsems, 0)
    for copy in over_x(groups[0]):
        copy.start()

    @pl.when(seq < seq_count - 1)
    def _():
        edge.start()

    for copy in own(groups[0]):
        copy.start()
    gain = par[NORM_GAIN, :model]

    def norm_block(n, _):
        load(n).wait()
        write_normed(yb.at[n, :, pl.ds(0, model)], yb.at[n, :, pl.ds(model, model)], gain, 32)
        return 0

    lax.fori_loop(0, seqs * blocks, norm_block, 0)
    forward(groups[0], True)
    for group in groups[1:]:
        for copy in over_x(group):
            copy.start()
    relay(groups[0], True)

    @pl.when(seq == 0)
    def _():
        halo[...] = jnp.zeros_like(halo)

    @pl.when(seq > 0)
    def _():
        edge.wait_recv()

    @pl.when(seq < seq_count - 1)
    def _():
        edge.wait_send()

    settle(groups[0])
    for group in groups[1:]:
        for copy in own(group):
            copy.start()

    def pick(dst, table, idx_ref, at=0):
        for q in range(seqs):
            dst[q, :, at : at + table.shape[2]] = table[idx_ref[q]]

    pick(down_in, down_in_all, in_idx)
    pick(up_in, up_mix_all, in_idx, inner)
    wtail[:, :heads] = wmix[:, mixer:]

    half = inner // 2
    wide = half // PARTS

    def cols(base, q):
        return pl.ds(pl.multiple_of(base * half + q * wide, LANES), wide)

    def chain(d, s):
        my_pair = pairs - 1 - pair if d else pair
        my_side = 1 - side if d else side
        ahead = lower if d else upper
        total, result = (gown, end) if d else (tot, start)

        def decs():
            return send(dtot.at[s], theirs_dec.at[d, s], partner, csems, d, s, 3, 0)

        def swap(q):
            return send(total.at[s, :, cols(1 - my_side, q)], theirs.at[d, s, q], partner, csems, d, s, 0, q)

        def hop(q):
            return send(passed.at[d, s, q], prefix.at[d, s, q], ahead, csems, d, s, 1, q)

        def give(q):
            return send(tail.at[d, s, q], result.at[s, :, cols(my_side, q)], partner, csems, d, s, 2, q)

        return my_pair, my_side, total, result, decs, swap, hop, give

    def chain_start(d, s):
        _, _, _, _, decs, swap, _, _ = chain(d, s)
        decs().start()
        for q in range(PARTS):
            swap(q).start()

    def chain_tick(d, s, tick, final):
        my_pair, my_side, total, result, decs, swap, hop, give = chain(d, s)
        for q in range(PARTS):
            turn = jnp.minimum(my_pair + (1 if q else 0), final)

            @pl.when(tick == turn)
            def _(q=q):
                if q == 0:
                    decs().wait_recv()
                swap(q).wait_recv()

                @pl.when(my_pair == 0)
                def _():
                    prefix[d, s, q] = jnp.zeros_like(prefix[d, s, q])

                @pl.when(my_pair > 0)
                def _():
                    hop(q).wait_recv()

                own_dec = dtot[s, 0:1, cols(my_side, q)]
                their_dec = theirs_dec[d, s, 0:1, cols(my_side, q)]
                own_total = total[s, :, cols(my_side, q)].astype(F32)
                other = theirs[d, s, q].astype(F32)
                before = prefix[d, s, q].astype(F32)
                left = my_side == 0
                first = jnp.where(left, own_total, other)
                second = jnp.where(left, other, own_total)
                first_dec = jnp.where(left, own_dec, their_dec)
                second_dec = jnp.where(left, their_dec, own_dec)
                middle = first_dec * before + first
                passed[d, s, q] = (second_dec * middle + second).astype(BF)

                @pl.when(my_pair < pairs - 1)
                def _():
                    hop(q).start()

                result[s, :, cols(my_side, q)] = jnp.where(left, before, middle).astype(BF)
                tail[d, s, q] = jnp.where(left, middle, before).astype(BF)
                give(q).start()

    def chain_end(d, s):
        my_pair, _, _, _, decs, swap, hop, give = chain(d, s)
        decs().wait_send()
        for q in range(PARTS):
            give(q).wait()
            swap(q).wait_send()

            @pl.when(my_pair < pairs - 1)
            def _(q=q):
                hop(q).wait_send()

    def chunk_of(n):
        return pl.ds(n * per, per)

    def project_block(n, _):
        s, k = n // blocks, lax.rem(n, blocks)
        project_step(
            heads, k == 0, yb.at[n, :, pl.ds(0, model)], halo.at[s], wmix, wtail, down_in.at[s], up_in.at[s], par, low.at[n],
            xbc.at[n], dact.at[n], wid.at[n], cum.at[n], sig.at[n], sloc.at[chunk_of(n)], cpre.at[chunk_of(n)],
            ext, state, run, onehot,
        )

        @pl.when(k == blocks - 1)
        def _():
            tot[s] = state[...].astype(BF)
            dtot[s] = spread(jnp.exp(run[...]), onehot[...], heads)

        @pl.when(n == blocks - 2)
        def _():
            forward(groups[1], True)

        @pl.when(n == blocks - 1)
        def _():
            forward(groups[2], True)
            chain_start(0, 0)

        @pl.when(n >= blocks)
        def _():
            chain_tick(0, 0, n - blocks, FINAL)

        return 0

    lax.fori_loop(0, seqs * blocks, project_block, 0)
    chain_start(0, 1)
    relay(groups[1], True)
    settle(groups[1])
    pick(up_in, up_gate_all, in_idx)

    def intra_block(n):
        s = n // blocks
        intra_step(
            heads, yb.at[n, :, pl.ds(0, model)], low.at[n], wgate, up_in.at[s], xbc.at[n], wid.at[n], cum.at[n], gate.at[n],
            yb.at[n], onehot,
        )

    def staged(s, k):
        rows = pl.ds(k * BLOCK, BLOCK)
        return [
            pltpu.make_async_copy(res_ref.at[s, rows], stage_res, lsems.at[0]),
            pltpu.make_async_copy(cot_ref.at[s, rows], stage_cot, lsems.at[1]),
        ]

    def stored(ref, s, k):
        return pltpu.make_async_copy(stage_out, ref.at[s, pl.ds(k * BLOCK, BLOCK)], lsems.at[2])

    first = blocks + 1
    second = seqs * blocks + blocks

    def output_block(i):
        s = jnp.where(i < second, 0, 1)
        k = blocks - 1 - (i - jnp.where(i < second, first, second))
        n = s * blocks + k
        for copy in staged(s, k):
            copy.start()

        @pl.when(i == first)
        def _():
            relay(groups[2], True)
            settle(groups[2])
            pick(down_out, down_out_all, out_idx)
            pick(up_out, up_out_all, out_idx)
            chain_end(0, 0)

        @pl.when(i == second)
        def _():
            chain_end(0, 1)

        def middle():
            chain_tick(1, 0, among(i, {second: 1, second + 2: FINAL}), FINAL)

        def loaded():
            for copy in staged(s, k):
                copy.wait()

            @pl.when(i > first)
            def _():
                stored(out_ref, s, k).wait()

        output_step(
            heads, k == blocks - 1, middle, loaded, yb.at[n], xbc.at[n], gate.at[n], cum.at[n], sloc.at[chunk_of(n)],
            cpre.at[chunk_of(n)], csuf.at[chunk_of(n)], start.at[s], stage_res, stage_cot, stage_out, wout, down_out.at[s],
            up_out.at[s], par, dreads.at[n], rowt.at[n], gup_out.at[s], gdown_out.at[s], onehot, snow, state, run, gated,
            nout, ext, prod,
        )
        stored(out_ref, s, k).start()

        @pl.when(k == 0)
        def _():
            gown[s] = state[...].astype(BF)

        @pl.when(i == first + blocks - 1)
        def _():
            chain_start(1, 0)

    def among(i, turns):
        found = -1
        for at, tick in turns.items():
            found = jnp.where(i == at, tick, found)
        return found

    def middle_block(i, _):
        inside = (i < first) | ((i >= first + blocks) & (i < second))

        @pl.when(inside)
        def _():
            intra_block(jnp.where(i < first, i, i - blocks))

        @pl.when(jnp.logical_not(inside))
        def _():
            output_block(i)

        chain_tick(0, 0, among(i, {1: FINAL - 1, blocks: FINAL}), FINAL)
        chain_tick(0, 1, among(i, {1: 0, blocks: 1, first: 2, first + 1: 3, first + 2: FINAL}), FINAL)
        chain_tick(1, 0, among(i, {second - 1: 0, second: 2, second + 1: 3}), FINAL)
        return 0

    lax.fori_loop(0, 2 * seqs * blocks, middle_block, 0)
    stored(out_ref, seqs - 1, 0).wait()
    chain_start(1, 1)

    def rim_edge(s):
        return send(dact.at[s * blocks, pl.ds(0, RIM)], rim.at[s], earlier, hsems, 1 + s)

    period = 2 * blocks

    def back_block(i, _):
        s, r = i // period, lax.rem(i, period)

        @pl.when(r < blocks)
        def _():
            k = blocks - 1 - r
            n = s * blocks + k

            @pl.when(i == 0)
            def _():
                chain_end(1, 0)

            @pl.when(i == period)
            def _():
                chain_end(1, 1)

            def between(j):
                if j == 0:
                    chain_tick(1, 1, jnp.where(i < blocks, i, -1), FINAL)

            adjoint_step(
                heads, k == blocks - 1, between, xbc.at[n], dact.at[n], wid.at[n], cum.at[n], sig.at[n], yb.at[n], dreads.at[n],
                rowt.at[n], sloc.at[chunk_of(n)], csuf.at[chunk_of(n)], end.at[s],
                lambda t: tot[s, :, t].astype(F32) + dtot[s, 0:1, t] * start[s, :, t].astype(F32),
                par, onehot, nout.at[pl.ds(0, CHUNK)], prod, z, held,
            )

            @pl.when(k == 0)
            def _():
                for q in range(seqs):
                    @pl.when((s == q) & (seq > 0))
                    def _(q=q):
                        rim_edge(q).start()

        @pl.when(r >= blocks)
        def _():
            k = r - blocks
            n = s * blocks + k
            late_one = k == blocks - 1
            for copy in staged(s, k):
                copy.start()
            for q in range(seqs):
                @pl.when((s == q) & (k == 0) & (seq > 0))
                def _(q=q):
                    rim_edge(q).wait_send()

                @pl.when((s == q) & late_one & (seq < seq_count - 1))
                def _(q=q):
                    rim_edge(q).wait_recv()

                @pl.when((s == q) & late_one & (seq == seq_count - 1))
                def _(q=q):
                    rim[q] = jnp.zeros_like(rim[q])

            def loaded():
                for copy in staged(s, k):
                    copy.wait()

                @pl.when(i > blocks)
                def _():
                    stored(gin_ref, s, k).wait()

            def following():
                @pl.when(late_one)
                def _():
                    for m, t in enumerate(tiles(mixer)):
                        ext[m, BLOCK : BLOCK + RIM, :] = rim[s, :, t].astype(F32)

                @pl.when(jnp.logical_not(late_one))
                def _():
                    for m, t in enumerate(tiles(mixer)):
                        ext[m, BLOCK : BLOCK + RIM, :] = dact[n + 1, 0:RIM, t].astype(F32)

            input_step(
                heads, k == 0, loaded, following, dact.at[n], gate.at[n], sig.at[n], low.at[n], stage_res, stage_cot, stage_out,
                wgate, wmix, wtail, down_in.at[s], up_in.at[s], par, gup_in.at[s], gdown_in.at[s], ext, gn,
                nout.at[:, pl.ds(0, model)],
            )
            stored(gin_ref, s, k).start()
            chain_tick(1, 1, jnp.where(i < period, i, -1), FINAL)

        return 0

    lax.fori_loop(0, seqs * period, back_block, 0)
    stored(gin_ref, seqs - 1, blocks - 1).wait()


def block_call(in_index, out_index, tensors, tables, vectors, sizes, dp_count, seq_count):
    heads, inner, mixer, rank = sizes
    residual, _, in_weight, _ = tensors
    seqs, tokens, model = residual.shape
    states = (mixer - inner) // 2
    count = tokens // BLOCK * seqs
    chunks = tokens // CHUNK * seqs
    proj = in_weight.shape[1]
    lanes = -(-proj // LANES) * LANES
    adapters = tables[0].shape[0] * dp_count
    every = lambda width: pltpu.VMEM((adapters, rank, width), BF)
    rows = lambda width, kind: pltpu.VMEM((count, BLOCK, width), kind)
    state = lambda: pltpu.VMEM((seqs, states, inner), BF)
    slots = lambda: pltpu.VMEM((2, seqs, PARTS, states, inner // 2 // PARTS), BF)
    stage = lambda: pltpu.VMEM((BLOCK, model), BF)
    picked = lambda width: pltpu.VMEM((seqs, rank, width), BF)
    any_space = pl.BlockSpec(memory_space=pl.ANY)
    vmem = pl.BlockSpec(memory_space=pltpu.VMEM)
    smem = pl.BlockSpec(memory_space=pltpu.SMEM)
    return pl.pallas_call(
        functools.partial(block_kernel, dp_count, seq_count),
        out_shape=[
            jax.ShapeDtypeStruct(residual.shape, BF),
            jax.ShapeDtypeStruct(residual.shape, BF),
            jax.ShapeDtypeStruct((seqs, rank, proj), F32),
            jax.ShapeDtypeStruct((seqs, rank, model), F32),
            jax.ShapeDtypeStruct((seqs, rank, model), F32),
            jax.ShapeDtypeStruct((seqs, rank, inner), F32),
        ],
        in_specs=[smem, smem] + [any_space] * 8 + [vmem] * len(vectors),
        out_specs=[any_space] * 2 + [vmem] * 4,
        scratch_shapes=[
            rows(mixer, BF),
            rows(mixer, BF),
            rows(inner, BF),
            rows(inner, BF),
            pltpu.VMEM((chunks, states, inner), BF),
            rows(rank, BF),
            rows(LANES, F32),
            rows(LANES, F32),
            rows(LANES, F32),
            rows(LANES, F32),
            rows(states, F32),
            pltpu.VMEM((chunks, 8, LANES), F32),
            pltpu.VMEM((chunks, 8, LANES), F32),
            state(),
            pltpu.VMEM((seqs, 8, inner), F32),
            state(),
            state(),
            state(),
            slots(),
            pltpu.VMEM((2, seqs, 8, inner), F32),
            slots(),
            slots(),
            slots(),
            pltpu.VMEM((model, proj - inner), BF),
            pltpu.VMEM((model, LANES), BF),
            pltpu.VMEM((model, inner), BF),
            pltpu.VMEM((inner, model), BF),
            every(proj - inner),
            every(inner),
            every(model),
            every(model),
            every(inner),
            picked(lanes),
            picked(model),
            picked(model),
            picked(inner),
            pltpu.VMEM((16, mixer), F32),
            pltpu.VMEM((seqs, RIM, model), BF),
            pltpu.VMEM((seqs, RIM, mixer), BF),
            stage(),
            stage(),
            stage(),
            pltpu.VMEM((mixer // LANES, BLOCK + RIM, LANES), F32),
            pltpu.VMEM((states, inner), F32),
            pltpu.VMEM((BLOCK // CHUNK, states, inner), BF),
            pltpu.VMEM((BLOCK, inner), BF),
            pltpu.VMEM((BLOCK, inner), BF),
            pltpu.VMEM((CHUNK, inner), BF),
            pltpu.VMEM((8, LANES), F32),
            pltpu.VMEM((8, LANES), F32),
            pltpu.VMEM((LANES, inner), BF),
            pltpu.VMEM((CHUNK, inner), F32),
            pltpu.VMEM((BLOCK, model), F32),
            pltpu.SemaphoreType.DMA((2, 8, max(dp_count // 2, 1), 9)),
            pltpu.SemaphoreType.DMA((2, 2, seqs, 4, PARTS)),
            pltpu.SemaphoreType.DMA((2, 1 + seqs)),
            pltpu.SemaphoreType.DMA((max(count, 3),)),
        ],
        compiler_params=pltpu.CompilerParams(collective_id=1, has_side_effects=True, vmem_limit_bytes=VMEM_LIMIT),
        name="block",
    )(in_index, out_index, *tensors, *tables, *vectors)


def sums_kernel(
    count, dp_count, up_in_ref, down_in_ref, up_out_ref, down_out_ref, coef_ref,
    final,
    pack, half, half_sent, first, line, red, give, owners, sems,
):
    dp = lax.axis_index("dp")
    seq = lax.axis_index("seq")
    pair, side = seq // 2, lax.rem(seq, 2)
    pairs = count // 2
    share = red.shape[0]
    seqs, rank, _ = up_in_ref.shape
    owned = final.shape[1] // rank
    partner = (seq + 1 - 2 * side, dp)
    along = [(lax.rem(pair + k, pairs) * 2 + side, dp) for k in range(1, pairs)]
    across = [(seq, lax.rem(dp + k, dp_count)) for k in range(1, dp_count)]
    barrier = pltpu.get_barrier_semaphore()
    for other in [partner] + along + across:
        pl.semaphore_signal(barrier, inc=1, device_id=other, device_id_type=MESH)

    places = []
    for n, ref in enumerate((up_in_ref, down_in_ref, up_out_ref, down_out_ref)):
        if n == 2:
            in_tiles = len(places)
        places += [(ref, t.start, t.stop - t.start) for t in tiles(ref.shape[2])]
    for n, (ref, at, wide) in enumerate(places):
        for s in range(seqs):
            v = ref[s, :, at : at + wide]
            if wide < LANES:
                v = jnp.concatenate([v, jnp.zeros((rank, LANES - wide), F32)], axis=1)
            pack[n, s * rank : (s + 1) * rank, :] = v.astype(BF)
    for n in range(len(places), pack.shape[0]):
        pack[n] = jnp.zeros_like(pack[n])
    pl.semaphore_wait(barrier, 1 + len(along) + len(across))

    def send(src, dst, to, *at):
        return pltpu.make_async_remote_copy(
            src_ref=src, dst_ref=dst, send_sem=sems.at[(0,) + at], recv_sem=sems.at[(1,) + at],
            device_id=to, device_id_type=MESH,
        )

    wide = pairs * share
    copy = send(pack.at[pl.ds((1 - side) * wide, wide)], first, partner, 0, 0)
    copy.start()
    copy.wait()

    def add(n, _):
        v = pack[side * wide + n].astype(F32) + first[n].astype(F32)
        half[n] = v
        half_sent[n] = v.astype(BF)
        return 0

    lax.fori_loop(0, wide, add, 0)
    copies = []
    for k in range(1, pairs):
        there = lax.rem(pair + k, pairs)
        copies.append(send(half_sent.at[pl.ds(there * share, share)], line.at[k - 1], along[k - 1], 1, k))
        copies[-1].start()
    for copy in copies:
        copy.wait()
    for n in range(share):
        v = half[pair * share + n]
        for k in range(pairs - 1):
            v = v + line[k, n].astype(F32)
        red[n] = v

    def part(owner, n, a):
        tile = (side * pairs + pair) * share + n
        kind = jnp.where(tile < in_tiles, 0, 1)
        total = None
        for s in range(seqs):
            c = coef_ref[kind, (owner * owned + a) * seqs + s]
            term = c * red[n, s * rank : (s + 1) * rank, :]
            total = term if total is None else total + term
        return total

    copies = []
    for k in range(1, dp_count):
        owner = lax.rem(dp + k, dp_count)
        for n in range(share):
            for a in range(owned):
                give[k - 1, n, a * rank : (a + 1) * rank, :] = part(owner, n, a).astype(BF)
        copies.append(send(give.at[k - 1], owners.at[k - 1], across[k - 1], 2, k))
        copies[-1].start()
    mine = [[part(dp, n, a) for a in range(owned)] for n in range(share)]
    for copy in copies:
        copy.wait()
    here = pl.ds((side * pairs + pair) * share, share)
    for n in range(share):
        for a in range(owned):
            v = mine[n][a]
            for k in range(dp_count - 1):
                v = v + owners[k, n, a * rank : (a + 1) * rank, :].astype(F32)
            final[(side * pairs + pair) * share + n, a * rank : (a + 1) * rank, :] = v.astype(BF)
    copies = []
    for k in range(1, pairs):
        copies.append(send(final.at[here], final.at[here], along[k - 1], 3, k))
        copies[-1].start()
    for copy in copies:
        copy.wait()
    ours = final.at[pl.ds(side * wide, wide)]
    copy = send(ours, ours, partner, 4, 0)
    copy.start()
    copy.wait()

def unpack_kernel(final, up_in_out, down_in_out, up_out_out, down_out_out):
    owned, rank, _ = up_in_out.shape
    n = 0
    for out in (up_in_out, down_in_out, up_out_out, down_out_out):
        for t in tiles(out.shape[2]):
            for a in range(owned):
                out[a, :, t] = final[n, a * rank : (a + 1) * rank, : t.stop - t.start].astype(F32)
            n += 1


def adapter_sums(grads, coef, owned, count, dp_count):
    up_in, down_in, up_out, down_out = grads
    seqs, rank, _ = up_in.shape
    total = sum(-(-g.shape[2] // LANES) for g in grads)
    share = -(-total // count)
    pairs = count // 2
    rows = seqs * rank
    own_rows = owned * rank
    whole = pl.BlockSpec(memory_space=pltpu.VMEM)
    final = pl.pallas_call(
        functools.partial(sums_kernel, count, dp_count),
        out_shape=jax.ShapeDtypeStruct((share * count, own_rows, LANES), BF),
        in_specs=[whole] * 4 + [pl.BlockSpec(memory_space=pltpu.SMEM)],
        out_specs=whole,
        scratch_shapes=[
            pltpu.VMEM((share * count, rows, LANES), BF),
            pltpu.VMEM((share * pairs, rows, LANES), F32),
            pltpu.VMEM((share * pairs, rows, LANES), BF),
            pltpu.VMEM((share * pairs, rows, LANES), BF),
            pltpu.VMEM((max(pairs - 1, 1), share, rows, LANES), BF),
            pltpu.VMEM((share, rows, LANES), F32),
            pltpu.VMEM((max(dp_count - 1, 1), share, own_rows, LANES), BF),
            pltpu.VMEM((max(dp_count - 1, 1), share, own_rows, LANES), BF),
            pltpu.SemaphoreType.DMA((2, 5, max(pairs, dp_count))),
        ],
        compiler_params=pltpu.CompilerParams(collective_id=4, has_side_effects=True, vmem_limit_bytes=VMEM_LIMIT),
        name="adapter_sums",
    )(up_in, down_in, up_out, down_out, coef)
    return pl.pallas_call(
        unpack_kernel,
        out_shape=[jax.ShapeDtypeStruct((owned, rank, g.shape[2]), F32) for g in grads],
        in_specs=[whole],
        out_specs=[whole] * 4,
        name="unpack",
    )(final)


def on_device(
    residual_in,
    cotangent,
    norm_gain,
    in_weight,
    conv_weight,
    conv_bias,
    step_bias,
    decay_log,
    skip_gain,
    gate_gain,
    out_weight,
    in_down,
    in_up,
    out_down,
    out_up,
    in_index,
    out_index,
):
    heads = step_bias.shape[0]
    inner = gate_gain.shape[0]
    mixer = conv_weight.shape[0]
    rank = in_up.shape[1]
    seq_count = lax.axis_size("seq")
    dp_count = lax.axis_size("dp")
    adapters = in_down.shape[0] * dp_count

    block_out, grad_input, gin_up, gin_down, gout_up, gout_down = block_call(
        in_index.reshape(-1),
        out_index.reshape(-1),
        (residual_in, cotangent, in_weight, out_weight),
        (in_up, in_down.transpose(0, 2, 1), out_up, out_down.transpose(0, 2, 1)),
        (conv_weight.T, conv_bias, gate_gain, norm_gain, skip_gain, step_bias, decay_log),
        (heads, inner, mixer, rank),
        dp_count,
        seq_count,
    )
    owners = jnp.arange(adapters)[:, None]
    coef = jnp.stack([(index[:, 0][None, :] == owners).astype(F32).reshape(-1) for index in (in_index, out_index)])
    gin_up, gin_down, gout_up, gout_down = adapter_sums(
        (gin_up, gin_down, gout_up, gout_down), coef, in_down.shape[0], seq_count, dp_count
    )
    gin_down, gout_down = (g.transpose(0, 2, 1) for g in (gin_down, gout_down))
    return (block_out, grad_input, gin_down, gin_up, gout_down, gout_up)


def solution(mesh):
    rows = P("dp", "seq", None)
    split = P("dp", None, None)
    return jax.shard_map(
        on_device,
        mesh=mesh,
        in_specs=(
            rows,
            rows,
            P(),
            P("dp", None),
            P(),
            P(),
            P(),
            P(),
            P(),
            P(),
            P("dp", None),
            split,
            split,
            split,
            split,
            P("dp", None),
            P("dp", None),
        ),
        out_specs=(rows, rows, split, split, split, split),
        check_vma=False,
    )
```

```python
import functools

import jax
import jax.numpy as jnp
from jax import lax
from jax.experimental import pallas as pl
from jax.experimental.pallas import tpu as pltpu
from jax.sharding import PartitionSpec as P

EPS = 1e-05
CHUNK = 128
BLOCK = 256
BAND = 32
RIM = 16
LANES = 128
LOG2E = 1.4426950408889634
BF = jnp.bfloat16
F32 = jnp.float32
MESH = pl.DeviceIdType.MESH
VMEM_LIMIT = 62 * 2**20
PARTS = 3
FINAL = 4
CONV_BIAS, GATE_GAIN, NORM_GAIN, SKIP, STEP_BIAS, RATE = (slice(4 + n, 5 + n) for n in range(6))


def nn(a, b):
    return lax.dot_general(a, b, (((1,), (0,)), ((), ())), preferred_element_type=F32)


def nt(a, b):
    return lax.dot_general(a, b, (((1,), (1,)), ((), ())), preferred_element_type=F32)


def tn(a, b):
    return lax.dot_general(a, b, (((0,), (0,)), ((), ())), preferred_element_type=F32)


def sigmoid(v):
    return 0.5 * jnp.tanh(0.5 * v) + 0.5


def two_terms(values, heads):
    lane = lax.broadcasted_iota(jnp.int32, values.shape, 1)
    values = jnp.where(lane < heads, values, 0.0)
    high = values.astype(BF).astype(F32)
    return (high + pltpu.roll(values - high, LANES // 2, 1)).astype(BF)


def spread(values, onehot, heads):
    return nn(two_terms(values, heads), onehot)


def gather_heads(values, onehot, heads):
    sums = nt(values, onehot)
    lane = lax.broadcasted_iota(jnp.int32, sums.shape, 1)
    return jnp.where(lane < heads, sums, 0.0)


def running(ones, values, heads):
    sums = nn(ones.astype(BF), two_terms(values, heads))
    return sums + pltpu.roll(sums, LANES // 2, 1)


def head_onehot(heads, inner):
    width = inner // heads
    row = lax.broadcasted_iota(jnp.int32, (LANES, inner), 0)
    col = lax.broadcasted_iota(jnp.int32, (LANES, inner), 1)
    row = jnp.where(row < LANES // 2, row, row - LANES // 2)
    low = row * width
    return jnp.where((col >= low) & (col < low + width), 1.0, 0.0).astype(BF)


def lower_ones(length):
    row = lax.broadcasted_iota(jnp.int32, (length, length), 0)
    col = lax.broadcasted_iota(jnp.int32, (length, length), 1)
    return jnp.where(row >= col, 1.0, 0.0).astype(F32)


def upper_ones(length):
    row = lax.broadcasted_iota(jnp.int32, (length, length), 0)
    col = lax.broadcasted_iota(jnp.int32, (length, length), 1)
    return jnp.where(row <= col, 1.0, 0.0).astype(F32)


def tiles(width):
    return [slice(at, min(at + LANES, width)) for at in range(0, width, LANES)]


def rows_of(j):
    return slice(j * CHUNK, (j + 1) * CHUNK)


def bands(j):
    return [(slice(at, at + BAND), slice(j * CHUNK + at, j * CHUNK + at + BAND)) for at in range(0, CHUNK, BAND)]


def write_normed(dst, src, gain, step):
    rows = src.shape[0]

    def body(k, _):
        at = pl.ds(pl.multiple_of(k * step, step), step)
        v = src[at, :].astype(F32)
        scale = lax.rsqrt(jnp.mean(v * v, axis=1, keepdims=True) + EPS)
        dst[at, :] = (v * scale * gain).astype(BF)
        return 0

    lax.fori_loop(0, rows // step, body, 0)


def project_step(heads, first_block, normed, halo, win, wtail, down, up, par, low_ref, xbc, dact, wid, cum, sig, sloc, cpre, ext, state, run, onehot):
    rows = normed.shape[0]
    inner = onehot.shape[1]
    mixer = xbc.shape[1]
    states = (mixer - inner) // 2

    @pl.when(first_block)
    def _():
        state[...] = jnp.zeros_like(state)
        run[...] = jnp.zeros_like(run)
        v = halo[...].astype(F32)
        scale = lax.rsqrt(jnp.mean(v * v, axis=1, keepdims=True) + EPS)
        first = (v * scale * par[NORM_GAIN, : normed.shape[1]]).astype(BF)
        both = jnp.concatenate([first, nt(first, down[...]).astype(BF)], axis=1)
        for at in range(0, mixer, 2 * LANES):
            t = slice(at, at + 2 * LANES)
            v = nn(both, jnp.concatenate([win[:, t], up[:, inner + at : inner + at + 2 * LANES]], axis=0))
            ext[at // LANES, 0:RIM, :] = v[:, :LANES]
            ext[at // LANES + 1, 0:RIM, :] = v[:, LANES:]

    @pl.when(jnp.logical_not(first_block))
    def _():
        ext[:, 0:RIM, :] = ext[:, rows : rows + RIM, :]

    tokens = normed[...]
    low = nt(tokens, down[...]).astype(BF)
    low_ref[...] = low
    both = jnp.concatenate([tokens, low], axis=1)
    raw = nn(both, jnp.concatenate([wtail[...], up[:, inner + mixer :]], axis=0))
    raw = raw + par[STEP_BIAS, :LANES]
    sig[...] = sigmoid(raw)
    widths = jnp.maximum(raw, 0.0) + jnp.log1p(jnp.exp(-jnp.abs(raw)))
    wid[...] = widths
    ones = lower_ones(CHUNK)

    def convolve(n):
        t = slice(n * LANES, n * LANES + LANES)
        for start in range(0, rows, BAND):
            pre = par[CONV_BIAS, t]
            for k in range(4):
                at = RIM - 3 + k + start
                pre = pre + par[k : k + 1, t] * ext[n, at : at + BAND, :]
            s = sigmoid(pre)
            act = pre * s
            xbc[start : start + BAND, t] = act.astype(BF)
            dact[start : start + BAND, t] = (s + act * (1.0 - s)).astype(BF)

    for n in range(0, mixer // LANES + 2, 2):
        if n < mixer // LANES:
            at = n * LANES
            v = nn(both, jnp.concatenate([win[:, at : at + 2 * LANES], up[:, inner + at : inner + at + 2 * LANES]], axis=0))
            ext[n, RIM : RIM + rows, :] = v[:, :LANES]
            ext[n + 1, RIM : RIM + rows, :] = v[:, LANES:]
        if n > 0:
            convolve(n - 2)
            convolve(n - 1)
    for j in range(rows // CHUNK):
        w = widths[rows_of(j)]
        c = running(ones, w * par[RATE, :LANES], heads)
        cum[rows_of(j)] = c
        last = c[CHUNK - 1 : CHUNK]
        tail = spread(jnp.exp(last - c) * w, onehot[...], heads)
        weighted = jnp.concatenate(
            [(xbc[rows_of(j), t].astype(F32) * tail[:, t]).astype(BF) for t in tiles(inner)], axis=1
        )
        inputs_t = xbc[rows_of(j), inner : inner + states].astype(F32).T.astype(BF)
        update = nn(inputs_t, weighted)
        before = run[...]
        cpre[j] = before
        keep = spread(jnp.exp(jnp.broadcast_to(last, before.shape)), onehot[...], heads)[0:1]
        for t in tiles(inner):
            old = state[:, t]
            sloc[j, :, t] = old.astype(BF)
            state[:, t] = keep[:, t] * old + update[:, t]
        run[...] = before + last


def intra_step(heads, normed, low_ref, win, up, xbc, wid, cum, gate, y, onehot):
    inner = onehot.shape[1]
    states = (xbc.shape[1] - inner) // 2
    width = inner // heads
    per = LANES // width
    both = jnp.concatenate([normed[...], low_ref[...]], axis=1)
    lane = lax.broadcasted_iota(jnp.int32, (CHUNK, LANES), 1)
    mask = lower_ones(CHUNK)
    ready = []
    for j in range(xbc.shape[0] // CHUNK):
        c = cum[rows_of(j)] * LOG2E
        wide = spread(wid[rows_of(j)], onehot[...], heads)
        inputs = xbc[rows_of(j), inner : inner + states]
        reads = xbc[rows_of(j), inner + states :]
        ready.append((c, c.T, wide, nt(reads, inputs) * mask))
    columns = tiles(inner)
    order = list(range(normed.shape[1] // LANES, len(columns))) + list(range(normed.shape[1] // LANES))
    for n, k in enumerate(order):
        t = columns[k]
        if n < inner // (2 * LANES):
            g = slice(n * 2 * LANES, (n + 1) * 2 * LANES)
            gate[:, g] = nn(both, jnp.concatenate([win[:, g], up[:, g]], axis=0)).astype(BF)
        for j, (c, c_rows, wide, scores) in enumerate(ready):
            weighted = xbc[rows_of(j), t].astype(F32) * wide[:, t]
            mixing, parts = [], []
            for p in range(per):
                h = k * per + p
                kernel = jnp.exp2(jnp.minimum(c[:, h : h + 1] - c_rows[h : h + 1, :], 0.0))
                mixing.append((kernel * scores).astype(BF))
                inside = (lane >= p * width) & (lane < (p + 1) * width)
                parts.append(jnp.where(inside, weighted, 0.0).astype(BF))
            y[rows_of(j), t] = nn(jnp.concatenate(mixing, axis=1), jnp.concatenate(parts, axis=0)).astype(BF)


def output_step(
    heads, first_block, middle, loaded, y, xbc, gate, cum, sloc, cpre, csuf, start, res, cot, out, wout, down, up, par,
    dreads, rowt, gup, gdown, onehot, snow, adj, run, gated, nout, gno, prod,
):
    rows = res.shape[0]
    inner = onehot.shape[1]
    states = (xbc.shape[1] - inner) // 2
    chunks = rows // CHUNK

    @pl.when(first_block)
    def _():
        adj[...] = jnp.zeros_like(adj)
        run[...] = jnp.zeros_like(run)
        gup[...] = jnp.zeros_like(gup)
        gdown[...] = jnp.zeros_like(gdown)

    reach, scale = [], []
    for j in range(chunks):
        since = spread(jnp.exp(cpre[j]), onehot[...], heads)
        for t in tiles(inner):
            snow[j, :, t] = (sloc[j, :, t].astype(F32) + since[0:1, t] * start[:, t].astype(F32)).astype(BF)
        carried = nn(xbc[rows_of(j), inner + states :], snow[j])
        grow = spread(jnp.exp(cum[rows_of(j)]), onehot[...], heads)
        reach.append(grow)
        for here, at in bands(j):
            total = jnp.zeros((BAND, LANES), F32)
            for t in tiles(inner):
                local = y[at, t].astype(F32) + grow[here, t] * carried[here, t]
                y[at, t] = local.astype(BF)
                g = gate[at, t].astype(F32)
                v = (local + par[SKIP, t] * xbc[at, t].astype(F32)) * (g * sigmoid(g))
                gated[at, t] = v.astype(BF)
                total = total + v * v
            r = lax.rsqrt(jnp.sum(total, axis=1, keepdims=True) * (1.0 / inner) + EPS)
            scale.append(r)
            for t in tiles(inner):
                nout[at, t] = (gated[at, t].astype(F32) * r * par[GATE_GAIN, t]).astype(BF)

    middle()
    loaded()
    normed_out = nout[...]
    cot_rows = cot[...]
    low_out = nt(normed_out, down[...]).astype(BF)
    both = jnp.concatenate([normed_out, low_out], axis=1)
    for at in range(0, out.shape[1], 2 * LANES):
        t = slice(at, at + 2 * LANES)
        part = nn(both, jnp.concatenate([wout[:, t], up[:, t]], axis=0))
        out[:, t] = (res[:, t].astype(F32) + part).astype(BF)
    grad_low = nt(cot_rows, up[...]).astype(BF)
    for at in range(0, inner, 2 * LANES):
        t = slice(at, at + 2 * LANES)
        v = nt(cot_rows, wout[t, :]) + nn(grad_low, down[:, t])
        gno[at // LANES, 0:rows, :] = v[:, :LANES]
        gno[at // LANES + 1, 0:rows, :] = v[:, LANES:]
    gup[...] += tn(low_out, cot_rows)
    gdown[...] += tn(grad_low, normed_out)

    for j in reversed(range(chunks)):
        pieces = []
        for m, (here, at) in enumerate(bands(j)):
            total = jnp.zeros((BAND, LANES), F32)
            for n, t in enumerate(tiles(inner)):
                q = gno[n, at, :] * par[GATE_GAIN, t]
                total = total + gated[at, t].astype(F32) * q
            r = scale[j * (CHUNK // BAND) + m]
            shrink = jnp.sum(total, axis=1, keepdims=True) * (1.0 / inner) * (r * r * r)
            scaled = []
            for n, t in enumerate(tiles(inner)):
                q = gno[n, at, :] * par[GATE_GAIN, t]
                grad = r * q - gated[at, t].astype(F32) * shrink
                local = y[at, t].astype(F32)
                g = gate[at, t].astype(F32)
                s = sigmoid(g)
                dy = grad * (g * s)
                y[at, t] = dy.astype(BF)
                full = local + par[SKIP, t] * xbc[at, t].astype(F32)
                gate[at, t] = (grad * full * (s * (1.0 + g * (1.0 - s)))).astype(BF)
                prod[here, t] = (dy * local).astype(BF)
                scaled.append((dy * reach[j][here, t]).astype(BF))
            pieces.append(jnp.concatenate(scaled, axis=1))
        rowt[rows_of(j)] = gather_heads(prod[...], onehot[...], heads)
        scaled = jnp.concatenate(pieces, axis=0)
        reads_t = xbc[rows_of(j), inner + states :].astype(F32).T.astype(BF)
        update = nn(reads_t, scaled)
        dreads[rows_of(j)] = nt(scaled, snow[j])
        last = cum[j * CHUNK + CHUNK - 1 : j * CHUNK + CHUNK]
        before = run[...]
        csuf[j] = before
        keep = reach[j][CHUNK - 1 : CHUNK]
        for t in tiles(inner):
            old = adj[:, t]
            sloc[j, :, t] = old.astype(BF)
            adj[:, t] = keep[:, t] * old + update[:, t]
        run[...] = before + last


def adjoint_step(heads, first_block, between, xbc, dact, wid, cum, sig, dy, dreads, rowt, gloc, csuf, end, final, par, onehot, adj, prod, z, held):
    inner = onehot.shape[1]
    states = (xbc.shape[1] - inner) // 2
    width = inner // heads
    per = LANES // width
    mask = upper_ones(CHUNK)
    lane = lax.broadcasted_iota(jnp.int32, (CHUNK, LANES), 1)

    @pl.when(first_block)
    def _():
        overlap = []
        for t in tiles(inner):
            overlap.append(jnp.sum(end[:, t].astype(F32) * final(t), axis=0, keepdims=True))
        v = jnp.broadcast_to(jnp.concatenate(overlap, axis=1), (8, inner))
        high = v.astype(BF)
        rest = (v - high.astype(F32)).astype(BF)
        held[...] = gather_heads(high, onehot[...], heads) + gather_heads(rest, onehot[...], heads)

    for j in reversed(range(xbc.shape[0] // CHUNK)):
        at = rows_of(j)
        c = cum[at]
        w = wid[at]
        c_two = c * LOG2E
        c_rows = c_two.T
        wide = spread(w, onehot[...], heads)
        inputs = xbc[at, inner : inner + states]
        reads = xbc[at, inner + states :]
        scores_t = nt(inputs, reads) * mask
        total = jnp.zeros((CHUNK, CHUNK), F32)
        for k, t in enumerate(tiles(inner)):
            weighted = (xbc[at, t].astype(F32) * wide[:, t]).astype(BF)
            grads = dy[at, t].astype(F32)
            mixing, right = [], []
            for p in range(per):
                inside = (lane >= p * width) & (lane < (p + 1) * width)
                right.append(jnp.where(inside, grads, 0.0).astype(BF))
            right = jnp.concatenate(right, axis=0)
            products = nt(weighted, right)
            for p in range(per):
                h = k * per + p
                kernel = jnp.exp2(jnp.minimum(c_rows[h : h + 1, :] - c_two[:, h : h + 1], 0.0))
                mixing.append((kernel * scores_t).astype(BF))
                total = total + kernel * products[:, p * CHUNK : (p + 1) * CHUNK]
            z[:, t] = nn(jnp.concatenate(mixing, axis=1), right)
        total = total * mask
        dinputs = nn(total.astype(BF), reads)
        dreads_all = dreads[at] + nn(total.T.astype(BF), inputs)

        since = spread(jnp.exp(csuf[j]), onehot[...], heads)
        for t in tiles(inner):
            adj[:, t] = (gloc[j, :, t].astype(F32) + since[0:1, t] * end[:, t].astype(F32)).astype(BF)
        last = c[CHUNK - 1 : CHUNK]
        tail = spread(jnp.exp(last - c), onehot[...], heads)
        carried = nn(inputs, adj[...])
        weighted = []
        for t in tiles(inner):
            x = xbc[at, t].astype(F32)
            v = z[:, t] + tail[:, t] * carried[:, t]
            prod[:, t] = (x * v).astype(BF)
            grad = wide[:, t] * v + par[SKIP, t] * dy[at, t].astype(F32)
            dact[at, t] = (grad * dact[at, t].astype(F32)).astype(BF)
            weighted.append((x * (wide[:, t] * tail[:, t])).astype(BF))
        dinputs = dinputs + nt(jnp.concatenate(weighted, axis=1), adj[...])
        t = slice(inner, inner + states)
        dact[at, t] = (dinputs * dact[at, t].astype(F32)).astype(BF)
        t = slice(inner + states, inner + 2 * states)
        dact[at, t] = (dreads_all * dact[at, t].astype(F32)).astype(BF)
        direct = gather_heads(prod[...], onehot[...], heads)
        grad_rate = held[0:1] + running(mask, rowt[at] - w * direct, heads)
        held[...] = jnp.broadcast_to(grad_rate[0:1], held.shape)
        sig[at] = (direct + par[RATE, :LANES] * grad_rate) * sig[at]
        between(j)


def input_step(heads, first_block, loaded, following, gpre, ggate, graw, low_ref, res, cot, gin, wgate, win, wtail, down, up, par, gup, gdown, ext, gn, nrm):
    rows = res.shape[0]
    inner = ggate.shape[1]
    mixer = gpre.shape[1]
    proj = inner + mixer + heads
    model = res.shape[1]
    gain = par[NORM_GAIN, :model]

    @pl.when(first_block)
    def _():
        gup[...] = jnp.zeros_like(gup)
        gdown[...] = jnp.zeros_like(gdown)

    for n, t in enumerate(tiles(mixer)):
        for j in range(rows // CHUNK):
            ext[n, rows_of(j), :] = gpre[rows_of(j), t].astype(F32)
    following()
    for n, t in enumerate(tiles(mixer)):
        for start in range(0, rows, BAND):
            total = None
            for k in range(4):
                at = 3 - k + start
                term = par[k : k + 1, t] * ext[n, at : at + BAND, :]
                total = term if total is None else total + term
            gpre[start : start + BAND, t] = total.astype(BF)
    grads_gate, grads_mix = ggate[...], jnp.concatenate([gpre[...], graw[...].astype(BF)], axis=1)
    grad_low = (nt(grads_gate, up[:, :inner]) + nt(grads_mix, up[:, inner:])).astype(BF)
    for at in range(0, model, 2 * LANES):
        t = slice(at, at + 2 * LANES)
        mix = jnp.concatenate([win[t, :mixer], wtail[t, :]], axis=1)
        gn[:, t] = nt(grads_gate, wgate[t, :]) + nt(grads_mix, mix) + nn(grad_low, down[:, t])
    loaded()

    def body(k, _):
        at = pl.ds(pl.multiple_of(k * 32, 32), 32)
        v = res[at, :].astype(F32)
        u = lax.rsqrt(jnp.mean(v * v, axis=1, keepdims=True) + EPS)
        nrm[at, :] = (v * u * gain).astype(BF)
        w = gn[at, :] * gain
        m = jnp.mean(v * w, axis=1, keepdims=True)
        gin[at, :] = (cot[at, :].astype(F32) + u * w - v * (u * u * u * m)).astype(BF)
        return 0

    lax.fori_loop(0, rows // 32, body, 0)
    low = low_ref[...]
    gup[:, :inner] += tn(low, grads_gate)
    gup[:, inner:] += tn(low, grads_mix)[:, : proj - inner]
    gdown[...] += tn(grad_low, nrm[...])


def block_kernel(
    dp_count, seq_count,
    in_idx, out_idx, coef_ref, res_ref, cot_ref, win_ref, wout_ref, up_in_ref, down_in_ref, up_out_ref, down_out_ref,
    taps_ref, conv_bias_ref, gate_gain_ref, norm_gain_ref, skip_ref, step_bias_ref, decay_ref,
    out_ref, gin_ref, sums_ref,
    xbc, dact, gate, yb, sloc, low, wid, cum, sig, rowt, dreads, cpre, csuf, tot, dtot, start, gown, end,
    theirs, theirs_dec, prefix, passed, tail, wmix, wtail, wgate, wout, up_mix_all, up_gate_all, down_in_all, up_out_all, down_out_all,
    up_in, down_in, up_out, down_out, par,
    halo, rim, stage_res, stage_cot, stage_out, ext, state, snow, gated, nout, prod, run, held, onehot, z, gn,
    gup_in, gdown_in, gup_out, gdown_out, pack, first_half, half_sum, half_sent, line, red, give, owners,
    wsems, csems, hsems, lsems, rsems,
):
    dp = lax.axis_index("dp")
    seq = lax.axis_index("seq")
    seqs, tokens, model = res_ref.shape
    blocks = tokens // BLOCK
    per = BLOCK // CHUNK
    heads = step_bias_ref.shape[0]
    inner = onehot.shape[1]
    mixer = xbc.shape[2]
    proj = win_ref.shape[1]
    pairs = seq_count // 2
    side = lax.rem(seq, 2)
    pair = seq // 2
    chips = dp_count // 2
    partner = (seq + 1 - 2 * side, dp)
    sibling = (seq, dp + 1 - 2 * lax.rem(dp, 2))
    later = (lax.rem(seq + 1, seq_count), dp)
    earlier = (lax.rem(seq + seq_count - 1, seq_count), dp)
    upper = (lax.rem(pair + 1, pairs) * 2 + side, dp)
    lower = (lax.rem(pair + pairs - 1, pairs) * 2 + side, dp)
    others = [(seq, lax.rem(dp + 2 * k, dp_count)) for k in range(1, chips)]
    barrier = pltpu.get_barrier_semaphore()
    along = [(lax.rem(pair + k, pairs) * 2 + side, dp) for k in range(1, pairs)]
    across = [(seq, lax.rem(dp + k, dp_count)) for k in range(1, dp_count)]
    for other in [partner] + along + across:
        pl.semaphore_signal(barrier, inc=1, device_id=other, device_id_type=MESH)
    greeted = pairs + dp_count - 1
    for other, there in ((later, seq < seq_count - 1), (earlier, seq > 0)):
        greeted = greeted + jnp.where(there, 1, 0)

        @pl.when(there)
        def _(other=other):
            pl.semaphore_signal(barrier, inc=1, device_id=other, device_id_type=MESH)

    def load(n):
        s, k = n // blocks, lax.rem(n, blocks) if not isinstance(n, int) else n % blocks
        rows = pl.ds(k * BLOCK, BLOCK)
        return pltpu.make_async_copy(res_ref.at[s, rows], yb.at[n, :, pl.ds(model, model)], lsems.at[n])

    for n in range(seqs * blocks):
        load(n).start()
    onehot[...] = head_onehot(heads, inner)
    par[...] = jnp.zeros_like(par)
    par[0:4] = taps_ref[...]
    par[CONV_BIAS] = conv_bias_ref[...][None, :]
    par[GATE_GAIN, :inner] = gate_gain_ref[...][None, :]
    par[NORM_GAIN, :model] = norm_gain_ref[...][None, :]
    par[STEP_BIAS, :heads] = step_bias_ref[...][None, :]
    par[RATE, :heads] = -jnp.exp(decay_ref[...][None, :])
    par[SKIP, :heads] = skip_ref[...][None, :]
    v = jnp.broadcast_to(par[SKIP, :LANES], (8, LANES))
    par[SKIP, :inner] = spread(v, onehot[...], heads)[0:1]
    wtail[...] = jnp.zeros_like(wtail)
    up_in[:, :, inner + mixer :] = jnp.zeros(up_in.shape[:2] + (LANES,), BF)
    pl.semaphore_wait(barrier, greeted)

    def send(src, dst, to, sems, *at):
        return pltpu.make_async_remote_copy(
            src_ref=src, dst_ref=dst, send_sem=sems.at[(0,) + at], recv_sem=sems.at[(1,) + at],
            device_id=to, device_id_type=MESH,
        )

    def rows_piece(ref, out, at, to, wide, n):
        share = ref.shape[0]
        half = share // 2

        def source(which):
            return ref.at[pl.ds(pl.multiple_of(which * half, 16), half), pl.ds(at, wide)]

        def target(owner, which):
            return out.at[pl.ds(pl.multiple_of(owner * share + which * half, 16), half), pl.ds(to, wide)]

        return source, target, n

    def table_piece(ref, out, at, wide, n):
        owned = ref.shape[0]
        return (lambda _: ref.at[:, :, pl.ds(at, wide)]), (lambda owner, _: out.at[pl.ds(owner * owned, owned)]), n, None, 0

    width = proj - inner
    split = mixer // 2 // LANES * LANES
    odd = lax.rem(pair, 2)
    across_y = (partner, side)
    across_z = (((pair + 1 - 2 * odd) * 2 + side, dp), odd)
    groups = [
        [
            (*rows_piece(win_ref, wmix, inner, 0, split, 0), *across_y),
            (*rows_piece(win_ref, wmix, inner + split, split, width - split, 1), *across_y),
            table_piece(down_in_ref, down_in_all, 0, model, 2),
            table_piece(up_in_ref, up_mix_all, inner, width, 3),
        ],
        [
            table_piece(up_in_ref, up_gate_all, 0, inner, 4),
            (*rows_piece(win_ref, wgate, 0, 0, inner, 5), *across_z),
        ],
        [
            (*rows_piece(wout_ref, wout, 0, 0, wout_ref.shape[1], 6), *across_z),
            table_piece(down_out_ref, down_out_all, 0, inner, 7),
            table_piece(up_out_ref, up_out_all, 0, model, 8),
        ],
    ]

    def shards(k):
        return lax.rem(dp - 2 * k + dp_count, dp_count)

    def over_x(group):
        return [
            send(source(mine), target(dp, mine), others[k - 1], wsems, 0, k, n)
            for source, target, n, _, mine in group
            for k in range(1, chips)
        ]

    def own(group):
        copies = []
        for source, target, n, mate, _ in group:
            for which in range(1 if mate is None else 2):
                copies.append(pltpu.make_async_copy(source(which), target(dp, which), wsems.at[0, 6 + which, 0, n]))
                copies.append(send(source(which), target(dp, which), sibling, wsems, 3 + which, 0, n))
        return copies

    def forward(group, start_it):
        for source, target, n, mate, mine in group:
            for k in range(1, chips):
                here = target(shards(k), mine)
                if start_it:
                    send(source(mine), here, others[k - 1], wsems, 0, k, n).wait_recv()
                copies = [send(here, here, sibling, wsems, 2, k, n)]
                if mate is not None:
                    copies.append(send(here, here, mate, wsems, 1, k, n))
                if start_it:
                    for copy in copies:
                        copy.start()
                else:
                    copies[0].wait()
                    if mate is not None:
                        copies[1].wait_send()

    def relay(group, start_it):
        for source, target, n, mate, mine in group:
            if mate is None:
                continue
            for k in range(1, chips):
                there = target(shards(k), 1 - mine)
                if start_it:
                    send(there, there, mate, wsems, 1, k, n).wait_recv()
                over = send(there, there, sibling, wsems, 5, k, n)
                if start_it:
                    over.start()
                else:
                    over.wait()

    def settle(group):
        for copy in over_x(group):
            copy.wait_send()
        for copy in own(group):
            copy.wait()
        forward(group, False)
        relay(group, False)

    edge = send(res_ref.at[:, pl.ds(tokens - RIM, RIM)], halo, later, hsems, 0)
    for copy in over_x(groups[0]):
        copy.start()

    @pl.when(seq < seq_count - 1)
    def _():
        edge.start()

    for copy in own(groups[0]):
        copy.start()
    gain = par[NORM_GAIN, :model]

    def norm_block(n, _):
        load(n).wait()
        write_normed(yb.at[n, :, pl.ds(0, model)], yb.at[n, :, pl.ds(model, model)], gain, 32)
        return 0

    lax.fori_loop(0, seqs * blocks, norm_block, 0)
    forward(groups[0], True)
    for group in groups[1:]:
        for copy in over_x(group):
            copy.start()
    relay(groups[0], True)

    @pl.when(seq == 0)
    def _():
        halo[...] = jnp.zeros_like(halo)

    @pl.when(seq > 0)
    def _():
        edge.wait_recv()

    @pl.when(seq < seq_count - 1)
    def _():
        edge.wait_send()

    settle(groups[0])
    for group in groups[1:]:
        for copy in own(group):
            copy.start()

    def pick(dst, table, idx_ref, at=0):
        for q in range(seqs):
            dst[q, :, at : at + table.shape[2]] = table[idx_ref[q]]

    pick(down_in, down_in_all, in_idx)
    pick(up_in, up_mix_all, in_idx, inner)
    wtail[:, :heads] = wmix[:, mixer:]

    half = inner // 2
    wide = half // PARTS

    def cols(base, q):
        return pl.ds(pl.multiple_of(base * half + q * wide, LANES), wide)

    def chain(d, s):
        my_pair = pairs - 1 - pair if d else pair
        my_side = 1 - side if d else side
        ahead = lower if d else upper
        total, result = (gown, end) if d else (tot, start)

        def decs():
            return send(dtot.at[s], theirs_dec.at[d, s], partner, csems, d, s, 3, 0)

        def swap(q):
            return send(total.at[s, :, cols(1 - my_side, q)], theirs.at[d, s, q], partner, csems, d, s, 0, q)

        def hop(q):
            return send(passed.at[d, s, q], prefix.at[d, s, q], ahead, csems, d, s, 1, q)

        def give(q):
            return send(tail.at[d, s, q], result.at[s, :, cols(my_side, q)], partner, csems, d, s, 2, q)

        return my_pair, my_side, total, result, decs, swap, hop, give

    def chain_start(d, s):
        _, _, _, _, decs, swap, _, _ = chain(d, s)
        decs().start()
        for q in range(PARTS):
            swap(q).start()

    def chain_tick(d, s, tick, final):
        my_pair, my_side, total, result, decs, swap, hop, give = chain(d, s)
        for q in range(PARTS):
            turn = jnp.minimum(my_pair + (1 if q else 0), final)

            @pl.when(tick == turn)
            def _(q=q):
                if q == 0:
                    decs().wait_recv()
                swap(q).wait_recv()

                @pl.when(my_pair == 0)
                def _():
                    prefix[d, s, q] = jnp.zeros_like(prefix[d, s, q])

                @pl.when(my_pair > 0)
                def _():
                    hop(q).wait_recv()

                own_dec = dtot[s, 0:1, cols(my_side, q)]
                their_dec = theirs_dec[d, s, 0:1, cols(my_side, q)]
                own_total = total[s, :, cols(my_side, q)].astype(F32)
                other = theirs[d, s, q].astype(F32)
                before = prefix[d, s, q].astype(F32)
                left = my_side == 0
                first = jnp.where(left, own_total, other)
                second = jnp.where(left, other, own_total)
                first_dec = jnp.where(left, own_dec, their_dec)
                second_dec = jnp.where(left, their_dec, own_dec)
                middle = first_dec * before + first
                passed[d, s, q] = (second_dec * middle + second).astype(BF)

                @pl.when(my_pair < pairs - 1)
                def _():
                    hop(q).start()

                result[s, :, cols(my_side, q)] = jnp.where(left, before, middle).astype(BF)
                tail[d, s, q] = jnp.where(left, middle, before).astype(BF)
                give(q).start()

    def chain_end(d, s):
        my_pair, _, _, _, decs, swap, hop, give = chain(d, s)
        decs().wait_send()
        for q in range(PARTS):
            give(q).wait()
            swap(q).wait_send()

            @pl.when(my_pair < pairs - 1)
            def _(q=q):
                hop(q).wait_send()

    rank = gup_in.shape[1]
    owned = up_in_ref.shape[0]

    def reduction(number, parts):
        counts = [sum(-(-g.shape[2] // LANES) for g in pair_of) for pair_of in ((gup_out, gdown_out), (gup_in, gdown_in))]
        shares = [-(-n // seq_count) for n in counts]
        share = shares[number]
        wide = pairs * share
        before = sum(shares[:number])
        base, middle, small = before * seq_count, before * pairs, pl.ds(before, share)
        place = pl.ds(base + (side * pairs + pair) * share, share)

        def swap():
            theirs_of = pack.at[pl.ds(base + (1 - side) * wide, wide)]
            return send(theirs_of, first_half.at[pl.ds(middle, wide)], partner, rsems, number, 0, 0)

        def along_line(k):
            there = lax.rem(pair + k, pairs)
            mine = half_sent.at[pl.ds(middle + there * share, share)]
            return send(mine, line.at[k - 1, small], along[k - 1], rsems, number, 1, k)

        def to_owner(k):
            return send(give.at[k - 1, small], owners.at[k - 1, small], across[k - 1], rsems, number, 2, k)

        def back_along(k):
            return send(sums_ref.at[place], sums_ref.at[place], along[k - 1], rsems, number, 3, k)

        def back_across():
            ours = sums_ref.at[pl.ds(base + side * wide, wide)]
            return send(ours, ours, partner, rsems, number, 4, 0)

        def part(owner, n, a):
            total = None
            for q in range(seqs):
                c = coef_ref[1 - number, (owner * owned + a) * seqs + q]
                term = c * red[before + n, q * rank : (q + 1) * rank, :]
                total = term if total is None else total + term
            return total

        def start():
            n = base
            for ref in parts:
                for t in tiles(ref.shape[2]):
                    for q in range(seqs):
                        v = ref[q, :, t]
                        if t.stop - t.start < LANES:
                            v = jnp.concatenate([v, jnp.zeros((rank, LANES - t.stop + t.start), F32)], axis=1)
                        pack[n, q * rank : (q + 1) * rank, :] = v.astype(BF)
                    n += 1
            for m in range(n, base + share * seq_count):
                pack[m] = jnp.zeros_like(pack[m])
            swap().start()

        def second():
            swap().wait()

            def add(n, _):
                v = pack[base + side * wide + n].astype(F32) + first_half[middle + n].astype(F32)
                half_sum[n] = v
                half_sent[middle + n] = v.astype(BF)
                return 0

            lax.fori_loop(0, wide, add, 0)
            for k in range(1, pairs):
                along_line(k).start()

        def third():
            for k in range(1, pairs):
                along_line(k).wait()
            for n in range(share):
                v = half_sum[pair * share + n]
                for k in range(pairs - 1):
                    v = v + line[k, before + n].astype(F32)
                red[before + n] = v
            for k in range(1, dp_count):
                owner = lax.rem(dp + k, dp_count)
                for n in range(share):
                    for a in range(owned):
                        give[k - 1, before + n, a * rank : (a + 1) * rank, :] = part(owner, n, a).astype(BF)
                to_owner(k).start()

        def fourth():
            for k in range(1, dp_count):
                to_owner(k).wait()
            for n in range(share):
                for a in range(owned):
                    v = part(dp, n, a)
                    for k in range(dp_count - 1):
                        v = v + owners[k, before + n, a * rank : (a + 1) * rank, :].astype(F32)
                    sums_ref[base + (side * pairs + pair) * share + n, a * rank : (a + 1) * rank, :] = v.astype(BF)
            for k in range(1, pairs):
                back_along(k).start()

        def fifth():
            for k in range(1, pairs):
                back_along(k).wait()
            back_across().start()

        def finish():
            back_across().wait()

        return [start, second, third, fourth, fifth, finish]

    def chunk_of(n):
        return pl.ds(n * per, per)

    def project_block(n, _):
        s, k = n // blocks, lax.rem(n, blocks)
        project_step(
            heads, k == 0, yb.at[n, :, pl.ds(0, model)], halo.at[s], wmix, wtail, down_in.at[s], up_in.at[s], par, low.at[n],
            xbc.at[n], dact.at[n], wid.at[n], cum.at[n], sig.at[n], sloc.at[chunk_of(n)], cpre.at[chunk_of(n)],
            ext, state, run, onehot,
        )

        @pl.when(k == blocks - 1)
        def _():
            tot[s] = state[...].astype(BF)
            dtot[s] = spread(jnp.exp(run[...]), onehot[...], heads)

        @pl.when(n == blocks - 2)
        def _():
            forward(groups[1], True)

        @pl.when(n == blocks - 1)
        def _():
            forward(groups[2], True)
            chain_start(0, 0)

        @pl.when(n >= blocks)
        def _():
            chain_tick(0, 0, n - blocks, FINAL)

        return 0

    lax.fori_loop(0, seqs * blocks, project_block, 0)
    chain_start(0, 1)
    relay(groups[1], True)
    settle(groups[1])
    pick(up_in, up_gate_all, in_idx)

    def intra_block(n):
        s = n // blocks
        intra_step(
            heads, yb.at[n, :, pl.ds(0, model)], low.at[n], wgate, up_in.at[s], xbc.at[n], wid.at[n], cum.at[n], gate.at[n],
            yb.at[n], onehot,
        )

    def staged(s, k, slot):
        rows = pl.ds(k * BLOCK, BLOCK)
        return [
            pltpu.make_async_copy(res_ref.at[s, rows], stage_res.at[slot], lsems.at[slot]),
            pltpu.make_async_copy(cot_ref.at[s, rows], stage_cot.at[slot], lsems.at[2 + slot]),
        ]

    def stored(ref, s, k):
        return pltpu.make_async_copy(stage_out, ref.at[s, pl.ds(k * BLOCK, BLOCK)], lsems.at[4])

    def stage(n, backwards):
        s, k = n // blocks, lax.rem(n, blocks)
        return staged(s, blocks - 1 - k if backwards else k, lax.rem(n, 2))

    first = blocks + 1
    second = seqs * blocks + blocks

    def output_block(i):
        s = jnp.where(i < second, 0, 1)
        k = blocks - 1 - (i - jnp.where(i < second, first, second))
        n = s * blocks + k
        turn = s * blocks + blocks - 1 - k
        slot = lax.rem(turn, 2)

        @pl.when(i == first)
        def _():
            relay(groups[2], True)
            settle(groups[2])
            pick(down_out, down_out_all, out_idx)
            pick(up_out, up_out_all, out_idx)
            chain_end(0, 0)

        @pl.when(i == second)
        def _():
            chain_end(0, 1)

        def middle():
            chain_tick(1, 0, among(i, {second: 1, second + 2: FINAL}), FINAL)

        def loaded():
            for copy in stage(turn, True):
                copy.wait()

            @pl.when(turn < seqs * blocks - 1)
            def _():
                for copy in stage(turn + 1, True):
                    copy.start()

            @pl.when(i > first)
            def _():
                stored(out_ref, s, k).wait()

        output_step(
            heads, k == blocks - 1, middle, loaded, yb.at[n], xbc.at[n], gate.at[n], cum.at[n], sloc.at[chunk_of(n)],
            cpre.at[chunk_of(n)], csuf.at[chunk_of(n)], start.at[s], stage_res.at[slot], stage_cot.at[slot], stage_out, wout, down_out.at[s],
            up_out.at[s], par, dreads.at[n], rowt.at[n], gup_out.at[s], gdown_out.at[s], onehot, snow, state, run, gated,
            nout, ext, prod,
        )
        stored(out_ref, s, k).start()

        @pl.when(k == 0)
        def _():
            gown[s] = state[...].astype(BF)

        @pl.when(i == first + blocks - 1)
        def _():
            chain_start(1, 0)

    def among(i, turns):
        found = -1
        for at, tick in turns.items():
            found = jnp.where(i == at, tick, found)
        return found

    def middle_block(i, _):
        inside = (i < first) | ((i >= first + blocks) & (i < second))

        @pl.when(inside)
        def _():
            intra_block(jnp.where(i < first, i, i - blocks))

        @pl.when(jnp.logical_not(inside))
        def _():
            output_block(i)

        chain_tick(0, 0, among(i, {1: FINAL - 1, blocks: FINAL}), FINAL)
        chain_tick(0, 1, among(i, {1: 0, blocks: 1, first: 2, first + 1: 3, first + 2: FINAL}), FINAL)
        chain_tick(1, 0, among(i, {second - 1: 0, second: 2, second + 1: 3}), FINAL)
        return 0

    for copy in stage(0, True):
        copy.start()
    lax.fori_loop(0, 2 * seqs * blocks, middle_block, 0)
    stored(out_ref, seqs - 1, 0).wait()
    chain_start(1, 1)

    def rim_edge(s):
        return send(dact.at[s * blocks, pl.ds(0, RIM)], rim.at[s], earlier, hsems, 1 + s)

    period = 2 * blocks

    def back_block(i, _):
        s, r = i // period, lax.rem(i, period)

        @pl.when(r < blocks)
        def _():
            k = blocks - 1 - r
            n = s * blocks + k

            @pl.when(i == 0)
            def _():
                chain_end(1, 0)

            @pl.when(i == period)
            def _():
                chain_end(1, 1)

            def between(j):
                if j == 0:
                    chain_tick(1, 1, jnp.where(i < blocks, i, -1), FINAL)

            adjoint_step(
                heads, k == blocks - 1, between, xbc.at[n], dact.at[n], wid.at[n], cum.at[n], sig.at[n], yb.at[n], dreads.at[n],
                rowt.at[n], sloc.at[chunk_of(n)], csuf.at[chunk_of(n)], end.at[s],
                lambda t: tot[s, :, t].astype(F32) + dtot[s, 0:1, t] * start[s, :, t].astype(F32),
                par, onehot, nout.at[pl.ds(0, CHUNK)], prod, z, held,
            )

            @pl.when(k == 0)
            def _():
                for q in range(seqs):
                    @pl.when((s == q) & (seq > 0))
                    def _(q=q):
                        rim_edge(q).start()

        @pl.when(r >= blocks)
        def _():
            k = r - blocks
            n = s * blocks + k
            late_one = k == blocks - 1
            slot = lax.rem(n, 2)
            for q in range(seqs):
                @pl.when((s == q) & (k == 0) & (seq > 0))
                def _(q=q):
                    rim_edge(q).wait_send()

                @pl.when((s == q) & late_one & (seq < seq_count - 1))
                def _(q=q):
                    rim_edge(q).wait_recv()

                @pl.when((s == q) & late_one & (seq == seq_count - 1))
                def _(q=q):
                    rim[q] = jnp.zeros_like(rim[q])

            def loaded():
                for copy in stage(n, False):
                    copy.wait()

                @pl.when(n < seqs * blocks - 1)
                def _():
                    for copy in stage(n + 1, False):
                        copy.start()

                @pl.when(i > blocks)
                def _():
                    stored(gin_ref, s, k).wait()

            def following():
                @pl.when(late_one)
                def _():
                    for m, t in enumerate(tiles(mixer)):
                        ext[m, BLOCK : BLOCK + RIM, :] = rim[s, :, t].astype(F32)

                @pl.when(jnp.logical_not(late_one))
                def _():
                    for m, t in enumerate(tiles(mixer)):
                        ext[m, BLOCK : BLOCK + RIM, :] = dact[n + 1, 0:RIM, t].astype(F32)

            input_step(
                heads, k == 0, loaded, following, dact.at[n], gate.at[n], sig.at[n], low.at[n], stage_res.at[slot], stage_cot.at[slot], stage_out,
                wgate, wmix, wtail, down_in.at[s], up_in.at[s], par, gup_in.at[s], gdown_in.at[s], ext, gn,
                nout.at[:, pl.ds(0, model)],
            )
            stored(gin_ref, s, k).start()
            chain_tick(1, 1, jnp.where(i < period, i, -1), FINAL)

        for at, step in zip((2, 4, 5, 6, 7, 9), reduction(0, (gup_out, gdown_out))):
            pl.when(i == at)(step)
        return 0

    for copy in stage(0, False):
        copy.start()
    lax.fori_loop(0, seqs * period, back_block, 0)
    for step in reduction(1, (gup_in, gdown_in)):
        step()
    stored(gin_ref, seqs - 1, blocks - 1).wait()


def block_call(in_index, out_index, coef, tensors, tables, vectors, sizes, dp_count, seq_count):
    heads, inner, mixer, rank = sizes
    residual, _, in_weight, _ = tensors
    seqs, tokens, model = residual.shape
    states = (mixer - inner) // 2
    count = tokens // BLOCK * seqs
    chunks = tokens // CHUNK * seqs
    proj = in_weight.shape[1]
    lanes = -(-proj // LANES) * LANES
    adapters = tables[0].shape[0] * dp_count
    own_rows = tables[0].shape[0] * rank
    pairs = seq_count // 2
    shares = tile_shares((model, inner), (proj, model), seq_count)
    every = lambda width: pltpu.VMEM((adapters, rank, width), BF)
    rows = lambda width, kind: pltpu.VMEM((count, BLOCK, width), kind)
    state = lambda: pltpu.VMEM((seqs, states, inner), BF)
    slots = lambda: pltpu.VMEM((2, seqs, PARTS, states, inner // 2 // PARTS), BF)
    stage = lambda *slots: pltpu.VMEM((*slots, BLOCK, model), BF)
    picked = lambda width: pltpu.VMEM((seqs, rank, width), BF)
    any_space = pl.BlockSpec(memory_space=pl.ANY)
    vmem = pl.BlockSpec(memory_space=pltpu.VMEM)
    smem = pl.BlockSpec(memory_space=pltpu.SMEM)
    return pl.pallas_call(
        functools.partial(block_kernel, dp_count, seq_count),
        out_shape=[
            jax.ShapeDtypeStruct(residual.shape, BF),
            jax.ShapeDtypeStruct(residual.shape, BF),
            jax.ShapeDtypeStruct((sum(shares) * seq_count, own_rows, LANES), BF),
        ],
        in_specs=[smem, smem, smem] + [any_space] * 8 + [vmem] * len(vectors),
        out_specs=[any_space] * 2 + [vmem],
        scratch_shapes=[
            rows(mixer, BF),
            rows(mixer, BF),
            rows(inner, BF),
            rows(inner, BF),
            pltpu.VMEM((chunks, states, inner), BF),
            rows(rank, BF),
            rows(LANES, F32),
            rows(LANES, F32),
            rows(LANES, F32),
            rows(LANES, F32),
            rows(states, F32),
            pltpu.VMEM((chunks, 8, LANES), F32),
            pltpu.VMEM((chunks, 8, LANES), F32),
            state(),
            pltpu.VMEM((seqs, 8, inner), F32),
            state(),
            state(),
            state(),
            slots(),
            pltpu.VMEM((2, seqs, 8, inner), F32),
            slots(),
            slots(),
            slots(),
            pltpu.VMEM((model, proj - inner), BF),
            pltpu.VMEM((model, LANES), BF),
            pltpu.VMEM((model, inner), BF),
            pltpu.VMEM((inner, model), BF),
            every(proj - inner),
            every(inner),
            every(model),
            every(model),
            every(inner),
            picked(lanes),
            picked(model),
            picked(model),
            picked(inner),
            pltpu.VMEM((16, mixer), F32),
            pltpu.VMEM((seqs, RIM, model), BF),
            pltpu.VMEM((seqs, RIM, mixer), BF),
            stage(2),
            stage(2),
            stage(),
            pltpu.VMEM((mixer // LANES, BLOCK + RIM, LANES), F32),
            pltpu.VMEM((states, inner), F32),
            pltpu.VMEM((BLOCK // CHUNK, states, inner), BF),
            pltpu.VMEM((BLOCK, inner), BF),
            pltpu.VMEM((BLOCK, inner), BF),
            pltpu.VMEM((CHUNK, inner), BF),
            pltpu.VMEM((8, LANES), F32),
            pltpu.VMEM((8, LANES), F32),
            pltpu.VMEM((LANES, inner), BF),
            pltpu.VMEM((CHUNK, inner), F32),
            pltpu.VMEM((BLOCK, model), F32),
            pltpu.VMEM((seqs, rank, proj), F32),
            pltpu.VMEM((seqs, rank, model), F32),
            pltpu.VMEM((seqs, rank, model), F32),
            pltpu.VMEM((seqs, rank, inner), F32),
            pltpu.VMEM((sum(shares) * seq_count, seqs * rank, LANES), BF),
            pltpu.VMEM((sum(shares) * pairs, seqs * rank, LANES), BF),
            pltpu.VMEM((max(shares) * pairs, seqs * rank, LANES), F32),
            pltpu.VMEM((sum(shares) * pairs, seqs * rank, LANES), BF),
            pltpu.VMEM((max(pairs - 1, 1), sum(shares), seqs * rank, LANES), BF),
            pltpu.VMEM((sum(shares), seqs * rank, LANES), F32),
            pltpu.VMEM((max(dp_count - 1, 1), sum(shares), own_rows, LANES), BF),
            pltpu.VMEM((max(dp_count - 1, 1), sum(shares), own_rows, LANES), BF),
            pltpu.SemaphoreType.DMA((2, 8, max(dp_count // 2, 1), 9)),
            pltpu.SemaphoreType.DMA((2, 2, seqs, 4, PARTS)),
            pltpu.SemaphoreType.DMA((2, 1 + seqs)),
            pltpu.SemaphoreType.DMA((max(count, 5),)),
            pltpu.SemaphoreType.DMA((2, 2, 5, max(pairs, dp_count))),
        ],
        compiler_params=pltpu.CompilerParams(collective_id=1, has_side_effects=True, vmem_limit_bytes=VMEM_LIMIT),
        name="block",
    )(in_index, out_index, coef, *tensors, *tables, *vectors)


def tile_shares(outs, ins, count):
    return [-(-sum(-(-width // LANES) for width in widths) // count) for widths in (outs, ins)]


def unpack_kernel(second, sums, up_out, down_out, up_in, down_in):
    owned, rank, _ = up_out.shape
    for n, pair_of in ((0, (up_out, down_out)), (second, (up_in, down_in))):
        for out in pair_of:
            for t in tiles(out.shape[2]):
                for a in range(owned):
                    out[a, :, t] = sums[n, a * rank : (a + 1) * rank, : t.stop - t.start].astype(F32)
                n += 1


def unpack(sums, owned, rank, widths, count):
    up_out, down_out, up_in, down_in = widths
    shares = tile_shares((up_out, down_out), (up_in, down_in), count)
    whole = pl.BlockSpec(memory_space=pltpu.VMEM)
    return pl.pallas_call(
        functools.partial(unpack_kernel, shares[0] * count),
        out_shape=[jax.ShapeDtypeStruct((owned, rank, width), F32) for width in widths],
        in_specs=[whole],
        out_specs=[whole] * 4,
        name="unpack",
    )(sums)


def on_device(
    residual_in,
    cotangent,
    norm_gain,
    in_weight,
    conv_weight,
    conv_bias,
    step_bias,
    decay_log,
    skip_gain,
    gate_gain,
    out_weight,
    in_down,
    in_up,
    out_down,
    out_up,
    in_index,
    out_index,
):
    heads = step_bias.shape[0]
    inner = gate_gain.shape[0]
    mixer = conv_weight.shape[0]
    rank = in_up.shape[1]
    seq_count = lax.axis_size("seq")
    dp_count = lax.axis_size("dp")
    adapters = in_down.shape[0] * dp_count

    owners = jnp.arange(adapters)[:, None]
    coef = jnp.stack([(index[:, 0][None, :] == owners).astype(F32).reshape(-1) for index in (in_index, out_index)])
    block_out, grad_input, sums = block_call(
        in_index.reshape(-1),
        out_index.reshape(-1),
        coef,
        (residual_in, cotangent, in_weight, out_weight),
        (in_up, in_down.transpose(0, 2, 1), out_up, out_down.transpose(0, 2, 1)),
        (conv_weight.T, conv_bias, gate_gain, norm_gain, skip_gain, step_bias, decay_log),
        (heads, inner, mixer, rank),
        dp_count,
        seq_count,
    )
    model, proj = in_weight.shape[0] * dp_count, in_weight.shape[1]
    gout_up, gout_down, gin_up, gin_down = unpack(sums, in_down.shape[0], rank, (model, inner, proj, model), seq_count)
    gin_down, gout_down = (g.transpose(0, 2, 1) for g in (gin_down, gout_down))
    return (block_out, grad_input, gin_down, gin_up, gout_down, gout_up)


def solution(mesh):
    rows = P("dp", "seq", None)
    split = P("dp", None, None)
    return jax.shard_map(
        on_device,
        mesh=mesh,
        in_specs=(
            rows,
            rows,
            P(),
            P("dp", None),
            P(),
            P(),
            P(),
            P(),
            P(),
            P(),
            P("dp", None),
            split,
            split,
            split,
            split,
            P("dp", None),
            P("dp", None),
        ),
        out_specs=(rows, rows, split, split, split, split),
        check_vma=False,
    )
```

```python
import functools

import jax
import jax.numpy as jnp
from jax import lax
from jax.experimental import pallas as pl
from jax.experimental.pallas import tpu as pltpu
from jax.sharding import PartitionSpec as P

EPS = 1e-05
CHUNK = 128
BLOCK = 256
BAND = 32
RIM = 16
LANES = 128
LOG2E = 1.4426950408889634
BF = jnp.bfloat16
F32 = jnp.float32
MESH = pl.DeviceIdType.MESH
VMEM_LIMIT = 62 * 2**20
PARTS = 3
FINAL = 4
CONV_BIAS, GATE_GAIN, NORM_GAIN, SKIP, STEP_BIAS, RATE = (slice(4 + n, 5 + n) for n in range(6))


def nn(a, b):
    return lax.dot_general(a, b, (((1,), (0,)), ((), ())), preferred_element_type=F32)


def nt(a, b):
    return lax.dot_general(a, b, (((1,), (1,)), ((), ())), preferred_element_type=F32)


def tn(a, b):
    return lax.dot_general(a, b, (((0,), (0,)), ((), ())), preferred_element_type=F32)


def sigmoid(v):
    return 0.5 * jnp.tanh(0.5 * v) + 0.5


def two_terms(values, heads):
    lane = lax.broadcasted_iota(jnp.int32, values.shape, 1)
    values = jnp.where(lane < heads, values, 0.0)
    high = values.astype(BF).astype(F32)
    return (high + pltpu.roll(values - high, LANES // 2, 1)).astype(BF)


def spread(values, onehot, heads):
    return nn(two_terms(values, heads), onehot)


def gather_heads(values, onehot, heads):
    sums = nt(values, onehot)
    lane = lax.broadcasted_iota(jnp.int32, sums.shape, 1)
    return jnp.where(lane < heads, sums, 0.0)


def running(ones, values, heads):
    sums = nn(ones.astype(BF), two_terms(values, heads))
    return sums + pltpu.roll(sums, LANES // 2, 1)


def head_onehot(heads, inner):
    width = inner // heads
    row = lax.broadcasted_iota(jnp.int32, (LANES, inner), 0)
    col = lax.broadcasted_iota(jnp.int32, (LANES, inner), 1)
    row = jnp.where(row < LANES // 2, row, row - LANES // 2)
    low = row * width
    return jnp.where((col >= low) & (col < low + width), 1.0, 0.0).astype(BF)


def lower_ones(length):
    row = lax.broadcasted_iota(jnp.int32, (length, length), 0)
    col = lax.broadcasted_iota(jnp.int32, (length, length), 1)
    return jnp.where(row >= col, 1.0, 0.0).astype(F32)


def upper_ones(length):
    row = lax.broadcasted_iota(jnp.int32, (length, length), 0)
    col = lax.broadcasted_iota(jnp.int32, (length, length), 1)
    return jnp.where(row <= col, 1.0, 0.0).astype(F32)


def tiles(width):
    return [slice(at, min(at + LANES, width)) for at in range(0, width, LANES)]


def rows_of(j):
    return slice(j * CHUNK, (j + 1) * CHUNK)


def bands(j):
    return [(slice(at, at + BAND), slice(j * CHUNK + at, j * CHUNK + at + BAND)) for at in range(0, CHUNK, BAND)]


def write_normed(dst, src, gain, step):
    rows = src.shape[0]

    def body(k, _):
        at = pl.ds(pl.multiple_of(k * step, step), step)
        v = src[at, :].astype(F32)
        scale = lax.rsqrt(jnp.mean(v * v, axis=1, keepdims=True) + EPS)
        dst[at, :] = (v * scale * gain).astype(BF)
        return 0

    lax.fori_loop(0, rows // step, body, 0)


def project_step(heads, first_block, normed, halo, win, wtail, down, up, par, low_ref, xbc, dact, wid, cum, sig, sloc, cpre, ext, state, run, onehot):
    rows = normed.shape[0]
    inner = onehot.shape[1]
    mixer = xbc.shape[1]
    states = (mixer - inner) // 2

    @pl.when(first_block)
    def _():
        state[...] = jnp.zeros_like(state)
        run[...] = jnp.zeros_like(run)
        v = halo[...].astype(F32)
        scale = lax.rsqrt(jnp.mean(v * v, axis=1, keepdims=True) + EPS)
        first = (v * scale * par[NORM_GAIN, : normed.shape[1]]).astype(BF)
        both = jnp.concatenate([first, nt(first, down[...]).astype(BF)], axis=1)
        for at in range(0, mixer, 2 * LANES):
            t = slice(at, at + 2 * LANES)
            v = nn(both, jnp.concatenate([win[:, t], up[:, inner + at : inner + at + 2 * LANES]], axis=0))
            ext[at // LANES, 0:RIM, :] = v[:, :LANES]
            ext[at // LANES + 1, 0:RIM, :] = v[:, LANES:]

    @pl.when(jnp.logical_not(first_block))
    def _():
        ext[:, 0:RIM, :] = ext[:, rows : rows + RIM, :]

    tokens = normed[...]
    low = nt(tokens, down[...]).astype(BF)
    low_ref[...] = low
    both = jnp.concatenate([tokens, low], axis=1)
    raw = nn(both, jnp.concatenate([wtail[...], up[:, inner + mixer :]], axis=0))
    raw = raw + par[STEP_BIAS, :LANES]
    sig[...] = sigmoid(raw)
    widths = jnp.maximum(raw, 0.0) + jnp.log1p(jnp.exp(-jnp.abs(raw)))
    wid[...] = widths
    ones = lower_ones(CHUNK)

    def convolve(n):
        t = slice(n * LANES, n * LANES + LANES)
        for start in range(0, rows, BAND):
            pre = par[CONV_BIAS, t]
            for k in range(4):
                at = RIM - 3 + k + start
                pre = pre + par[k : k + 1, t] * ext[n, at : at + BAND, :]
            s = sigmoid(pre)
            act = pre * s
            xbc[start : start + BAND, t] = act.astype(BF)
            dact[start : start + BAND, t] = (s + act * (1.0 - s)).astype(BF)

    for n in range(0, mixer // LANES + 2, 2):
        if n < mixer // LANES:
            at = n * LANES
            v = nn(both, jnp.concatenate([win[:, at : at + 2 * LANES], up[:, inner + at : inner + at + 2 * LANES]], axis=0))
            ext[n, RIM : RIM + rows, :] = v[:, :LANES]
            ext[n + 1, RIM : RIM + rows, :] = v[:, LANES:]
        if n > 0:
            convolve(n - 2)
            convolve(n - 1)
    for j in range(rows // CHUNK):
        w = widths[rows_of(j)]
        c = running(ones, w * par[RATE, :LANES], heads)
        cum[rows_of(j)] = c
        last = c[CHUNK - 1 : CHUNK]
        tail = spread(jnp.exp(last - c) * w, onehot[...], heads)
        weighted = jnp.concatenate(
            [(xbc[rows_of(j), t].astype(F32) * tail[:, t]).astype(BF) for t in tiles(inner)], axis=1
        )
        inputs_t = xbc[rows_of(j), inner : inner + states].astype(F32).T.astype(BF)
        update = nn(inputs_t, weighted)
        before = run[...]
        cpre[j] = before
        keep = spread(jnp.exp(jnp.broadcast_to(last, before.shape)), onehot[...], heads)[0:1]
        for t in tiles(inner):
            old = state[:, t]
            sloc[j, :, t] = old.astype(BF)
            state[:, t] = keep[:, t] * old + update[:, t]
        run[...] = before + last


def intra_step(heads, normed, low_ref, win, up, xbc, wid, cum, gate, y, onehot):
    inner = onehot.shape[1]
    states = (xbc.shape[1] - inner) // 2
    width = inner // heads
    per = LANES // width
    both = jnp.concatenate([normed[...], low_ref[...]], axis=1)
    lane = lax.broadcasted_iota(jnp.int32, (CHUNK, LANES), 1)
    mask = lower_ones(CHUNK)
    ready = []
    for j in range(xbc.shape[0] // CHUNK):
        c = cum[rows_of(j)] * LOG2E
        wide = spread(wid[rows_of(j)], onehot[...], heads)
        inputs = xbc[rows_of(j), inner : inner + states]
        reads = xbc[rows_of(j), inner + states :]
        ready.append((c, c.T, wide, nt(reads, inputs) * mask))
    columns = tiles(inner)
    order = list(range(normed.shape[1] // LANES, len(columns))) + list(range(normed.shape[1] // LANES))
    for n, k in enumerate(order):
        t = columns[k]
        if n < inner // (2 * LANES):
            g = slice(n * 2 * LANES, (n + 1) * 2 * LANES)
            gate[:, g] = nn(both, jnp.concatenate([win[:, g], up[:, g]], axis=0)).astype(BF)
        for j, (c, c_rows, wide, scores) in enumerate(ready):
            weighted = xbc[rows_of(j), t].astype(F32) * wide[:, t]
            mixing, parts = [], []
            for p in range(per):
                h = k * per + p
                kernel = jnp.exp2(jnp.minimum(c[:, h : h + 1] - c_rows[h : h + 1, :], 0.0))
                mixing.append((kernel * scores).astype(BF))
                inside = (lane >= p * width) & (lane < (p + 1) * width)
                parts.append(jnp.where(inside, weighted, 0.0).astype(BF))
            y[rows_of(j), t] = nn(jnp.concatenate(mixing, axis=1), jnp.concatenate(parts, axis=0)).astype(BF)


def output_step(
    heads, first_block, middle, loaded, y, xbc, gate, cum, sloc, cpre, csuf, start, res, cot, out, wout, down, up, par,
    dreads, rowt, gup, gdown, onehot, snow, adj, run, gated, nout, gno, prod,
):
    rows = res.shape[0]
    inner = onehot.shape[1]
    states = (xbc.shape[1] - inner) // 2
    chunks = rows // CHUNK

    @pl.when(first_block)
    def _():
        adj[...] = jnp.zeros_like(adj)
        run[...] = jnp.zeros_like(run)
        gup[...] = jnp.zeros_like(gup)
        gdown[...] = jnp.zeros_like(gdown)

    reach, scale = [], []
    for j in range(chunks):
        since = spread(jnp.exp(cpre[j]), onehot[...], heads)
        for t in tiles(inner):
            snow[j, :, t] = (sloc[j, :, t].astype(F32) + since[0:1, t] * start[:, t].astype(F32)).astype(BF)
        carried = nn(xbc[rows_of(j), inner + states :], snow[j])
        grow = spread(jnp.exp(cum[rows_of(j)]), onehot[...], heads)
        reach.append(grow)
        for here, at in bands(j):
            total = jnp.zeros((BAND, LANES), F32)
            for t in tiles(inner):
                local = y[at, t].astype(F32) + grow[here, t] * carried[here, t]
                y[at, t] = local.astype(BF)
                g = gate[at, t].astype(F32)
                v = (local + par[SKIP, t] * xbc[at, t].astype(F32)) * (g * sigmoid(g))
                gated[at, t] = v.astype(BF)
                total = total + v * v
            r = lax.rsqrt(jnp.sum(total, axis=1, keepdims=True) * (1.0 / inner) + EPS)
            scale.append(r)
            for t in tiles(inner):
                nout[at, t] = (gated[at, t].astype(F32) * r * par[GATE_GAIN, t]).astype(BF)

    middle()
    loaded()
    normed_out = nout[...]
    cot_rows = cot[...]
    low_out = nt(normed_out, down[...]).astype(BF)
    both = jnp.concatenate([normed_out, low_out], axis=1)
    for at in range(0, out.shape[1], 2 * LANES):
        t = slice(at, at + 2 * LANES)
        part = nn(both, jnp.concatenate([wout[:, t], up[:, t]], axis=0))
        out[:, t] = (res[:, t].astype(F32) + part).astype(BF)
    grad_low = nt(cot_rows, up[...]).astype(BF)
    for at in range(0, inner, 2 * LANES):
        t = slice(at, at + 2 * LANES)
        v = nt(cot_rows, wout[t, :]) + nn(grad_low, down[:, t])
        gno[at // LANES, 0:rows, :] = v[:, :LANES]
        gno[at // LANES + 1, 0:rows, :] = v[:, LANES:]

    def down_gradient(at):
        gdown[:, at : at + 2 * LANES] += tn(grad_low, normed_out[:, at : at + 2 * LANES])

    def up_gradient(at):
        gup[:, at : at + 2 * LANES] += tn(low_out, cot_rows[:, at : at + 2 * LANES])

    tasks = [(up_gradient, at) for at in range(0, out.shape[1], 2 * LANES)]
    tasks += [(down_gradient, at) for at in range(0, inner, 2 * LANES)]
    each = -(-len(tasks) // (rows // BAND))

    for j in reversed(range(chunks)):
        pieces = []
        for m, (here, at) in enumerate(bands(j)):
            total = jnp.zeros((BAND, LANES), F32)
            for n, t in enumerate(tiles(inner)):
                q = gno[n, at, :] * par[GATE_GAIN, t]
                total = total + gated[at, t].astype(F32) * q
            r = scale[j * (CHUNK // BAND) + m]
            shrink = jnp.sum(total, axis=1, keepdims=True) * (1.0 / inner) * (r * r * r)
            scaled = []
            for n, t in enumerate(tiles(inner)):
                q = gno[n, at, :] * par[GATE_GAIN, t]
                grad = r * q - gated[at, t].astype(F32) * shrink
                local = y[at, t].astype(F32)
                g = gate[at, t].astype(F32)
                s = sigmoid(g)
                dy = grad * (g * s)
                y[at, t] = dy.astype(BF)
                full = local + par[SKIP, t] * xbc[at, t].astype(F32)
                gate[at, t] = (grad * full * (s * (1.0 + g * (1.0 - s)))).astype(BF)
                prod[here, t] = (dy * local).astype(BF)
                scaled.append((dy * reach[j][here, t]).astype(BF))
            pieces.append(jnp.concatenate(scaled, axis=1))
            for task, first_column in tasks[:each]:
                task(first_column)
            tasks = tasks[each:]
        rowt[rows_of(j)] = gather_heads(prod[...], onehot[...], heads)
        scaled = jnp.concatenate(pieces, axis=0)
        reads_t = xbc[rows_of(j), inner + states :].astype(F32).T.astype(BF)
        update = nn(reads_t, scaled)
        dreads[rows_of(j)] = nt(scaled, snow[j])
        last = cum[j * CHUNK + CHUNK - 1 : j * CHUNK + CHUNK]
        before = run[...]
        csuf[j] = before
        keep = reach[j][CHUNK - 1 : CHUNK]
        for t in tiles(inner):
            old = adj[:, t]
            sloc[j, :, t] = old.astype(BF)
            adj[:, t] = keep[:, t] * old + update[:, t]
        run[...] = before + last


def adjoint_step(heads, first_block, between, xbc, dact, wid, cum, sig, dy, dreads, rowt, gloc, csuf, end, final, par, onehot, adj, prod, z, held):
    inner = onehot.shape[1]
    states = (xbc.shape[1] - inner) // 2
    width = inner // heads
    per = LANES // width
    mask = upper_ones(CHUNK)
    lane = lax.broadcasted_iota(jnp.int32, (CHUNK, LANES), 1)

    @pl.when(first_block)
    def _():
        overlap = []
        for t in tiles(inner):
            overlap.append(jnp.sum(end[:, t].astype(F32) * final(t), axis=0, keepdims=True))
        v = jnp.broadcast_to(jnp.concatenate(overlap, axis=1), (8, inner))
        high = v.astype(BF)
        rest = (v - high.astype(F32)).astype(BF)
        held[...] = gather_heads(high, onehot[...], heads) + gather_heads(rest, onehot[...], heads)

    for j in reversed(range(xbc.shape[0] // CHUNK)):
        at = rows_of(j)
        c = cum[at]
        w = wid[at]
        c_two = c * LOG2E
        c_rows = c_two.T
        wide = spread(w, onehot[...], heads)
        inputs = xbc[at, inner : inner + states]
        reads = xbc[at, inner + states :]
        scores_t = nt(inputs, reads) * mask
        total = jnp.zeros((CHUNK, CHUNK), F32)
        for k, t in enumerate(tiles(inner)):
            weighted = (xbc[at, t].astype(F32) * wide[:, t]).astype(BF)
            grads = dy[at, t].astype(F32)
            mixing, right = [], []
            for p in range(per):
                inside = (lane >= p * width) & (lane < (p + 1) * width)
                right.append(jnp.where(inside, grads, 0.0).astype(BF))
            right = jnp.concatenate(right, axis=0)
            products = nt(weighted, right)
            for p in range(per):
                h = k * per + p
                kernel = jnp.exp2(jnp.minimum(c_rows[h : h + 1, :] - c_two[:, h : h + 1], 0.0))
                mixing.append((kernel * scores_t).astype(BF))
                total = total + kernel * products[:, p * CHUNK : (p + 1) * CHUNK]
            z[:, t] = nn(jnp.concatenate(mixing, axis=1), right)
        total = total * mask
        dinputs = nn(total.astype(BF), reads)
        dreads_all = dreads[at] + nn(total.T.astype(BF), inputs)

        since = spread(jnp.exp(csuf[j]), onehot[...], heads)
        for t in tiles(inner):
            adj[:, t] = (gloc[j, :, t].astype(F32) + since[0:1, t] * end[:, t].astype(F32)).astype(BF)
        last = c[CHUNK - 1 : CHUNK]
        tail = spread(jnp.exp(last - c), onehot[...], heads)
        carried = nn(inputs, adj[...])
        weighted = []
        for t in tiles(inner):
            x = xbc[at, t].astype(F32)
            v = z[:, t] + tail[:, t] * carried[:, t]
            prod[:, t] = (x * v).astype(BF)
            grad = wide[:, t] * v + par[SKIP, t] * dy[at, t].astype(F32)
            dact[at, t] = (grad * dact[at, t].astype(F32)).astype(BF)
            weighted.append((x * (wide[:, t] * tail[:, t])).astype(BF))
        dinputs = dinputs + nt(jnp.concatenate(weighted, axis=1), adj[...])
        t = slice(inner, inner + states)
        dact[at, t] = (dinputs * dact[at, t].astype(F32)).astype(BF)
        t = slice(inner + states, inner + 2 * states)
        dact[at, t] = (dreads_all * dact[at, t].astype(F32)).astype(BF)
        direct = gather_heads(prod[...], onehot[...], heads)
        grad_rate = held[0:1] + running(mask, rowt[at] - w * direct, heads)
        held[...] = jnp.broadcast_to(grad_rate[0:1], held.shape)
        sig[at] = (direct + par[RATE, :LANES] * grad_rate) * sig[at]
        between(j)


def input_step(heads, first_block, loaded, following, gpre, ggate, graw, low_ref, res, cot, gin, wgate, win, wtail, down, up, par, gup, gdown, ext, gn, nrm):
    rows = res.shape[0]
    inner = ggate.shape[1]
    mixer = gpre.shape[1]
    proj = inner + mixer + heads
    model = res.shape[1]
    gain = par[NORM_GAIN, :model]

    @pl.when(first_block)
    def _():
        gup[...] = jnp.zeros_like(gup)
        gdown[...] = jnp.zeros_like(gdown)

    for n, t in enumerate(tiles(mixer)):
        for j in range(rows // CHUNK):
            ext[n, rows_of(j), :] = gpre[rows_of(j), t].astype(F32)
    following()
    for n, t in enumerate(tiles(mixer)):
        for start in range(0, rows, BAND):
            total = None
            for k in range(4):
                at = 3 - k + start
                term = par[k : k + 1, t] * ext[n, at : at + BAND, :]
                total = term if total is None else total + term
            gpre[start : start + BAND, t] = total.astype(BF)
    grads_gate, grads_mix = ggate[...], jnp.concatenate([gpre[...], graw[...].astype(BF)], axis=1)
    grad_low = (nt(grads_gate, up[:, :inner]) + nt(grads_mix, up[:, inner:])).astype(BF)
    for at in range(0, model, 2 * LANES):
        t = slice(at, at + 2 * LANES)
        mix = jnp.concatenate([win[t, :mixer], wtail[t, :]], axis=1)
        gn[:, t] = nt(grads_gate, wgate[t, :]) + nt(grads_mix, mix) + nn(grad_low, down[:, t])
    loaded()

    low = low_ref[...]
    tasks = []
    for at in range(0, proj, 2 * LANES):
        tasks.append(slice(at, min(at + 2 * LANES, proj)))

    def up_gradient(t):
        grads = grads_gate[:, t] if t.stop <= inner else grads_mix[:, t.start - inner : -(-t.stop // LANES) * LANES - inner]
        gup[:, t] += tn(low, grads)[:, : t.stop - t.start]

    each = -(-len(tasks) // (rows // BAND))
    for n, start in enumerate(range(0, rows, BAND)):
        at = slice(start, start + BAND)
        v = res[at, :].astype(F32)
        u = lax.rsqrt(jnp.mean(v * v, axis=1, keepdims=True) + EPS)
        nrm[at, :] = (v * u * gain).astype(BF)
        w = gn[at, :] * gain
        m = jnp.mean(v * w, axis=1, keepdims=True)
        gin[at, :] = (cot[at, :].astype(F32) + u * w - v * (u * u * u * m)).astype(BF)
        for t in tasks[n * each : (n + 1) * each]:
            up_gradient(t)
    gdown[...] += tn(grad_low, nrm[...])


def block_kernel(
    dp_count, seq_count,
    in_idx, out_idx, coef_ref, res_ref, cot_ref, win_ref, wout_ref, up_in_ref, down_in_ref, up_out_ref, down_out_ref,
    taps_ref, conv_bias_ref, gate_gain_ref, norm_gain_ref, skip_ref, step_bias_ref, decay_ref,
    out_ref, gin_ref, sums_ref,
    xbc, dact, gate, yb, sloc, low, wid, cum, sig, rowt, dreads, cpre, csuf, tot, dtot, start, gown, end,
    theirs, theirs_dec, prefix, passed, tail, wmix, wtail, wgate, wout, up_mix_all, up_gate_all, down_in_all, up_out_all, down_out_all,
    up_in, down_in, up_out, down_out, par,
    halo, rim, stage_res, stage_cot, stage_out, ext, state, snow, gated, nout, prod, run, held, onehot, z, gn,
    gup_in, gdown_in, gup_out, gdown_out, pack, first_half, half_sum, half_sent, line, red, give, owners,
    wsems, csems, hsems, lsems, rsems,
):
    dp = lax.axis_index("dp")
    seq = lax.axis_index("seq")
    seqs, tokens, model = res_ref.shape
    blocks = tokens // BLOCK
    per = BLOCK // CHUNK
    heads = step_bias_ref.shape[0]
    inner = onehot.shape[1]
    mixer = xbc.shape[2]
    proj = win_ref.shape[1]
    pairs = seq_count // 2
    side = lax.rem(seq, 2)
    pair = seq // 2
    chips = dp_count // 2
    partner = (seq + 1 - 2 * side, dp)
    sibling = (seq, dp + 1 - 2 * lax.rem(dp, 2))
    later = (lax.rem(seq + 1, seq_count), dp)
    earlier = (lax.rem(seq + seq_count - 1, seq_count), dp)
    upper = (lax.rem(pair + 1, pairs) * 2 + side, dp)
    lower = (lax.rem(pair + pairs - 1, pairs) * 2 + side, dp)
    others = [(seq, lax.rem(dp + 2 * k, dp_count)) for k in range(1, chips)]
    barrier = pltpu.get_barrier_semaphore()
    along = [(lax.rem(pair + k, pairs) * 2 + side, dp) for k in range(1, pairs)]
    across = [(seq, lax.rem(dp + k, dp_count)) for k in range(1, dp_count)]
    for other in [partner] + along + across:
        pl.semaphore_signal(barrier, inc=1, device_id=other, device_id_type=MESH)
    greeted = pairs + dp_count - 1
    for other, there in ((later, seq < seq_count - 1), (earlier, seq > 0)):
        greeted = greeted + jnp.where(there, 1, 0)

        @pl.when(there)
        def _(other=other):
            pl.semaphore_signal(barrier, inc=1, device_id=other, device_id_type=MESH)

    def load(n):
        s, k = n // blocks, lax.rem(n, blocks) if not isinstance(n, int) else n % blocks
        rows = pl.ds(k * BLOCK, BLOCK)
        return pltpu.make_async_copy(res_ref.at[s, rows], yb.at[n, :, pl.ds(model, model)], lsems.at[n])

    for n in range(seqs * blocks):
        load(n).start()
    onehot[...] = head_onehot(heads, inner)
    par[...] = jnp.zeros_like(par)
    par[0:4] = taps_ref[...]
    par[CONV_BIAS] = conv_bias_ref[...][None, :]
    par[GATE_GAIN, :inner] = gate_gain_ref[...][None, :]
    par[NORM_GAIN, :model] = norm_gain_ref[...][None, :]
    par[STEP_BIAS, :heads] = step_bias_ref[...][None, :]
    par[RATE, :heads] = -jnp.exp(decay_ref[...][None, :])
    par[SKIP, :heads] = skip_ref[...][None, :]
    v = jnp.broadcast_to(par[SKIP, :LANES], (8, LANES))
    par[SKIP, :inner] = spread(v, onehot[...], heads)[0:1]
    wtail[...] = jnp.zeros_like(wtail)
    up_in[:, :, inner + mixer :] = jnp.zeros(up_in.shape[:2] + (LANES,), BF)
    pl.semaphore_wait(barrier, greeted)

    def send(src, dst, to, sems, *at):
        return pltpu.make_async_remote_copy(
            src_ref=src, dst_ref=dst, send_sem=sems.at[(0,) + at], recv_sem=sems.at[(1,) + at],
            device_id=to, device_id_type=MESH,
        )

    def rows_piece(ref, out, at, to, wide, n):
        share = ref.shape[0]
        half = share // 2

        def source(which):
            return ref.at[pl.ds(pl.multiple_of(which * half, 16), half), pl.ds(at, wide)]

        def target(owner, which):
            return out.at[pl.ds(pl.multiple_of(owner * share + which * half, 16), half), pl.ds(to, wide)]

        return source, target, n

    def table_piece(ref, out, at, wide, n):
        owned = ref.shape[0]
        return (lambda _: ref.at[:, :, pl.ds(at, wide)]), (lambda owner, _: out.at[pl.ds(owner * owned, owned)]), n, None, 0

    width = proj - inner
    split = mixer // 2 // LANES * LANES
    odd = lax.rem(pair, 2)
    across_y = (partner, side)
    across_z = (((pair + 1 - 2 * odd) * 2 + side, dp), odd)
    groups = [
        [
            (*rows_piece(win_ref, wmix, inner, 0, split, 0), *across_y),
            (*rows_piece(win_ref, wmix, inner + split, split, width - split, 1), *across_y),
            table_piece(down_in_ref, down_in_all, 0, model, 2),
            table_piece(up_in_ref, up_mix_all, inner, width, 3),
        ],
        [
            table_piece(up_in_ref, up_gate_all, 0, inner, 4),
            (*rows_piece(win_ref, wgate, 0, 0, inner, 5), *across_z),
        ],
        [
            (*rows_piece(wout_ref, wout, 0, 0, wout_ref.shape[1], 6), *across_z),
            table_piece(down_out_ref, down_out_all, 0, inner, 7),
            table_piece(up_out_ref, up_out_all, 0, model, 8),
        ],
    ]

    def shards(k):
        return lax.rem(dp - 2 * k + dp_count, dp_count)

    def over_x(group):
        return [
            send(source(mine), target(dp, mine), others[k - 1], wsems, 0, k, n)
            for source, target, n, _, mine in group
            for k in range(1, chips)
        ]

    def own(group):
        copies = []
        for source, target, n, mate, _ in group:
            for which in range(1 if mate is None else 2):
                copies.append(pltpu.make_async_copy(source(which), target(dp, which), wsems.at[0, 6 + which, 0, n]))
                copies.append(send(source(which), target(dp, which), sibling, wsems, 3 + which, 0, n))
        return copies

    def forward(group, start_it):
        for source, target, n, mate, mine in group:
            for k in range(1, chips):
                here = target(shards(k), mine)
                if start_it:
                    send(source(mine), here, others[k - 1], wsems, 0, k, n).wait_recv()
                copies = [send(here, here, sibling, wsems, 2, k, n)]
                if mate is not None:
                    copies.append(send(here, here, mate, wsems, 1, k, n))
                if start_it:
                    for copy in copies:
                        copy.start()
                else:
                    copies[0].wait()
                    if mate is not None:
                        copies[1].wait_send()

    def relay(group, start_it):
        for source, target, n, mate, mine in group:
            if mate is None:
                continue
            for k in range(1, chips):
                there = target(shards(k), 1 - mine)
                if start_it:
                    send(there, there, mate, wsems, 1, k, n).wait_recv()
                over = send(there, there, sibling, wsems, 5, k, n)
                if start_it:
                    over.start()
                else:
                    over.wait()

    def settle(group):
        for copy in over_x(group):
            copy.wait_send()
        for copy in own(group):
            copy.wait()
        forward(group, False)
        relay(group, False)

    edge = send(res_ref.at[:, pl.ds(tokens - RIM, RIM)], halo, later, hsems, 0)
    for copy in over_x(groups[0]):
        copy.start()

    @pl.when(seq < seq_count - 1)
    def _():
        edge.start()

    for copy in own(groups[0]):
        copy.start()
    gain = par[NORM_GAIN, :model]

    def norm_block(n, _):
        load(n).wait()
        write_normed(yb.at[n, :, pl.ds(0, model)], yb.at[n, :, pl.ds(model, model)], gain, 32)
        return 0

    lax.fori_loop(0, seqs * blocks, norm_block, 0)
    forward(groups[0], True)
    for copy in over_x(groups[1]):
        copy.start()
    relay(groups[0], True)

    @pl.when(seq == 0)
    def _():
        halo[...] = jnp.zeros_like(halo)

    @pl.when(seq > 0)
    def _():
        edge.wait_recv()

    @pl.when(seq < seq_count - 1)
    def _():
        edge.wait_send()

    settle(groups[0])
    for copy in own(groups[1]):
        copy.start()

    def pick(dst, table, idx_ref, at=0):
        for q in range(seqs):
            dst[q, :, at : at + table.shape[2]] = table[idx_ref[q]]

    pick(down_in, down_in_all, in_idx)
    pick(up_in, up_mix_all, in_idx, inner)
    wtail[:, :heads] = wmix[:, mixer:]

    half = inner // 2
    wide = half // PARTS

    def cols(base, q):
        return pl.ds(pl.multiple_of(base * half + q * wide, LANES), wide)

    def chain(d, s):
        my_pair = pairs - 1 - pair if d else pair
        my_side = 1 - side if d else side
        ahead = lower if d else upper
        total, result = (gown, end) if d else (tot, start)

        def decs():
            return send(dtot.at[s], theirs_dec.at[d, s], partner, csems, d, s, 3, 0)

        def swap(q):
            return send(total.at[s, :, cols(1 - my_side, q)], theirs.at[d, s, q], partner, csems, d, s, 0, q)

        def hop(q):
            return send(passed.at[d, s, q], prefix.at[d, s, q], ahead, csems, d, s, 1, q)

        def give(q):
            return send(tail.at[d, s, q], result.at[s, :, cols(my_side, q)], partner, csems, d, s, 2, q)

        return my_pair, my_side, total, result, decs, swap, hop, give

    def chain_start(d, s):
        _, _, _, _, decs, swap, _, _ = chain(d, s)
        decs().start()
        for q in range(PARTS):
            swap(q).start()

    def chain_tick(d, s, tick, final):
        my_pair, my_side, total, result, decs, swap, hop, give = chain(d, s)
        for q in range(PARTS):
            turn = jnp.minimum(my_pair + (1 if q else 0), final)

            @pl.when(tick == turn)
            def _(q=q):
                if q == 0:
                    decs().wait_recv()
                swap(q).wait_recv()

                @pl.when(my_pair == 0)
                def _():
                    prefix[d, s, q] = jnp.zeros_like(prefix[d, s, q])

                @pl.when(my_pair > 0)
                def _():
                    hop(q).wait_recv()

                own_dec = dtot[s, 0:1, cols(my_side, q)]
                their_dec = theirs_dec[d, s, 0:1, cols(my_side, q)]
                own_total = total[s, :, cols(my_side, q)].astype(F32)
                other = theirs[d, s, q].astype(F32)
                before = prefix[d, s, q].astype(F32)
                left = my_side == 0
                first = jnp.where(left, own_total, other)
                second = jnp.where(left, other, own_total)
                first_dec = jnp.where(left, own_dec, their_dec)
                second_dec = jnp.where(left, their_dec, own_dec)
                middle = first_dec * before + first
                passed[d, s, q] = (second_dec * middle + second).astype(BF)

                @pl.when(my_pair < pairs - 1)
                def _():
                    hop(q).start()

                result[s, :, cols(my_side, q)] = jnp.where(left, before, middle).astype(BF)
                tail[d, s, q] = jnp.where(left, middle, before).astype(BF)
                give(q).start()

    def chain_end(d, s):
        my_pair, _, _, _, decs, swap, hop, give = chain(d, s)
        decs().wait_send()
        for q in range(PARTS):
            give(q).wait()
            swap(q).wait_send()

            @pl.when(my_pair < pairs - 1)
            def _(q=q):
                hop(q).wait_send()

    rank = gup_in.shape[1]
    owned = up_in_ref.shape[0]

    def reduction(number, parts):
        counts = [sum(-(-g.shape[2] // LANES) for g in pair_of) for pair_of in ((gup_out, gdown_out), (gup_in, gdown_in))]
        shares = [-(-n // seq_count) for n in counts]
        share = shares[number]
        wide = pairs * share
        before = sum(shares[:number])
        base, middle, small = before * seq_count, before * pairs, pl.ds(before, share)
        place = pl.ds(base + (side * pairs + pair) * share, share)

        def swap(there):
            theirs_of = pack.at[pl.ds(base + ((1 - side) * pairs + there) * share, share)]
            here = first_half.at[pl.ds(middle + there * share, share)]
            return send(theirs_of, here, partner, rsems, number, 0, there)

        def along_line(k):
            there = lax.rem(pair + k, pairs)
            mine = half_sent.at[pl.ds(middle + there * share, share)]
            return send(mine, line.at[k - 1, small], along[k - 1], rsems, number, 1, k)

        def to_owner(k):
            return send(give.at[k - 1, small], owners.at[k - 1, small], across[k - 1], rsems, number, 2, k)

        def back_along(k):
            return send(sums_ref.at[place], sums_ref.at[place], along[k - 1], rsems, number, 3, k)

        def back_across(k):
            there = lax.rem(pair + pairs - k, pairs)
            ours = sums_ref.at[pl.ds(base + (side * pairs + there) * share, share)]
            return send(ours, ours, partner, rsems, number, 4, k)

        def part(owner, n, a):
            total = None
            for q in range(seqs):
                c = coef_ref[1 - number, (owner * owned + a) * seqs + q]
                term = c * red[before + n, q * rank : (q + 1) * rank, :]
                total = term if total is None else total + term
            return total

        def start():
            n = base
            for ref in parts:
                for t in tiles(ref.shape[2]):
                    for q in range(seqs):
                        v = ref[q, :, t]
                        if t.stop - t.start < LANES:
                            v = jnp.concatenate([v, jnp.zeros((rank, LANES - t.stop + t.start), F32)], axis=1)
                        pack[n, q * rank : (q + 1) * rank, :] = v.astype(BF)
                    n += 1
            for m in range(n, base + share * seq_count):
                pack[m] = jnp.zeros_like(pack[m])
            for k in list(range(1, pairs)) + [0]:
                swap(lax.rem(pair + k, pairs)).start()

        def second():
            for k in list(range(1, pairs)) + [0]:
                there = lax.rem(pair + k, pairs)
                swap(there).wait()

                def add(n, _, there=there):
                    at = there * share + n
                    v = pack[base + side * wide + at].astype(F32) + first_half[middle + at].astype(F32)
                    half_sum[at] = v
                    half_sent[middle + at] = v.astype(BF)
                    return 0

                lax.fori_loop(0, share, add, 0)
                if k:
                    along_line(k).start()

        def third():
            for k in range(1, pairs):
                along_line(k).wait()
            for n in range(share):
                v = half_sum[pair * share + n]
                for k in range(pairs - 1):
                    v = v + line[k, before + n].astype(F32)
                red[before + n] = v
            for k in range(1, dp_count):
                owner = lax.rem(dp + k, dp_count)
                for n in range(share):
                    for a in range(owned):
                        give[k - 1, before + n, a * rank : (a + 1) * rank, :] = part(owner, n, a).astype(BF)
                to_owner(k).start()

        def fourth():
            for k in range(1, dp_count):
                to_owner(k).wait()
            for n in range(share):
                for a in range(owned):
                    v = part(dp, n, a)
                    for k in range(dp_count - 1):
                        v = v + owners[k, before + n, a * rank : (a + 1) * rank, :].astype(F32)
                    sums_ref[base + (side * pairs + pair) * share + n, a * rank : (a + 1) * rank, :] = v.astype(BF)
            for k in range(1, pairs):
                back_along(k).start()
            back_across(0).start()

        def fifth():
            for k in range(1, pairs):
                back_along(k).wait()
                back_across(k).start()

        def finish():
            for k in range(pairs):
                back_across(k).wait()

        return [start, second, third, fourth, fifth, finish]

    def chunk_of(n):
        return pl.ds(n * per, per)

    def project_block(n, _):
        s, k = n // blocks, lax.rem(n, blocks)
        project_step(
            heads, k == 0, yb.at[n, :, pl.ds(0, model)], halo.at[s], wmix, wtail, down_in.at[s], up_in.at[s], par, low.at[n],
            xbc.at[n], dact.at[n], wid.at[n], cum.at[n], sig.at[n], sloc.at[chunk_of(n)], cpre.at[chunk_of(n)],
            ext, state, run, onehot,
        )

        @pl.when(k == blocks - 1)
        def _():
            tot[s] = state[...].astype(BF)
            dtot[s] = spread(jnp.exp(run[...]), onehot[...], heads)

        @pl.when(n == blocks - 2)
        def _():
            forward(groups[1], True)
            for copy in over_x(groups[2]) + own(groups[2]):
                copy.start()

        @pl.when(n == blocks - 1)
        def _():
            chain_start(0, 0)

        @pl.when(n == blocks + 1)
        def _():
            forward(groups[2], True)

        @pl.when(n >= blocks)
        def _():
            chain_tick(0, 0, n - blocks, FINAL)

        return 0

    lax.fori_loop(0, seqs * blocks, project_block, 0)
    chain_start(0, 1)
    relay(groups[1], True)
    settle(groups[1])
    pick(up_in, up_gate_all, in_idx)

    def intra_block(n):
        s = n // blocks
        intra_step(
            heads, yb.at[n, :, pl.ds(0, model)], low.at[n], wgate, up_in.at[s], xbc.at[n], wid.at[n], cum.at[n], gate.at[n],
            yb.at[n], onehot,
        )

    def staged(s, k, slot):
        rows = pl.ds(k * BLOCK, BLOCK)
        return [
            pltpu.make_async_copy(res_ref.at[s, rows], stage_res.at[slot], lsems.at[slot]),
            pltpu.make_async_copy(cot_ref.at[s, rows], stage_cot.at[slot], lsems.at[2 + slot]),
        ]

    def stored(ref, s, k):
        return pltpu.make_async_copy(stage_out, ref.at[s, pl.ds(k * BLOCK, BLOCK)], lsems.at[4])

    def stage(n, backwards):
        s, k = n // blocks, lax.rem(n, blocks)
        return staged(s, blocks - 1 - k if backwards else k, lax.rem(n, 2))

    first = blocks + 1
    second = seqs * blocks + blocks

    def output_block(i):
        s = jnp.where(i < second, 0, 1)
        k = blocks - 1 - (i - jnp.where(i < second, first, second))
        n = s * blocks + k
        turn = s * blocks + blocks - 1 - k
        slot = lax.rem(turn, 2)

        @pl.when(i == first)
        def _():
            relay(groups[2], True)
            settle(groups[2])
            pick(down_out, down_out_all, out_idx)
            pick(up_out, up_out_all, out_idx)
            chain_end(0, 0)

        @pl.when(i == second)
        def _():
            chain_end(0, 1)

        def middle():
            chain_tick(1, 0, among(i, {second: 1, second + 2: FINAL}), FINAL)

        def loaded():
            for copy in stage(turn, True):
                copy.wait()

            @pl.when(turn < seqs * blocks - 1)
            def _():
                for copy in stage(turn + 1, True):
                    copy.start()

            @pl.when(i > first)
            def _():
                stored(out_ref, s, k).wait()

        output_step(
            heads, k == blocks - 1, middle, loaded, yb.at[n], xbc.at[n], gate.at[n], cum.at[n], sloc.at[chunk_of(n)],
            cpre.at[chunk_of(n)], csuf.at[chunk_of(n)], start.at[s], stage_res.at[slot], stage_cot.at[slot], stage_out, wout, down_out.at[s],
            up_out.at[s], par, dreads.at[n], rowt.at[n], gup_out.at[s], gdown_out.at[s], onehot, snow, state, run, gated,
            nout, ext, prod,
        )
        stored(out_ref, s, k).start()

        @pl.when(k == 0)
        def _():
            gown[s] = state[...].astype(BF)

        @pl.when(i == first + blocks - 1)
        def _():
            chain_start(1, 0)

    def among(i, turns):
        found = -1
        for at, tick in turns.items():
            found = jnp.where(i == at, tick, found)
        return found

    def middle_block(i, _):
        inside = (i < first) | ((i >= first + blocks) & (i < second))

        @pl.when(inside)
        def _():
            intra_block(jnp.where(i < first, i, i - blocks))

        @pl.when(jnp.logical_not(inside))
        def _():
            output_block(i)

        chain_tick(0, 0, among(i, {1: FINAL - 1, blocks: FINAL}), FINAL)
        chain_tick(0, 1, among(i, {1: 0, blocks: 1, first: 2, first + 1: 3, first + 2: FINAL}), FINAL)
        chain_tick(1, 0, among(i, {second - 1: 0, second: 2, second + 1: 3}), FINAL)
        return 0

    for copy in stage(0, True):
        copy.start()
    lax.fori_loop(0, 2 * seqs * blocks, middle_block, 0)
    stored(out_ref, seqs - 1, 0).wait()
    chain_start(1, 1)

    def rim_edge(s):
        return send(dact.at[s * blocks, pl.ds(0, RIM)], rim.at[s], earlier, hsems, 1 + s)

    period = 2 * blocks

    def back_block(i, _):
        s, r = i // period, lax.rem(i, period)

        @pl.when(r < blocks)
        def _():
            k = blocks - 1 - r
            n = s * blocks + k

            @pl.when(i == 0)
            def _():
                chain_end(1, 0)

            @pl.when(i == period)
            def _():
                chain_end(1, 1)

            def between(j):
                if j == 0:
                    chain_tick(1, 1, jnp.where(i < blocks, i, -1), FINAL)

            adjoint_step(
                heads, k == blocks - 1, between, xbc.at[n], dact.at[n], wid.at[n], cum.at[n], sig.at[n], yb.at[n], dreads.at[n],
                rowt.at[n], sloc.at[chunk_of(n)], csuf.at[chunk_of(n)], end.at[s],
                lambda t: tot[s, :, t].astype(F32) + dtot[s, 0:1, t] * start[s, :, t].astype(F32),
                par, onehot, nout.at[pl.ds(0, CHUNK)], prod, z, held,
            )

            @pl.when(k == 0)
            def _():
                for q in range(seqs):
                    @pl.when((s == q) & (seq > 0))
                    def _(q=q):
                        rim_edge(q).start()

        @pl.when(r >= blocks)
        def _():
            k = r - blocks
            n = s * blocks + k
            late_one = k == blocks - 1
            slot = lax.rem(n, 2)
            for q in range(seqs):
                @pl.when((s == q) & (k == 0) & (seq > 0))
                def _(q=q):
                    rim_edge(q).wait_send()

                @pl.when((s == q) & late_one & (seq < seq_count - 1))
                def _(q=q):
                    rim_edge(q).wait_recv()

                @pl.when((s == q) & late_one & (seq == seq_count - 1))
                def _(q=q):
                    rim[q] = jnp.zeros_like(rim[q])

            def loaded():
                for copy in stage(n, False):
                    copy.wait()

                @pl.when(n < seqs * blocks - 1)
                def _():
                    for copy in stage(n + 1, False):
                        copy.start()

                @pl.when(i > blocks)
                def _():
                    stored(gin_ref, s, k).wait()

            def following():
                @pl.when(late_one)
                def _():
                    for m, t in enumerate(tiles(mixer)):
                        ext[m, BLOCK : BLOCK + RIM, :] = rim[s, :, t].astype(F32)

                @pl.when(jnp.logical_not(late_one))
                def _():
                    for m, t in enumerate(tiles(mixer)):
                        ext[m, BLOCK : BLOCK + RIM, :] = dact[n + 1, 0:RIM, t].astype(F32)

            input_step(
                heads, k == 0, loaded, following, dact.at[n], gate.at[n], sig.at[n], low.at[n], stage_res.at[slot], stage_cot.at[slot], stage_out,
                wgate, wmix, wtail, down_in.at[s], up_in.at[s], par, gup_in.at[s], gdown_in.at[s], ext, gn,
                nout.at[:, pl.ds(0, model)],
            )
            stored(gin_ref, s, k).start()
            chain_tick(1, 1, jnp.where(i < period, i, -1), FINAL)

        for at, step in zip((2, 4, 5, 6, 7, 9), reduction(0, (gup_out, gdown_out))):
            pl.when(i == at)(step)
        return 0

    for copy in stage(0, False):
        copy.start()
    lax.fori_loop(0, seqs * period, back_block, 0)
    for step in reduction(1, (gup_in, gdown_in)):
        step()
    stored(gin_ref, seqs - 1, blocks - 1).wait()


def block_call(in_index, out_index, coef, tensors, tables, vectors, sizes, dp_count, seq_count):
    heads, inner, mixer, rank = sizes
    residual, _, in_weight, _ = tensors
    seqs, tokens, model = residual.shape
    states = (mixer - inner) // 2
    count = tokens // BLOCK * seqs
    chunks = tokens // CHUNK * seqs
    proj = in_weight.shape[1]
    lanes = -(-proj // LANES) * LANES
    adapters = tables[0].shape[0] * dp_count
    own_rows = tables[0].shape[0] * rank
    pairs = seq_count // 2
    shares = tile_shares((model, inner), (proj, model), seq_count)
    every = lambda width: pltpu.VMEM((adapters, rank, width), BF)
    rows = lambda width, kind: pltpu.VMEM((count, BLOCK, width), kind)
    state = lambda: pltpu.VMEM((seqs, states, inner), BF)
    slots = lambda: pltpu.VMEM((2, seqs, PARTS, states, inner // 2 // PARTS), BF)
    stage = lambda *slots: pltpu.VMEM((*slots, BLOCK, model), BF)
    picked = lambda width: pltpu.VMEM((seqs, rank, width), BF)
    any_space = pl.BlockSpec(memory_space=pl.ANY)
    vmem = pl.BlockSpec(memory_space=pltpu.VMEM)
    smem = pl.BlockSpec(memory_space=pltpu.SMEM)
    return pl.pallas_call(
        functools.partial(block_kernel, dp_count, seq_count),
        out_shape=[
            jax.ShapeDtypeStruct(residual.shape, BF),
            jax.ShapeDtypeStruct(residual.shape, BF),
            jax.ShapeDtypeStruct((sum(shares) * seq_count, own_rows, LANES), BF),
        ],
        in_specs=[smem, smem, smem] + [any_space] * 8 + [vmem] * len(vectors),
        out_specs=[any_space] * 2 + [vmem],
        scratch_shapes=[
            rows(mixer, BF),
            rows(mixer, BF),
            rows(inner, BF),
            rows(inner, BF),
            pltpu.VMEM((chunks, states, inner), BF),
            rows(rank, BF),
            rows(LANES, F32),
            rows(LANES, F32),
            rows(LANES, F32),
            rows(LANES, F32),
            rows(states, F32),
            pltpu.VMEM((chunks, 8, LANES), F32),
            pltpu.VMEM((chunks, 8, LANES), F32),
            state(),
            pltpu.VMEM((seqs, 8, inner), F32),
            state(),
            state(),
            state(),
            slots(),
            pltpu.VMEM((2, seqs, 8, inner), F32),
            slots(),
            slots(),
            slots(),
            pltpu.VMEM((model, proj - inner), BF),
            pltpu.VMEM((model, LANES), BF),
            pltpu.VMEM((model, inner), BF),
            pltpu.VMEM((inner, model), BF),
            every(proj - inner),
            every(inner),
            every(model),
            every(model),
            every(inner),
            picked(lanes),
            picked(model),
            picked(model),
            picked(inner),
            pltpu.VMEM((16, mixer), F32),
            pltpu.VMEM((seqs, RIM, model), BF),
            pltpu.VMEM((seqs, RIM, mixer), BF),
            stage(2),
            stage(2),
            stage(),
            pltpu.VMEM((mixer // LANES, BLOCK + RIM, LANES), F32),
            pltpu.VMEM((states, inner), F32),
            pltpu.VMEM((BLOCK // CHUNK, states, inner), BF),
            pltpu.VMEM((BLOCK, inner), BF),
            pltpu.VMEM((BLOCK, inner), BF),
            pltpu.VMEM((CHUNK, inner), BF),
            pltpu.VMEM((8, LANES), F32),
            pltpu.VMEM((8, LANES), F32),
            pltpu.VMEM((LANES, inner), BF),
            pltpu.VMEM((CHUNK, inner), F32),
            pltpu.VMEM((BLOCK, model), F32),
            pltpu.VMEM((seqs, rank, proj), F32),
            pltpu.VMEM((seqs, rank, model), F32),
            pltpu.VMEM((seqs, rank, model), F32),
            pltpu.VMEM((seqs, rank, inner), F32),
            pltpu.VMEM((sum(shares) * seq_count, seqs * rank, LANES), BF),
            pltpu.VMEM((sum(shares) * pairs, seqs * rank, LANES), BF),
            pltpu.VMEM((max(shares) * pairs, seqs * rank, LANES), F32),
            pltpu.VMEM((sum(shares) * pairs, seqs * rank, LANES), BF),
            pltpu.VMEM((max(pairs - 1, 1), sum(shares), seqs * rank, LANES), BF),
            pltpu.VMEM((sum(shares), seqs * rank, LANES), F32),
            pltpu.VMEM((max(dp_count - 1, 1), sum(shares), own_rows, LANES), BF),
            pltpu.VMEM((max(dp_count - 1, 1), sum(shares), own_rows, LANES), BF),
            pltpu.SemaphoreType.DMA((2, 8, max(dp_count // 2, 1), 9)),
            pltpu.SemaphoreType.DMA((2, 2, seqs, 4, PARTS)),
            pltpu.SemaphoreType.DMA((2, 1 + seqs)),
            pltpu.SemaphoreType.DMA((max(count, 5),)),
            pltpu.SemaphoreType.DMA((2, 2, 5, max(pairs, dp_count))),
        ],
        compiler_params=pltpu.CompilerParams(collective_id=1, has_side_effects=True, vmem_limit_bytes=VMEM_LIMIT),
        name="block",
    )(in_index, out_index, coef, *tensors, *tables, *vectors)


def tile_shares(outs, ins, count):
    return [-(-sum(-(-width // LANES) for width in widths) // count) for widths in (outs, ins)]


def unpack_kernel(second, sums, up_out, down_out, up_in, down_in):
    owned, rank, _ = up_out.shape
    for n, pair_of in ((0, (up_out, down_out)), (second, (up_in, down_in))):
        for out in pair_of:
            for t in tiles(out.shape[2]):
                for a in range(owned):
                    out[a, :, t] = sums[n, a * rank : (a + 1) * rank, : t.stop - t.start].astype(F32)
                n += 1


def unpack(sums, owned, rank, widths, count):
    up_out, down_out, up_in, down_in = widths
    shares = tile_shares((up_out, down_out), (up_in, down_in), count)
    whole = pl.BlockSpec(memory_space=pltpu.VMEM)
    return pl.pallas_call(
        functools.partial(unpack_kernel, shares[0] * count),
        out_shape=[jax.ShapeDtypeStruct((owned, rank, width), F32) for width in widths],
        in_specs=[whole],
        out_specs=[whole] * 4,
        name="unpack",
    )(sums)


def on_device(
    residual_in,
    cotangent,
    norm_gain,
    in_weight,
    conv_weight,
    conv_bias,
    step_bias,
    decay_log,
    skip_gain,
    gate_gain,
    out_weight,
    in_down,
    in_up,
    out_down,
    out_up,
    in_index,
    out_index,
):
    heads = step_bias.shape[0]
    inner = gate_gain.shape[0]
    mixer = conv_weight.shape[0]
    rank = in_up.shape[1]
    seq_count = lax.axis_size("seq")
    dp_count = lax.axis_size("dp")
    adapters = in_down.shape[0] * dp_count

    owners = jnp.arange(adapters)[:, None]
    coef = jnp.stack([(index[:, 0][None, :] == owners).astype(F32).reshape(-1) for index in (in_index, out_index)])
    block_out, grad_input, sums = block_call(
        in_index.reshape(-1),
        out_index.reshape(-1),
        coef,
        (residual_in, cotangent, in_weight, out_weight),
        (in_up, in_down.transpose(0, 2, 1), out_up, out_down.transpose(0, 2, 1)),
        (conv_weight.T, conv_bias, gate_gain, norm_gain, skip_gain, step_bias, decay_log),
        (heads, inner, mixer, rank),
        dp_count,
        seq_count,
    )
    model, proj = in_weight.shape[0] * dp_count, in_weight.shape[1]
    gout_up, gout_down, gin_up, gin_down = unpack(sums, in_down.shape[0], rank, (model, inner, proj, model), seq_count)
    gin_down, gout_down = (g.transpose(0, 2, 1) for g in (gin_down, gout_down))
    return (block_out, grad_input, gin_down, gin_up, gout_down, gout_up)


def solution(mesh):
    rows = P("dp", "seq", None)
    split = P("dp", None, None)
    return jax.shard_map(
        on_device,
        mesh=mesh,
        in_specs=(
            rows,
            rows,
            P(),
            P("dp", None),
            P(),
            P(),
            P(),
            P(),
            P(),
            P(),
            P("dp", None),
            split,
            split,
            split,
            split,
            P("dp", None),
            P("dp", None),
        ),
        out_specs=(rows, rows, split, split, split, split),
        check_vma=False,
    )
```

```python
import functools

import jax
import jax.numpy as jnp
from jax import lax
from jax.experimental import pallas as pl
from jax.experimental.pallas import tpu as pltpu
from jax.sharding import PartitionSpec as P

EPS = 1e-05
CHUNK = 128
BLOCK = 256
BAND = 32
RIM = 16
LANES = 128
LOG2E = 1.4426950408889634
BF = jnp.bfloat16
F32 = jnp.float32
MESH = pl.DeviceIdType.MESH
VMEM_LIMIT = 62 * 2**20
PARTS = 3
FINAL = 4
CONV_BIAS, GATE_GAIN, NORM_GAIN, SKIP, STEP_BIAS, RATE = (slice(4 + n, 5 + n) for n in range(6))


def nn(a, b):
    return lax.dot_general(a, b, (((1,), (0,)), ((), ())), preferred_element_type=F32)


def nt(a, b):
    return lax.dot_general(a, b, (((1,), (1,)), ((), ())), preferred_element_type=F32)


def tn(a, b):
    return lax.dot_general(a, b, (((0,), (0,)), ((), ())), preferred_element_type=F32)


def sigmoid(v):
    return 0.5 * jnp.tanh(0.5 * v) + 0.5


def two_terms(values, heads):
    lane = lax.broadcasted_iota(jnp.int32, values.shape, 1)
    values = jnp.where(lane < heads, values, 0.0)
    high = values.astype(BF).astype(F32)
    return (high + pltpu.roll(values - high, LANES // 2, 1)).astype(BF)


def spread(values, onehot, heads):
    return nn(two_terms(values, heads), onehot)


def gather_heads(values, onehot, heads):
    sums = nt(values, onehot)
    lane = lax.broadcasted_iota(jnp.int32, sums.shape, 1)
    return jnp.where(lane < heads, sums, 0.0)


def running(ones, values, heads):
    sums = nn(ones.astype(BF), two_terms(values, heads))
    return sums + pltpu.roll(sums, LANES // 2, 1)


def head_onehot(heads, inner):
    width = inner // heads
    row = lax.broadcasted_iota(jnp.int32, (LANES, inner), 0)
    col = lax.broadcasted_iota(jnp.int32, (LANES, inner), 1)
    row = jnp.where(row < LANES // 2, row, row - LANES // 2)
    low = row * width
    return jnp.where((col >= low) & (col < low + width), 1.0, 0.0).astype(BF)


def lower_ones(length):
    row = lax.broadcasted_iota(jnp.int32, (length, length), 0)
    col = lax.broadcasted_iota(jnp.int32, (length, length), 1)
    return jnp.where(row >= col, 1.0, 0.0).astype(F32)


def upper_ones(length):
    row = lax.broadcasted_iota(jnp.int32, (length, length), 0)
    col = lax.broadcasted_iota(jnp.int32, (length, length), 1)
    return jnp.where(row <= col, 1.0, 0.0).astype(F32)


def tiles(width):
    return [slice(at, min(at + LANES, width)) for at in range(0, width, LANES)]


def rows_of(j):
    return slice(j * CHUNK, (j + 1) * CHUNK)


def bands(j):
    return [(slice(at, at + BAND), slice(j * CHUNK + at, j * CHUNK + at + BAND)) for at in range(0, CHUNK, BAND)]


def write_normed(dst, src, gain, step):
    rows = src.shape[0]

    def body(k, _):
        at = pl.ds(pl.multiple_of(k * step, step), step)
        v = src[at, :].astype(F32)
        scale = lax.rsqrt(jnp.mean(v * v, axis=1, keepdims=True) + EPS)
        dst[at, :] = (v * scale * gain).astype(BF)
        return 0

    lax.fori_loop(0, rows // step, body, 0)


def project_step(heads, first_block, normed, halo, win, wtail, down, up, par, low_ref, xbc, dact, wid, cum, sig, sloc, cpre, ext, state, run, onehot):
    rows = normed.shape[0]
    inner = onehot.shape[1]
    mixer = xbc.shape[1]
    states = (mixer - inner) // 2

    @pl.when(first_block)
    def _():
        state[...] = jnp.zeros_like(state)
        run[...] = jnp.zeros_like(run)
        v = halo[...].astype(F32)
        scale = lax.rsqrt(jnp.mean(v * v, axis=1, keepdims=True) + EPS)
        first = (v * scale * par[NORM_GAIN, : normed.shape[1]]).astype(BF)
        both = jnp.concatenate([first, nt(first, down[...]).astype(BF)], axis=1)
        for at in range(0, mixer, 2 * LANES):
            t = slice(at, at + 2 * LANES)
            v = nn(both, jnp.concatenate([win[:, t], up[:, inner + at : inner + at + 2 * LANES]], axis=0))
            ext[at // LANES, 0:RIM, :] = v[:, :LANES]
            ext[at // LANES + 1, 0:RIM, :] = v[:, LANES:]

    @pl.when(jnp.logical_not(first_block))
    def _():
        ext[:, 0:RIM, :] = ext[:, rows : rows + RIM, :]

    tokens = normed[...]
    low = nt(tokens, down[...]).astype(BF)
    low_ref[...] = low
    both = jnp.concatenate([tokens, low], axis=1)
    raw = nn(both, jnp.concatenate([wtail[...], up[:, inner + mixer :]], axis=0))
    raw = raw + par[STEP_BIAS, :LANES]
    sig[...] = sigmoid(raw)
    widths = jnp.maximum(raw, 0.0) + jnp.log1p(jnp.exp(-jnp.abs(raw)))
    wid[...] = widths
    ones = lower_ones(CHUNK)

    def convolve(n):
        t = slice(n * LANES, n * LANES + LANES)
        for start in range(0, rows, BAND):
            pre = par[CONV_BIAS, t]
            for k in range(4):
                at = RIM - 3 + k + start
                pre = pre + par[k : k + 1, t] * ext[n, at : at + BAND, :]
            s = sigmoid(pre)
            act = pre * s
            xbc[start : start + BAND, t] = act.astype(BF)
            dact[start : start + BAND, t] = (s + act * (1.0 - s)).astype(BF)

    for n in range(0, mixer // LANES + 2, 2):
        if n < mixer // LANES:
            at = n * LANES
            v = nn(both, jnp.concatenate([win[:, at : at + 2 * LANES], up[:, inner + at : inner + at + 2 * LANES]], axis=0))
            ext[n, RIM : RIM + rows, :] = v[:, :LANES]
            ext[n + 1, RIM : RIM + rows, :] = v[:, LANES:]
        if n > 0:
            convolve(n - 2)
            convolve(n - 1)
    for j in range(rows // CHUNK):
        w = widths[rows_of(j)]
        c = running(ones, w * par[RATE, :LANES], heads)
        cum[rows_of(j)] = c
        last = c[CHUNK - 1 : CHUNK]
        tail = spread(jnp.exp(last - c) * w, onehot[...], heads)
        weighted = jnp.concatenate(
            [(xbc[rows_of(j), t].astype(F32) * tail[:, t]).astype(BF) for t in tiles(inner)], axis=1
        )
        inputs_t = xbc[rows_of(j), inner : inner + states].astype(F32).T.astype(BF)
        update = nn(inputs_t, weighted)
        before = run[...]
        cpre[j] = before
        keep = spread(jnp.exp(jnp.broadcast_to(last, before.shape)), onehot[...], heads)[0:1]
        for t in tiles(inner):
            old = state[:, t]
            sloc[j, :, t] = old.astype(BF)
            state[:, t] = keep[:, t] * old + update[:, t]
        run[...] = before + last


def intra_step(heads, normed, low_ref, win, up, xbc, wid, cum, gate, y, onehot):
    inner = onehot.shape[1]
    states = (xbc.shape[1] - inner) // 2
    width = inner // heads
    per = LANES // width
    both = jnp.concatenate([normed[...], low_ref[...]], axis=1)
    lane = lax.broadcasted_iota(jnp.int32, (CHUNK, LANES), 1)
    mask = lower_ones(CHUNK)
    ready = []
    for j in range(xbc.shape[0] // CHUNK):
        c = cum[rows_of(j)] * LOG2E
        wide = spread(wid[rows_of(j)], onehot[...], heads)
        inputs = xbc[rows_of(j), inner : inner + states]
        reads = xbc[rows_of(j), inner + states :]
        ready.append((c, c.T, wide, nt(reads, inputs) * mask))
    columns = tiles(inner)
    order = list(range(normed.shape[1] // LANES, len(columns))) + list(range(normed.shape[1] // LANES))
    for n, k in enumerate(order):
        t = columns[k]
        if n < inner // (2 * LANES):
            g = slice(n * 2 * LANES, (n + 1) * 2 * LANES)
            gate[:, g] = nn(both, jnp.concatenate([win[:, g], up[:, g]], axis=0)).astype(BF)
        for j, (c, c_rows, wide, scores) in enumerate(ready):
            weighted = xbc[rows_of(j), t].astype(F32) * wide[:, t]
            mixing, parts = [], []
            for p in range(per):
                h = k * per + p
                kernel = jnp.exp2(jnp.minimum(c[:, h : h + 1] - c_rows[h : h + 1, :], 0.0))
                mixing.append((kernel * scores).astype(BF))
                inside = (lane >= p * width) & (lane < (p + 1) * width)
                parts.append(jnp.where(inside, weighted, 0.0).astype(BF))
            y[rows_of(j), t] = nn(jnp.concatenate(mixing, axis=1), jnp.concatenate(parts, axis=0)).astype(BF)


def output_step(
    heads, first_block, middle, loaded, y, xbc, gate, cum, sloc, cpre, csuf, start, res, cot, out, wout, down, up, par,
    dreads, rowt, gup, gdown, onehot, snow, adj, run, gated, nout, gno, prod,
):
    rows = res.shape[0]
    inner = onehot.shape[1]
    states = (xbc.shape[1] - inner) // 2
    chunks = rows // CHUNK

    @pl.when(first_block)
    def _():
        adj[...] = jnp.zeros_like(adj)
        run[...] = jnp.zeros_like(run)
        gup[...] = jnp.zeros_like(gup)
        gdown[...] = jnp.zeros_like(gdown)

    reach, scale = [], []
    for j in range(chunks):
        since = spread(jnp.exp(cpre[j]), onehot[...], heads)
        for t in tiles(inner):
            snow[j, :, t] = (sloc[j, :, t].astype(F32) + since[0:1, t] * start[:, t].astype(F32)).astype(BF)
        carried = nn(xbc[rows_of(j), inner + states :], snow[j])
        grow = spread(jnp.exp(cum[rows_of(j)]), onehot[...], heads)
        reach.append(grow)
        for here, at in bands(j):
            total = jnp.zeros((BAND, LANES), F32)
            for t in tiles(inner):
                local = y[at, t].astype(F32) + grow[here, t] * carried[here, t]
                y[at, t] = local.astype(BF)
                g = gate[at, t].astype(F32)
                v = (local + par[SKIP, t] * xbc[at, t].astype(F32)) * (g * sigmoid(g))
                gated[at, t] = v.astype(BF)
                total = total + v * v
            r = lax.rsqrt(jnp.sum(total, axis=1, keepdims=True) * (1.0 / inner) + EPS)
            scale.append(r)
            for t in tiles(inner):
                nout[at, t] = (gated[at, t].astype(F32) * r * par[GATE_GAIN, t]).astype(BF)

    middle()
    loaded()
    normed_out = nout[...]
    cot_rows = cot[...]
    low_out = nt(normed_out, down[...]).astype(BF)
    both = jnp.concatenate([normed_out, low_out], axis=1)
    for at in range(0, out.shape[1], 2 * LANES):
        t = slice(at, at + 2 * LANES)
        part = nn(both, jnp.concatenate([wout[:, t], up[:, t]], axis=0))
        out[:, t] = (res[:, t].astype(F32) + part).astype(BF)
    grad_low = nt(cot_rows, up[...]).astype(BF)
    for at in range(0, inner, 2 * LANES):
        t = slice(at, at + 2 * LANES)
        v = nt(cot_rows, wout[t, :]) + nn(grad_low, down[:, t])
        gno[at // LANES, 0:rows, :] = v[:, :LANES]
        gno[at // LANES + 1, 0:rows, :] = v[:, LANES:]

    def down_gradient(at):
        gdown[:, at : at + 2 * LANES] += tn(grad_low, normed_out[:, at : at + 2 * LANES])

    def up_gradient(at):
        gup[:, at : at + 2 * LANES] += tn(low_out, cot_rows[:, at : at + 2 * LANES])

    tasks = [(up_gradient, at) for at in range(0, out.shape[1], 2 * LANES)]
    tasks += [(down_gradient, at) for at in range(0, inner, 2 * LANES)]
    each = -(-len(tasks) // (rows // BAND))

    for j in reversed(range(chunks)):
        pieces = []
        for m, (here, at) in enumerate(bands(j)):
            total = jnp.zeros((BAND, LANES), F32)
            for n, t in enumerate(tiles(inner)):
                q = gno[n, at, :] * par[GATE_GAIN, t]
                total = total + gated[at, t].astype(F32) * q
            r = scale[j * (CHUNK // BAND) + m]
            shrink = jnp.sum(total, axis=1, keepdims=True) * (1.0 / inner) * (r * r * r)
            scaled = []
            for n, t in enumerate(tiles(inner)):
                q = gno[n, at, :] * par[GATE_GAIN, t]
                grad = r * q - gated[at, t].astype(F32) * shrink
                local = y[at, t].astype(F32)
                g = gate[at, t].astype(F32)
                s = sigmoid(g)
                dy = grad * (g * s)
                y[at, t] = dy.astype(BF)
                full = local + par[SKIP, t] * xbc[at, t].astype(F32)
                gate[at, t] = (grad * full * (s * (1.0 + g * (1.0 - s)))).astype(BF)
                prod[here, t] = (dy * local).astype(BF)
                scaled.append((dy * reach[j][here, t]).astype(BF))
            pieces.append(jnp.concatenate(scaled, axis=1))
            for task, first_column in tasks[:each]:
                task(first_column)
            tasks = tasks[each:]
        rowt[rows_of(j)] = gather_heads(prod[...], onehot[...], heads)
        scaled = jnp.concatenate(pieces, axis=0)
        reads_t = xbc[rows_of(j), inner + states :].astype(F32).T.astype(BF)
        update = nn(reads_t, scaled)
        dreads[rows_of(j)] = nt(scaled, snow[j])
        last = cum[j * CHUNK + CHUNK - 1 : j * CHUNK + CHUNK]
        before = run[...]
        csuf[j] = before
        keep = reach[j][CHUNK - 1 : CHUNK]
        for t in tiles(inner):
            old = adj[:, t]
            sloc[j, :, t] = old.astype(BF)
            adj[:, t] = keep[:, t] * old + update[:, t]
        run[...] = before + last


def adjoint_step(heads, first_block, between, xbc, dact, wid, cum, sig, dy, dreads, rowt, gloc, csuf, end, final, par, onehot, adj, prod, z, held):
    inner = onehot.shape[1]
    states = (xbc.shape[1] - inner) // 2
    width = inner // heads
    per = LANES // width
    mask = upper_ones(CHUNK)
    lane = lax.broadcasted_iota(jnp.int32, (CHUNK, LANES), 1)

    @pl.when(first_block)
    def _():
        overlap = []
        for t in tiles(inner):
            overlap.append(jnp.sum(end[:, t].astype(F32) * final(t), axis=0, keepdims=True))
        v = jnp.broadcast_to(jnp.concatenate(overlap, axis=1), (8, inner))
        high = v.astype(BF)
        rest = (v - high.astype(F32)).astype(BF)
        held[...] = gather_heads(high, onehot[...], heads) + gather_heads(rest, onehot[...], heads)

    for j in reversed(range(xbc.shape[0] // CHUNK)):
        at = rows_of(j)
        c = cum[at]
        w = wid[at]
        c_two = c * LOG2E
        c_rows = c_two.T
        wide = spread(w, onehot[...], heads)
        inputs = xbc[at, inner : inner + states]
        reads = xbc[at, inner + states :]
        scores_t = nt(inputs, reads) * mask
        total = jnp.zeros((CHUNK, CHUNK), F32)
        for k, t in enumerate(tiles(inner)):
            weighted = (xbc[at, t].astype(F32) * wide[:, t]).astype(BF)
            grads = dy[at, t].astype(F32)
            mixing, right = [], []
            for p in range(per):
                inside = (lane >= p * width) & (lane < (p + 1) * width)
                right.append(jnp.where(inside, grads, 0.0).astype(BF))
            right = jnp.concatenate(right, axis=0)
            products = nt(weighted, right)
            for p in range(per):
                h = k * per + p
                kernel = jnp.exp2(jnp.minimum(c_rows[h : h + 1, :] - c_two[:, h : h + 1], 0.0))
                mixing.append((kernel * scores_t).astype(BF))
                total = total + kernel * products[:, p * CHUNK : (p + 1) * CHUNK]
            z[:, t] = nn(jnp.concatenate(mixing, axis=1), right)
        total = total * mask
        dinputs = nn(total.astype(BF), reads)
        dreads_all = dreads[at] + nn(total.T.astype(BF), inputs)

        since = spread(jnp.exp(csuf[j]), onehot[...], heads)
        for t in tiles(inner):
            adj[:, t] = (gloc[j, :, t].astype(F32) + since[0:1, t] * end[:, t].astype(F32)).astype(BF)
        last = c[CHUNK - 1 : CHUNK]
        tail = spread(jnp.exp(last - c), onehot[...], heads)
        carried = nn(inputs, adj[...])
        weighted = []
        for t in tiles(inner):
            x = xbc[at, t].astype(F32)
            v = z[:, t] + tail[:, t] * carried[:, t]
            prod[:, t] = (x * v).astype(BF)
            grad = wide[:, t] * v + par[SKIP, t] * dy[at, t].astype(F32)
            dact[at, t] = (grad * dact[at, t].astype(F32)).astype(BF)
            weighted.append((x * (wide[:, t] * tail[:, t])).astype(BF))
        dinputs = dinputs + nt(jnp.concatenate(weighted, axis=1), adj[...])
        t = slice(inner, inner + states)
        dact[at, t] = (dinputs * dact[at, t].astype(F32)).astype(BF)
        t = slice(inner + states, inner + 2 * states)
        dact[at, t] = (dreads_all * dact[at, t].astype(F32)).astype(BF)
        direct = gather_heads(prod[...], onehot[...], heads)
        grad_rate = held[0:1] + running(mask, rowt[at] - w * direct, heads)
        held[...] = jnp.broadcast_to(grad_rate[0:1], held.shape)
        sig[at] = (direct + par[RATE, :LANES] * grad_rate) * sig[at]
        between(j)


def input_step(heads, first_block, loaded, following, gpre, ggate, graw, low_ref, res, cot, gin, wgate, win, wtail, down, up, par, gup, gdown, ext, gn, nrm):
    rows = res.shape[0]
    inner = ggate.shape[1]
    mixer = gpre.shape[1]
    proj = inner + mixer + heads
    model = res.shape[1]
    gain = par[NORM_GAIN, :model]

    @pl.when(first_block)
    def _():
        gup[...] = jnp.zeros_like(gup)
        gdown[...] = jnp.zeros_like(gdown)

    for n, t in enumerate(tiles(mixer)):
        for j in range(rows // CHUNK):
            ext[n, rows_of(j), :] = gpre[rows_of(j), t].astype(F32)
    following()
    for n, t in enumerate(tiles(mixer)):
        for start in range(0, rows, BAND):
            total = None
            for k in range(4):
                at = 3 - k + start
                term = par[k : k + 1, t] * ext[n, at : at + BAND, :]
                total = term if total is None else total + term
            gpre[start : start + BAND, t] = total.astype(BF)
    grads_gate, grads_mix = ggate[...], jnp.concatenate([gpre[...], graw[...].astype(BF)], axis=1)
    grad_low = (nt(grads_gate, up[:, :inner]) + nt(grads_mix, up[:, inner:])).astype(BF)
    for at in range(0, model, 2 * LANES):
        t = slice(at, at + 2 * LANES)
        mix = jnp.concatenate([win[t, :mixer], wtail[t, :]], axis=1)
        gn[:, t] = nt(grads_gate, wgate[t, :]) + nt(grads_mix, mix) + nn(grad_low, down[:, t])
    loaded()

    low = low_ref[...]
    tasks = []
    for at in range(0, proj, 2 * LANES):
        tasks.append(slice(at, min(at + 2 * LANES, proj)))

    def up_gradient(t):
        grads = grads_gate[:, t] if t.stop <= inner else grads_mix[:, t.start - inner : -(-t.stop // LANES) * LANES - inner]
        gup[:, t] += tn(low, grads)[:, : t.stop - t.start]

    each = -(-len(tasks) // (rows // BAND))
    for n, start in enumerate(range(0, rows, BAND)):
        at = slice(start, start + BAND)
        v = res[at, :].astype(F32)
        u = lax.rsqrt(jnp.mean(v * v, axis=1, keepdims=True) + EPS)
        nrm[at, :] = (v * u * gain).astype(BF)
        w = gn[at, :] * gain
        m = jnp.mean(v * w, axis=1, keepdims=True)
        gin[at, :] = (cot[at, :].astype(F32) + u * w - v * (u * u * u * m)).astype(BF)
        for t in tasks[n * each : (n + 1) * each]:
            up_gradient(t)
    gdown[...] += tn(grad_low, nrm[...])


def block_kernel(
    dp_count, seq_count,
    in_idx, out_idx, res_ref, cot_ref, win_ref, wout_ref, up_in_ref, down_in_ref, up_out_ref, down_out_ref,
    taps_ref, conv_bias_ref, gate_gain_ref, norm_gain_ref, skip_ref, step_bias_ref, decay_ref,
    out_ref, gin_ref, sums_ref,
    xbc, dact, gate, yb, sloc, low, wid, cum, sig, rowt, dreads, cpre, csuf, tot, dtot, start, gown, end,
    theirs, theirs_dec, prefix, passed, tail, wmix, wtail, wgate, wout, up_mix_all, up_gate_all, down_in_all, up_out_all, down_out_all,
    up_in, down_in, up_out, down_out, par,
    halo, rim, stage_res, stage_cot, stage_out, ext, state, snow, gated, nout, prod, run, held, onehot, z, gn,
    gup_in, gdown_in, gup_out, gdown_out, pack, first_half, half_sum, half_sent, line, red, give, owners,
    wsems, csems, hsems, lsems, rsems,
):
    dp = lax.axis_index("dp")
    seq = lax.axis_index("seq")
    seqs, tokens, model = res_ref.shape
    blocks = tokens // BLOCK
    per = BLOCK // CHUNK
    heads = step_bias_ref.shape[0]
    inner = onehot.shape[1]
    mixer = xbc.shape[2]
    proj = win_ref.shape[1]
    pairs = seq_count // 2
    side = lax.rem(seq, 2)
    pair = seq // 2
    chips = dp_count // 2
    partner = (seq + 1 - 2 * side, dp)
    sibling = (seq, dp + 1 - 2 * lax.rem(dp, 2))
    later = (lax.rem(seq + 1, seq_count), dp)
    earlier = (lax.rem(seq + seq_count - 1, seq_count), dp)
    upper = (lax.rem(pair + 1, pairs) * 2 + side, dp)
    lower = (lax.rem(pair + pairs - 1, pairs) * 2 + side, dp)
    others = [(seq, lax.rem(dp + 2 * k, dp_count)) for k in range(1, chips)]
    barrier = pltpu.get_barrier_semaphore()
    along = [(lax.rem(pair + k, pairs) * 2 + side, dp) for k in range(1, pairs)]
    across = [(seq, lax.rem(dp + k, dp_count)) for k in range(1, dp_count)]
    for other in [partner] + along + across:
        pl.semaphore_signal(barrier, inc=1, device_id=other, device_id_type=MESH)
    greeted = pairs + dp_count - 1
    for other, there in ((later, seq < seq_count - 1), (earlier, seq > 0)):
        greeted = greeted + jnp.where(there, 1, 0)

        @pl.when(there)
        def _(other=other):
            pl.semaphore_signal(barrier, inc=1, device_id=other, device_id_type=MESH)

    def load(n):
        s, k = n // blocks, lax.rem(n, blocks) if not isinstance(n, int) else n % blocks
        rows = pl.ds(k * BLOCK, BLOCK)
        return pltpu.make_async_copy(res_ref.at[s, rows], yb.at[n, :, pl.ds(model, model)], lsems.at[n])

    for n in range(seqs * blocks):
        load(n).start()
    onehot[...] = head_onehot(heads, inner)
    par[...] = jnp.zeros_like(par)
    par[0:4] = taps_ref[...]
    par[CONV_BIAS] = conv_bias_ref[...][None, :]
    par[GATE_GAIN, :inner] = gate_gain_ref[...][None, :]
    par[NORM_GAIN, :model] = norm_gain_ref[...][None, :]
    par[STEP_BIAS, :heads] = step_bias_ref[...][None, :]
    par[RATE, :heads] = -jnp.exp(decay_ref[...][None, :])
    par[SKIP, :heads] = skip_ref[...][None, :]
    v = jnp.broadcast_to(par[SKIP, :LANES], (8, LANES))
    par[SKIP, :inner] = spread(v, onehot[...], heads)[0:1]
    wtail[...] = jnp.zeros_like(wtail)
    up_in[:, :, inner + mixer :] = jnp.zeros(up_in.shape[:2] + (LANES,), BF)
    pl.semaphore_wait(barrier, greeted)

    def send(src, dst, to, sems, *at):
        return pltpu.make_async_remote_copy(
            src_ref=src, dst_ref=dst, send_sem=sems.at[(0,) + at], recv_sem=sems.at[(1,) + at],
            device_id=to, device_id_type=MESH,
        )

    def rows_piece(ref, out, at, to, wide, n):
        share = ref.shape[0]
        half = share // 2

        def source(which):
            return ref.at[pl.ds(pl.multiple_of(which * half, 16), half), pl.ds(at, wide)]

        def target(owner, which):
            return out.at[pl.ds(pl.multiple_of(owner * share + which * half, 16), half), pl.ds(to, wide)]

        return source, target, n

    def table_piece(ref, out, at, wide, n):
        owned = ref.shape[0]
        return (lambda _: ref.at[:, :, pl.ds(at, wide)]), (lambda owner, _: out.at[pl.ds(owner * owned, owned)]), n, None, 0

    width = proj - inner
    split = mixer // 2 // LANES * LANES
    odd = lax.rem(pair, 2)
    across_y = (partner, side)
    across_z = (((pair + 1 - 2 * odd) * 2 + side, dp), odd)
    groups = [
        [
            (*rows_piece(win_ref, wmix, inner, 0, split, 0), *across_y),
            (*rows_piece(win_ref, wmix, inner + split, split, width - split, 1), *across_y),
            table_piece(down_in_ref, down_in_all, 0, model, 2),
            table_piece(up_in_ref, up_mix_all, inner, width, 3),
        ],
        [
            table_piece(up_in_ref, up_gate_all, 0, inner, 4),
            (*rows_piece(win_ref, wgate, 0, 0, inner, 5), *across_z),
        ],
        [
            (*rows_piece(wout_ref, wout, 0, 0, wout_ref.shape[1], 6), *across_z),
            table_piece(down_out_ref, down_out_all, 0, inner, 7),
            table_piece(up_out_ref, up_out_all, 0, model, 8),
        ],
    ]

    def shards(k):
        return lax.rem(dp - 2 * k + dp_count, dp_count)

    def over_x(group):
        return [
            send(source(mine), target(dp, mine), others[k - 1], wsems, 0, k, n)
            for source, target, n, _, mine in group
            for k in range(1, chips)
        ]

    def own(group):
        copies = []
        for source, target, n, mate, _ in group:
            for which in range(1 if mate is None else 2):
                copies.append(pltpu.make_async_copy(source(which), target(dp, which), wsems.at[0, 6 + which, 0, n]))
                copies.append(send(source(which), target(dp, which), sibling, wsems, 3 + which, 0, n))
        return copies

    def forward(group, start_it):
        for source, target, n, mate, mine in group:
            for k in range(1, chips):
                here = target(shards(k), mine)
                if start_it:
                    send(source(mine), here, others[k - 1], wsems, 0, k, n).wait_recv()
                copies = [send(here, here, sibling, wsems, 2, k, n)]
                if mate is not None:
                    copies.append(send(here, here, mate, wsems, 1, k, n))
                if start_it:
                    for copy in copies:
                        copy.start()
                else:
                    copies[0].wait()
                    if mate is not None:
                        copies[1].wait_send()

    def relay(group, start_it):
        for source, target, n, mate, mine in group:
            if mate is None:
                continue
            for k in range(1, chips):
                there = target(shards(k), 1 - mine)
                if start_it:
                    send(there, there, mate, wsems, 1, k, n).wait_recv()
                over = send(there, there, sibling, wsems, 5, k, n)
                if start_it:
                    over.start()
                else:
                    over.wait()

    def settle(group):
        for copy in over_x(group):
            copy.wait_send()
        for copy in own(group):
            copy.wait()
        forward(group, False)
        relay(group, False)

    edge = send(res_ref.at[:, pl.ds(tokens - RIM, RIM)], halo, later, hsems, 0)
    for copy in over_x(groups[0]):
        copy.start()

    @pl.when(seq < seq_count - 1)
    def _():
        edge.start()

    for copy in own(groups[0]):
        copy.start()
    gain = par[NORM_GAIN, :model]

    def norm_block(n, _):
        load(n).wait()
        write_normed(yb.at[n, :, pl.ds(0, model)], yb.at[n, :, pl.ds(model, model)], gain, 32)
        return 0

    lax.fori_loop(0, seqs * blocks, norm_block, 0)
    forward(groups[0], True)
    for copy in over_x(groups[1]):
        copy.start()
    relay(groups[0], True)

    @pl.when(seq == 0)
    def _():
        halo[...] = jnp.zeros_like(halo)

    @pl.when(seq > 0)
    def _():
        edge.wait_recv()

    @pl.when(seq < seq_count - 1)
    def _():
        edge.wait_send()

    settle(groups[0])
    for copy in own(groups[1]):
        copy.start()

    def pick(dst, table, idx_ref, at=0):
        for q in range(seqs):
            dst[q, :, at : at + table.shape[2]] = table[idx_ref[q]]

    pick(down_in, down_in_all, in_idx)
    pick(up_in, up_mix_all, in_idx, inner)
    wtail[:, :heads] = wmix[:, mixer:]

    half = inner // 2
    wide = half // PARTS

    def cols(base, q):
        return pl.ds(pl.multiple_of(base * half + q * wide, LANES), wide)

    def chain(d, s):
        my_pair = pairs - 1 - pair if d else pair
        my_side = 1 - side if d else side
        ahead = lower if d else upper
        total, result = (gown, end) if d else (tot, start)

        def decs():
            return send(dtot.at[s], theirs_dec.at[d, s], partner, csems, d, s, 3, 0)

        def swap(q):
            return send(total.at[s, :, cols(1 - my_side, q)], theirs.at[d, s, q], partner, csems, d, s, 0, q)

        def hop(q):
            return send(passed.at[d, s, q], prefix.at[d, s, q], ahead, csems, d, s, 1, q)

        def give(q):
            return send(tail.at[d, s, q], result.at[s, :, cols(my_side, q)], partner, csems, d, s, 2, q)

        return my_pair, my_side, total, result, decs, swap, hop, give

    def chain_start(d, s):
        _, _, _, _, decs, swap, _, _ = chain(d, s)
        decs().start()
        for q in range(PARTS):
            swap(q).start()

    def chain_tick(d, s, tick, final):
        my_pair, my_side, total, result, decs, swap, hop, give = chain(d, s)
        for q in range(PARTS):
            turn = jnp.minimum(my_pair + (1 if q else 0), final)

            @pl.when(tick == turn)
            def _(q=q):
                if q == 0:
                    decs().wait_recv()
                swap(q).wait_recv()

                @pl.when(my_pair == 0)
                def _():
                    prefix[d, s, q] = jnp.zeros_like(prefix[d, s, q])

                @pl.when(my_pair > 0)
                def _():
                    hop(q).wait_recv()

                own_dec = dtot[s, 0:1, cols(my_side, q)]
                their_dec = theirs_dec[d, s, 0:1, cols(my_side, q)]
                own_total = total[s, :, cols(my_side, q)].astype(F32)
                other = theirs[d, s, q].astype(F32)
                before = prefix[d, s, q].astype(F32)
                left = my_side == 0
                first = jnp.where(left, own_total, other)
                second = jnp.where(left, other, own_total)
                first_dec = jnp.where(left, own_dec, their_dec)
                second_dec = jnp.where(left, their_dec, own_dec)
                middle = first_dec * before + first
                passed[d, s, q] = (second_dec * middle + second).astype(BF)

                @pl.when(my_pair < pairs - 1)
                def _():
                    hop(q).start()

                result[s, :, cols(my_side, q)] = jnp.where(left, before, middle).astype(BF)
                tail[d, s, q] = jnp.where(left, middle, before).astype(BF)
                give(q).start()

    def chain_end(d, s):
        my_pair, _, _, _, decs, swap, hop, give = chain(d, s)
        decs().wait_send()
        for q in range(PARTS):
            give(q).wait()
            swap(q).wait_send()

            @pl.when(my_pair < pairs - 1)
            def _(q=q):
                hop(q).wait_send()

    rank = gup_in.shape[1]
    owned = up_in_ref.shape[0]

    def reduction(number, parts):
        counts = [sum(-(-g.shape[2] // LANES) for g in pair_of) for pair_of in ((gup_out, gdown_out), (gup_in, gdown_in))]
        shares = [-(-n // seq_count) for n in counts]
        share = shares[number]
        wide = pairs * share
        before = sum(shares[:number])
        base, middle, small = before * seq_count, before * pairs, pl.ds(before, share)
        place = pl.ds(base + (side * pairs + pair) * share, share)

        def rows_of_seq(q):
            return pl.ds(q * rank, rank)

        def swap(there, q):
            theirs_of = pack.at[pl.ds(base + ((1 - side) * pairs + there) * share, share), rows_of_seq(q)]
            here = first_half.at[pl.ds(middle + there * share, share), rows_of_seq(q)]
            return send(theirs_of, here, partner, rsems, number, 0, there, q)

        def along_line(k, q):
            there = lax.rem(pair + k, pairs)
            mine = half_sent.at[pl.ds(middle + there * share, share), rows_of_seq(q)]
            return send(mine, line.at[k - 1, small, rows_of_seq(q)], along[k - 1], rsems, number, 1, k, q)

        def to_owner(k):
            return send(give.at[k - 1, small], owners.at[k - 1, small], across[k - 1], rsems, number, 2, k, 0)

        def back_along(k):
            return send(sums_ref.at[place], sums_ref.at[place], along[k - 1], rsems, number, 3, k, 0)

        def back_across(k):
            there = lax.rem(pair + pairs - k, pairs)
            ours = sums_ref.at[pl.ds(base + (side * pairs + there) * share, share)]
            return send(ours, ours, partner, rsems, number, 4, k, 0)

        def part(owner, n, a):
            total = None
            for q in range(seqs):
                index = in_idx[q] if number else out_idx[q]
                c = jnp.where(index == owner * owned + a, 1.0, 0.0)
                term = c * red[before + n, q * rank : (q + 1) * rank, :]
                total = term if total is None else total + term
            return total

        def start(q):
            n = base
            for ref in parts:
                for t in tiles(ref.shape[2]):
                    v = ref[q, :, t]
                    if t.stop - t.start < LANES:
                        v = jnp.concatenate([v, jnp.zeros((rank, LANES - t.stop + t.start), F32)], axis=1)
                    pack[n, q * rank : (q + 1) * rank, :] = v.astype(BF)
                    n += 1
            for m in range(n, base + share * seq_count):
                pack[m, q * rank : (q + 1) * rank, :] = jnp.zeros((rank, LANES), BF)
            for k in list(range(1, pairs)) + [0]:
                swap(lax.rem(pair + k, pairs), q).start()

        def second(q):
            rows = slice(q * rank, (q + 1) * rank)
            for k in list(range(1, pairs)) + [0]:
                there = lax.rem(pair + k, pairs)
                swap(there, q).wait()

                def add(n, _, there=there):
                    at = there * share + n
                    v = pack[base + side * wide + at, rows, :].astype(F32) + first_half[middle + at, rows, :].astype(F32)
                    half_sum[middle + at, rows, :] = v
                    half_sent[middle + at, rows, :] = v.astype(BF)
                    return 0

                lax.fori_loop(0, share, add, 0)
                if k:
                    along_line(k, q).start()

        def third():
            for k in range(1, pairs):
                for q in range(seqs):
                    along_line(k, q).wait()
            for n in range(share):
                v = half_sum[middle + pair * share + n]
                for k in range(pairs - 1):
                    v = v + line[k, before + n].astype(F32)
                red[before + n] = v
            for k in range(1, dp_count):
                owner = lax.rem(dp + k, dp_count)
                for n in range(share):
                    for a in range(owned):
                        give[k - 1, before + n, a * rank : (a + 1) * rank, :] = part(owner, n, a).astype(BF)
                to_owner(k).start()

        def fourth():
            for k in range(1, dp_count):
                to_owner(k).wait()
            for n in range(share):
                for a in range(owned):
                    v = part(dp, n, a)
                    for k in range(dp_count - 1):
                        v = v + owners[k, before + n, a * rank : (a + 1) * rank, :].astype(F32)
                    sums_ref[base + (side * pairs + pair) * share + n, a * rank : (a + 1) * rank, :] = v.astype(BF)
            for k in range(1, pairs):
                back_along(k).start()
            back_across(0).start()

        def fifth():
            for k in range(1, pairs):
                back_along(k).wait()
                back_across(k).start()

        def finish():
            for k in range(pairs):
                back_across(k).wait()

        def every_seq(step):
            def steps():
                for q in range(seqs):
                    step(q)

            return steps

        return start, second, [every_seq(start), every_seq(second), third, fourth, fifth, finish]

    def chunk_of(n):
        return pl.ds(n * per, per)

    def project_block(n, _):
        s, k = n // blocks, lax.rem(n, blocks)
        project_step(
            heads, k == 0, yb.at[n, :, pl.ds(0, model)], halo.at[s], wmix, wtail, down_in.at[s], up_in.at[s], par, low.at[n],
            xbc.at[n], dact.at[n], wid.at[n], cum.at[n], sig.at[n], sloc.at[chunk_of(n)], cpre.at[chunk_of(n)],
            ext, state, run, onehot,
        )

        @pl.when(k == blocks - 1)
        def _():
            tot[s] = state[...].astype(BF)
            dtot[s] = spread(jnp.exp(run[...]), onehot[...], heads)

        @pl.when(n == blocks - 2)
        def _():
            forward(groups[1], True)
            for copy in over_x(groups[2]) + own(groups[2]):
                copy.start()

        @pl.when(n == blocks - 1)
        def _():
            chain_start(0, 0)

        @pl.when(n == blocks + 1)
        def _():
            forward(groups[2], True)

        @pl.when(n >= blocks)
        def _():
            chain_tick(0, 0, n - blocks, FINAL)

        return 0

    lax.fori_loop(0, seqs * blocks, project_block, 0)
    chain_start(0, 1)
    relay(groups[1], True)
    settle(groups[1])
    pick(up_in, up_gate_all, in_idx)

    def intra_block(n):
        s = n // blocks
        intra_step(
            heads, yb.at[n, :, pl.ds(0, model)], low.at[n], wgate, up_in.at[s], xbc.at[n], wid.at[n], cum.at[n], gate.at[n],
            yb.at[n], onehot,
        )

    def staged(s, k, slot):
        rows = pl.ds(k * BLOCK, BLOCK)
        return [
            pltpu.make_async_copy(res_ref.at[s, rows], stage_res.at[slot], lsems.at[slot]),
            pltpu.make_async_copy(cot_ref.at[s, rows], stage_cot.at[slot], lsems.at[2 + slot]),
        ]

    def stored(ref, s, k):
        return pltpu.make_async_copy(stage_out, ref.at[s, pl.ds(k * BLOCK, BLOCK)], lsems.at[4])

    def stage(n, backwards):
        s, k = n // blocks, lax.rem(n, blocks)
        return staged(s, blocks - 1 - k if backwards else k, lax.rem(n, 2))

    first = blocks + 1
    second = seqs * blocks + blocks

    def output_block(i):
        s = jnp.where(i < second, 0, 1)
        k = blocks - 1 - (i - jnp.where(i < second, first, second))
        n = s * blocks + k
        turn = s * blocks + blocks - 1 - k
        slot = lax.rem(turn, 2)

        @pl.when(i == first)
        def _():
            relay(groups[2], True)
            settle(groups[2])
            pick(down_out, down_out_all, out_idx)
            pick(up_out, up_out_all, out_idx)
            chain_end(0, 0)

        @pl.when(i == second)
        def _():
            chain_end(0, 1)

        def middle():
            chain_tick(1, 0, among(i, {second: 1, second + 2: FINAL}), FINAL)

        def loaded():
            for copy in stage(turn, True):
                copy.wait()

            @pl.when(turn < seqs * blocks - 1)
            def _():
                for copy in stage(turn + 1, True):
                    copy.start()

            @pl.when(i > first)
            def _():
                stored(out_ref, s, k).wait()

        output_step(
            heads, k == blocks - 1, middle, loaded, yb.at[n], xbc.at[n], gate.at[n], cum.at[n], sloc.at[chunk_of(n)],
            cpre.at[chunk_of(n)], csuf.at[chunk_of(n)], start.at[s], stage_res.at[slot], stage_cot.at[slot], stage_out, wout, down_out.at[s],
            up_out.at[s], par, dreads.at[n], rowt.at[n], gup_out.at[s], gdown_out.at[s], onehot, snow, state, run, gated,
            nout, ext, prod,
        )
        stored(out_ref, s, k).start()

        @pl.when(k == 0)
        def _():
            gown[s] = state[...].astype(BF)

        @pl.when(i == first + blocks - 1)
        def _():
            chain_start(1, 0)

    def among(i, turns):
        found = -1
        for at, tick in turns.items():
            found = jnp.where(i == at, tick, found)
        return found

    def middle_block(i, _):
        inside = (i < first) | ((i >= first + blocks) & (i < second))

        @pl.when(inside)
        def _():
            intra_block(jnp.where(i < first, i, i - blocks))

        @pl.when(jnp.logical_not(inside))
        def _():
            output_block(i)

        chain_tick(0, 0, among(i, {1: FINAL - 1, blocks: FINAL}), FINAL)
        chain_tick(0, 1, among(i, {1: 0, blocks: 1, first: 2, first + 1: 3, first + 2: FINAL}), FINAL)
        chain_tick(1, 0, among(i, {second - 1: 0, second: 2, second + 1: 3}), FINAL)
        return 0

    for copy in stage(0, True):
        copy.start()
    lax.fori_loop(0, 2 * seqs * blocks, middle_block, 0)
    stored(out_ref, seqs - 1, 0).wait()
    chain_start(1, 1)

    def rim_edge(s):
        return send(dact.at[s * blocks, pl.ds(0, RIM)], rim.at[s], earlier, hsems, 1 + s)

    period = 2 * blocks

    def back_block(i, _):
        s, r = i // period, lax.rem(i, period)

        @pl.when(r < blocks)
        def _():
            k = blocks - 1 - r
            n = s * blocks + k

            @pl.when(i == 0)
            def _():
                chain_end(1, 0)

            @pl.when(i == period)
            def _():
                chain_end(1, 1)

            def between(j):
                if j == 0:
                    chain_tick(1, 1, jnp.where(i < blocks, i, -1), FINAL)

            adjoint_step(
                heads, k == blocks - 1, between, xbc.at[n], dact.at[n], wid.at[n], cum.at[n], sig.at[n], yb.at[n], dreads.at[n],
                rowt.at[n], sloc.at[chunk_of(n)], csuf.at[chunk_of(n)], end.at[s],
                lambda t: tot[s, :, t].astype(F32) + dtot[s, 0:1, t] * start[s, :, t].astype(F32),
                par, onehot, nout.at[pl.ds(0, CHUNK)], prod, z, held,
            )

            @pl.when(k == 0)
            def _():
                for q in range(seqs):
                    @pl.when((s == q) & (seq > 0))
                    def _(q=q):
                        rim_edge(q).start()

        @pl.when(r >= blocks)
        def _():
            k = r - blocks
            n = s * blocks + k
            late_one = k == blocks - 1
            slot = lax.rem(n, 2)
            for q in range(seqs):
                @pl.when((s == q) & (k == 0) & (seq > 0))
                def _(q=q):
                    rim_edge(q).wait_send()

                @pl.when((s == q) & late_one & (seq < seq_count - 1))
                def _(q=q):
                    rim_edge(q).wait_recv()

                @pl.when((s == q) & late_one & (seq == seq_count - 1))
                def _(q=q):
                    rim[q] = jnp.zeros_like(rim[q])

            def loaded():
                for copy in stage(n, False):
                    copy.wait()

                @pl.when(n < seqs * blocks - 1)
                def _():
                    for copy in stage(n + 1, False):
                        copy.start()

                @pl.when(i > blocks)
                def _():
                    stored(gin_ref, s, k).wait()

            def following():
                @pl.when(late_one)
                def _():
                    for m, t in enumerate(tiles(mixer)):
                        ext[m, BLOCK : BLOCK + RIM, :] = rim[s, :, t].astype(F32)

                @pl.when(jnp.logical_not(late_one))
                def _():
                    for m, t in enumerate(tiles(mixer)):
                        ext[m, BLOCK : BLOCK + RIM, :] = dact[n + 1, 0:RIM, t].astype(F32)

            input_step(
                heads, k == 0, loaded, following, dact.at[n], gate.at[n], sig.at[n], low.at[n], stage_res.at[slot], stage_cot.at[slot], stage_out,
                wgate, wmix, wtail, down_in.at[s], up_in.at[s], par, gup_in.at[s], gdown_in.at[s], ext, gn,
                nout.at[:, pl.ds(0, model)],
            )
            stored(gin_ref, s, k).start()
            chain_tick(1, 1, jnp.where(i < period, i, -1), FINAL)

        for at, step in zip((2, 4, 5, 6, 7, 9), reduction(0, (gup_out, gdown_out))[2]):
            pl.when(i == at)(step)
        begin, again, _ = reduction(1, (gup_in, gdown_in))
        for q in range(seqs - 1):
            pl.when(i == (q + 1) * period)(functools.partial(begin, q))
            pl.when(i == (q + 1) * period + 2)(functools.partial(again, q))
        return 0

    for copy in stage(0, False):
        copy.start()
    lax.fori_loop(0, seqs * period, back_block, 0)
    begin, again, rest = reduction(1, (gup_in, gdown_in))
    begin(seqs - 1)
    again(seqs - 1)
    for step in rest[2:]:
        step()
    stored(gin_ref, seqs - 1, blocks - 1).wait()


def block_call(in_index, out_index, tensors, tables, vectors, sizes, dp_count, seq_count):
    heads, inner, mixer, rank = sizes
    residual, _, in_weight, _ = tensors
    seqs, tokens, model = residual.shape
    states = (mixer - inner) // 2
    count = tokens // BLOCK * seqs
    chunks = tokens // CHUNK * seqs
    proj = in_weight.shape[1]
    lanes = -(-proj // LANES) * LANES
    adapters = tables[0].shape[0] * dp_count
    own_rows = tables[0].shape[0] * rank
    pairs = seq_count // 2
    shares = tile_shares((model, inner), (proj, model), seq_count)
    every = lambda width: pltpu.VMEM((adapters, rank, width), BF)
    rows = lambda width, kind: pltpu.VMEM((count, BLOCK, width), kind)
    state = lambda: pltpu.VMEM((seqs, states, inner), BF)
    slots = lambda: pltpu.VMEM((2, seqs, PARTS, states, inner // 2 // PARTS), BF)
    stage = lambda *slots: pltpu.VMEM((*slots, BLOCK, model), BF)
    picked = lambda width: pltpu.VMEM((seqs, rank, width), BF)
    any_space = pl.BlockSpec(memory_space=pl.ANY)
    vmem = pl.BlockSpec(memory_space=pltpu.VMEM)
    smem = pl.BlockSpec(memory_space=pltpu.SMEM)
    return pl.pallas_call(
        functools.partial(block_kernel, dp_count, seq_count),
        out_shape=[
            jax.ShapeDtypeStruct(residual.shape, BF),
            jax.ShapeDtypeStruct(residual.shape, BF),
            jax.ShapeDtypeStruct((sum(shares) * seq_count, own_rows, LANES), BF),
        ],
        in_specs=[smem, smem] + [any_space] * 8 + [vmem] * len(vectors),
        out_specs=[any_space] * 2 + [vmem],
        scratch_shapes=[
            rows(mixer, BF),
            rows(mixer, BF),
            rows(inner, BF),
            rows(inner, BF),
            pltpu.VMEM((chunks, states, inner), BF),
            rows(rank, BF),
            rows(LANES, F32),
            rows(LANES, F32),
            rows(LANES, F32),
            rows(LANES, F32),
            rows(states, F32),
            pltpu.VMEM((chunks, 8, LANES), F32),
            pltpu.VMEM((chunks, 8, LANES), F32),
            state(),
            pltpu.VMEM((seqs, 8, inner), F32),
            state(),
            state(),
            state(),
            slots(),
            pltpu.VMEM((2, seqs, 8, inner), F32),
            slots(),
            slots(),
            slots(),
            pltpu.VMEM((model, proj - inner), BF),
            pltpu.VMEM((model, LANES), BF),
            pltpu.VMEM((model, inner), BF),
            pltpu.VMEM((inner, model), BF),
            every(proj - inner),
            every(inner),
            every(model),
            every(model),
            every(inner),
            picked(lanes),
            picked(model),
            picked(model),
            picked(inner),
            pltpu.VMEM((16, mixer), F32),
            pltpu.VMEM((seqs, RIM, model), BF),
            pltpu.VMEM((seqs, RIM, mixer), BF),
            stage(2),
            stage(2),
            stage(),
            pltpu.VMEM((mixer // LANES, BLOCK + RIM, LANES), F32),
            pltpu.VMEM((states, inner), F32),
            pltpu.VMEM((BLOCK // CHUNK, states, inner), BF),
            pltpu.VMEM((BLOCK, inner), BF),
            pltpu.VMEM((BLOCK, inner), BF),
            pltpu.VMEM((CHUNK, inner), BF),
            pltpu.VMEM((8, LANES), F32),
            pltpu.VMEM((8, LANES), F32),
            pltpu.VMEM((LANES, inner), BF),
            pltpu.VMEM((CHUNK, inner), F32),
            pltpu.VMEM((BLOCK, model), F32),
            pltpu.VMEM((seqs, rank, proj), F32),
            pltpu.VMEM((seqs, rank, model), F32),
            pltpu.VMEM((seqs, rank, model), F32),
            pltpu.VMEM((seqs, rank, inner), F32),
            pltpu.VMEM((sum(shares) * seq_count, seqs * rank, LANES), BF),
            pltpu.VMEM((sum(shares) * pairs, seqs * rank, LANES), BF),
            pltpu.VMEM((sum(shares) * pairs, seqs * rank, LANES), F32),
            pltpu.VMEM((sum(shares) * pairs, seqs * rank, LANES), BF),
            pltpu.VMEM((max(pairs - 1, 1), sum(shares), seqs * rank, LANES), BF),
            pltpu.VMEM((sum(shares), seqs * rank, LANES), F32),
            pltpu.VMEM((max(dp_count - 1, 1), sum(shares), own_rows, LANES), BF),
            pltpu.VMEM((max(dp_count - 1, 1), sum(shares), own_rows, LANES), BF),
            pltpu.SemaphoreType.DMA((2, 8, max(dp_count // 2, 1), 9)),
            pltpu.SemaphoreType.DMA((2, 2, seqs, 4, PARTS)),
            pltpu.SemaphoreType.DMA((2, 1 + seqs)),
            pltpu.SemaphoreType.DMA((max(count, 5),)),
            pltpu.SemaphoreType.DMA((2, 2, 5, max(pairs, dp_count), seqs)),
        ],
        compiler_params=pltpu.CompilerParams(collective_id=1, has_side_effects=True, vmem_limit_bytes=VMEM_LIMIT),
        name="block",
    )(in_index, out_index, *tensors, *tables, *vectors)


def tile_shares(outs, ins, count):
    return [-(-sum(-(-width // LANES) for width in widths) // count) for widths in (outs, ins)]


def unpack_kernel(second, out_ref, gin_ref, sums, block_out, grad_input, up_out, down_out, up_in, down_in):
    owned, rank, _ = up_out.shape
    block_out[...] = out_ref[...]
    grad_input[...] = gin_ref[...]

    @pl.when(pl.program_id(0) == 0)
    def _():
        for start, pair_of in ((0, (up_out, down_out)), (second, (up_in, down_in))):
            n = start
            for out in pair_of:
                for t in tiles(out.shape[2]):
                    for a in range(owned):
                        out[a, :, t] = sums[n, a * rank : (a + 1) * rank, : t.stop - t.start].astype(F32)
                    n += 1


def unpack(block_out, grad_input, sums, owned, rank, widths, count):
    up_out, down_out, up_in, down_in = widths
    shares = tile_shares((up_out, down_out), (up_in, down_in), count)
    seqs, tokens, model = block_out.shape
    large = pl.BlockSpec((1, tokens, model), lambda s: (s, 0, 0))
    small = [jax.ShapeDtypeStruct((owned, rank, width), F32) for width in widths]
    return pl.pallas_call(
        functools.partial(unpack_kernel, shares[0] * count),
        grid=(seqs,),
        out_shape=[jax.ShapeDtypeStruct(block_out.shape, BF)] * 2 + small,
        in_specs=[large, large, pl.BlockSpec(sums.shape, lambda s: (0, 0, 0))],
        out_specs=[large, large] + [pl.BlockSpec(v.shape, lambda s: (0, 0, 0)) for v in small],
        compiler_params=pltpu.CompilerParams(vmem_limit_bytes=VMEM_LIMIT // 2),
        name="unpack",
    )(block_out, grad_input, sums)


def on_device(
    residual_in,
    cotangent,
    norm_gain,
    in_weight,
    conv_weight,
    conv_bias,
    step_bias,
    decay_log,
    skip_gain,
    gate_gain,
    out_weight,
    in_down,
    in_up,
    out_down,
    out_up,
    in_index,
    out_index,
):
    heads = step_bias.shape[0]
    inner = gate_gain.shape[0]
    mixer = conv_weight.shape[0]
    rank = in_up.shape[1]
    seq_count = lax.axis_size("seq")
    dp_count = lax.axis_size("dp")
    block_out, grad_input, sums = block_call(
        in_index.reshape(-1),
        out_index.reshape(-1),
        (residual_in, cotangent, in_weight, out_weight),
        (in_up, in_down.transpose(0, 2, 1), out_up, out_down.transpose(0, 2, 1)),
        (conv_weight.T, conv_bias, gate_gain, norm_gain, skip_gain, step_bias, decay_log),
        (heads, inner, mixer, rank),
        dp_count,
        seq_count,
    )
    model, proj = in_weight.shape[0] * dp_count, in_weight.shape[1]
    block_out, grad_input, gout_up, gout_down, gin_up, gin_down = unpack(
        block_out, grad_input, sums, in_down.shape[0], rank, (model, inner, proj, model), seq_count
    )
    gin_down, gout_down = (g.transpose(0, 2, 1) for g in (gin_down, gout_down))
    return (block_out, grad_input, gin_down, gin_up, gout_down, gout_up)


def solution(mesh):
    rows = P("dp", "seq", None)
    split = P("dp", None, None)
    return jax.shard_map(
        on_device,
        mesh=mesh,
        in_specs=(
            rows,
            rows,
            P(),
            P("dp", None),
            P(),
            P(),
            P(),
            P(),
            P(),
            P(),
            P("dp", None),
            split,
            split,
            split,
            split,
            P("dp", None),
            P("dp", None),
        ),
        out_specs=(rows, rows, split, split, split, split),
        check_vma=False,
    )
```
